32 devices in a mesh: fsdp: 2 (over y), heads: 4 (over x, core), tensor: 4 (over z).
Axes of the slice: x: 2, y: 2, z: 4, core: 2. Of those that a mesh axis runs over, the one named last changes fastest.
Arguments:
- inputs: bfloat16 [32, 729, 1152], P(('fsdp', 'heads', 'tensor')), may hold values from -6 to 6
- slot_mask: int32 [32], P(('fsdp', 'heads', 'tensor')), may hold values from 0 to 1, as said below
- ln1_gain: float32 [1152], replicated, may hold values from 0.5 to 1.5
- ln1_bias: float32 [1152], replicated, may hold values from -0.625 to 0.625
- qkv_weight: float32 [1152, 3, 1152], P(('fsdp', 'tensor'), None, 'heads'), may hold values from -0.1875 to 0.1875
- qv_bias: float32 [2, 1152], replicated, may hold values from -0.625 to 0.625
- out_weight: float32 [1152, 1152], P('heads', ('fsdp', 'tensor')), may hold values from -3 to 3
- out_bias: float32 [1152], replicated, may hold values from -1.25 to 1.25
- ln2_gain: float32 [1152], replicated, may hold values from 0.5 to 1.5
- ln2_bias: float32 [1152], replicated, may hold values from -0.625 to 0.625
- up_weight: float32 [1152, 4304], P(('fsdp', 'heads'), 'tensor'), may hold values from -0.1875 to 0.1875
- up_bias: float32 [4304], replicated, may hold values from -1.25 to 1.25
- down_weight: float32 [4304, 1152], P('tensor', ('fsdp', 'heads')), may hold values from -0.09375 to 0.09375
- down_bias: float32 [1152], replicated, may hold values from -1.25 to 1.25
- out_grad: bfloat16 [32, 729, 1152], P(('fsdp', 'heads', 'tensor')), may hold values from -12 to 12
Outputs:
- output: bfloat16 [32, 729, 1152], P(('fsdp', 'heads', 'tensor'))
- input_grad: float32 [32, 729, 1152], P(('fsdp', 'heads', 'tensor'))
- ln1_gain_grad: float32 [1152], replicated
- ln1_bias_grad: float32 [1152], replicated
- qkv_weight_grad: float32 [1152, 3, 1152], P(('fsdp', 'tensor'), None, 'heads')
- qv_bias_grad: float32 [2, 1152], replicated
- out_weight_grad: float32 [1152, 1152], P('heads', ('fsdp', 'tensor'))
- out_bias_grad: float32 [1152], replicated
- ln2_gain_grad: float32 [1152], replicated
- ln2_bias_grad: float32 [1152], replicated
- up_weight_grad: float32 [1152, 4304], P(('fsdp', 'heads'), 'tensor')
- up_bias_grad: float32 [4304], replicated
- down_weight_grad: float32 [4304, 1152], P('tensor', ('fsdp', 'heads'))
- down_bias_grad: float32 [1152], replicated
The draws below stay inside these ranges and needn't reach their ends.
Inputs may be any that keep to these rules, and one draw needn't show every extreme that they name: slot_mask is 0 or 1; the 16 slots of some index of fsdp are all 1.
All inputs are finite; a program needn't handle non-finite values.
Results may differ from the reference program's by a relative error of at most 0.014.
Values may be sent and summed in bfloat16 or wider, within the bound.
No kernel may reach another device: no remote copies, remote signals or barrier semaphores. Data moves between devices by JAX's collectives and lax.ppermute only.
A program may use at most 256 MiB of HBM per device.

```python
import jax
import jax.numpy as jnp
from jax import lax

D = 1152
HEADS = 16
HEAD_DIM = 72
FF = 4304
SEQ = 729
HD = 1152
SLOTS = 16
IMAGES = 32
N_FSDP = 2


def draw_slot_mask(key, part):
    filled = (jax.random.randint(key, (IMAGES,), 0, 4) > 0).astype(jnp.int32)
    fullest = jax.random.randint(jax.random.fold_in(key, 7), (), 0, N_FSDP)
    group_index = jnp.arange(IMAGES, dtype=jnp.int32) // SLOTS
    return jnp.where(group_index == fullest, 1, filled).astype(jnp.int32)


def spiked(values, stream_key, source, target, shards_of, factor):
    def block_of(axis_at):
        return (jnp.arange(values.shape[axis_at]) // (values.shape[axis_at] // shards_of)).reshape((-1,) + (1,) * (values.ndim - 1 - axis_at))

    near = jax.random.permutation(stream_key, shards_of)[block_of(target)]
    second = (block_of(target) + shards_of // 2) % shards_of
    return jnp.where((block_of(source) == near) | (block_of(source) == second), factor * values, values)


def steps_of(stream_key, shape, cuts, least, top_value):
    def one(position, blocks):
        heights = jax.random.uniform(jax.random.fold_in(jax.random.fold_in(stream_key, 6), position), (blocks,), jnp.float32, least / len(cuts), top_value / len(cuts))
        return jnp.repeat(jnp.exp(heights), shape[position] // blocks).reshape((-1,) + (1,) * (len(shape) - position - 1))

    factor_of = one(*cuts[0])
    for cut in cuts[1:]:
        factor_of = factor_of * one(*cut)
    return factor_of


def noise(stream_key, extent, deviation, most, cuts=(), kind=jnp.bfloat16):
    values = jax.random.normal(stream_key, extent, jnp.float32) * deviation
    if len(cuts) > 0:
        values = steps_of(stream_key, extent, cuts, -0.22, 0.18) * values
    return jnp.clip(values, min=-most, max=most).astype(kind)


def bell_draw_with(own_key, dims, deviation, limit, split, heavy, kind=jnp.bfloat16):
    array = deviation * jax.random.normal(own_key, dims, jnp.float32)
    if split:
        array = array * steps_of(own_key, dims, split, -0.22, 0.18)
    return jnp.clip(spiked(array, jax.random.fold_in(own_key, 3), *heavy), -limit, limit).astype(kind)


def setup_inputs(seed: int = 0) -> dict:
    key_list = jax.random.split(jax.random.key(seed), 16)
    inputs = noise(key_list[0], (IMAGES, SEQ, D), 1.0, 6.0, ((0, 32),))
    slot_mask = draw_slot_mask(jax.random.fold_in(key_list[15], 71), 0)
    ln1_gain = jnp.clip(1.0 + 0.1 * jax.random.normal(key_list[2], (D,), jnp.float32), 0.5, 1.5)
    ln1_bias = noise(key_list[3], (D,), 0.1, 0.625, (), jnp.float32)
    qkv_weight = noise(key_list[4], (D, 3, HD), D ** -0.5, 0.1875, ((0, 8), (2, 4)), jnp.float32)
    qv_bias = noise(key_list[5], (2, HD), 0.1, 0.625, (), jnp.float32)
    out_weight = noise(key_list[6], (HD, D), 4 ** -0.5, 3.0, ((0, 4), (1, 8)), jnp.float32)
    out_bias = noise(key_list[7], (D,), 0.2, 1.25, (), jnp.float32)
    ln2_gain = jnp.clip(1.0 + 0.1 * jax.random.normal(key_list[8], (D,), jnp.float32), 0.5, 1.5)
    ln2_bias = noise(key_list[9], (D,), 0.1, 0.625, (), jnp.float32)
    up_weight = noise(key_list[10], (D, FF), D ** -0.5, 0.1875, ((0, 8), (1, 4)), jnp.float32)
    up_bias = noise(key_list[11], (FF,), 0.2, 1.25, (), jnp.float32)
    down_weight = noise(key_list[12], (FF, D), FF ** -0.5, 0.09375, ((0, 4), (1, 8)), jnp.float32)
    down_bias = noise(key_list[13], (D,), 0.2, 1.25, (), jnp.float32)
    out_grad = bell_draw_with(key_list[14], (IMAGES, SEQ, D), 1.0, 12.0, ((0, 32),), (0, 2, 32, 2.75))
    return dict(inputs=inputs, slot_mask=slot_mask, ln1_gain=ln1_gain, ln1_bias=ln1_bias, qkv_weight=qkv_weight, qv_bias=qv_bias, out_weight=out_weight, out_bias=out_bias, ln2_gain=ln2_gain, ln2_bias=ln2_bias, up_weight=up_weight, up_bias=up_bias, down_weight=down_weight, down_bias=down_bias, out_grad=out_grad)


@jax.custom_vjp
def low(v):
    return lax.optimization_barrier(v.astype(jnp.bfloat16)).astype(jnp.float32)

@jax.custom_vjp
def low_back(v):
    return v

def low_keep(v):
    return (low(v), None)

def low_pass(kept, grad):
    return (grad,)

def back_keep(v):
    return (v, None)

def back_low(kept, grad):
    return (low(grad),)
low.defvjp(low_keep, low_pass)
low_back.defvjp(back_keep, back_low)
epsilon = 1e-06

def both_ways(values):
    return low_back(low(values))

def matmul(left, right):
    return jnp.dot(left, right, precision=lax.Precision.HIGHEST, preferred_element_type=jnp.float32)

def layer_norm(values, scaling, offset):
    center = values - lax.optimization_barrier(jnp.mean(values, axis=-1, keepdims=True))
    spread = lax.optimization_barrier(jnp.mean(center * center, axis=-1, keepdims=True))
    return center * lax.rsqrt(spread + epsilon) * scaling + offset

def image_layer(image, valid_slot, params):
    ln1_gain, ln1_bias, qkv_weight, qv_bias, out_weight, out_bias, ln2_gain, ln2_bias, up_weight, up_bias, down_weight, down_bias = params
    length = image.shape[0]
    normed = low(layer_norm(image, ln1_gain, ln1_bias))
    qkv_low = low(qkv_weight)
    queries = both_ways(matmul(normed, qkv_low[:, 0]) + qv_bias[0]).reshape(length, HEADS, HEAD_DIM)
    key_rows = both_ways(matmul(normed, qkv_low[:, 1])).reshape(length, HEADS, HEAD_DIM)
    value_rows = both_ways(matmul(normed, qkv_low[:, 2]) + qv_bias[1]).reshape(length, HEADS, HEAD_DIM)
    scores = low_back(jnp.einsum('shd,thd->hst', queries, key_rows, precision=lax.Precision.HIGHEST) * HEAD_DIM ** (-0.5))
    probabilities = low(jax.nn.softmax(scores, axis=-1))
    mixed_rows = both_ways(jnp.einsum('hst,thd->shd', probabilities, value_rows, precision=lax.Precision.HIGHEST).reshape(length, HEADS * HEAD_DIM))
    attn_out = low_back(matmul(mixed_rows, low(out_weight)) + out_bias)
    hidden = image + attn_out
    normed_two = low(layer_norm(hidden, ln2_gain, ln2_bias))
    upper_pre = low_back(matmul(normed_two, low(up_weight)) + up_bias)
    active = low(jax.nn.gelu(upper_pre, approximate=True))
    mlp_out = low_back(matmul(active, low(down_weight)) + down_bias)
    return valid_slot * (hidden + mlp_out)

def reference(inputs, slot_mask, ln1_gain, ln1_bias, qkv_weight, qv_bias, out_weight, out_bias, ln2_gain, ln2_bias, up_weight, up_bias, down_weight, down_bias, out_grad):
    valid_slot = slot_mask.astype(jnp.float32)
    params = (ln1_gain, ln1_bias, qkv_weight, qv_bias, out_weight, out_bias, ln2_gain, ln2_bias, up_weight, up_bias, down_weight, down_bias)

    def forward(images, weights):

        def one_image(element):
            return jax.checkpoint(image_layer)(element[0], element[1], weights)
        return lax.map(one_image, (images, valid_slot))
    outputs, pullback = jax.vjp(forward, inputs.astype(jnp.float32), params)
    grad_inputs, grads = pullback(out_grad.astype(jnp.float32))
    return (outputs.astype(jnp.bfloat16), grad_inputs, grads[0], grads[1], grads[2], grads[3], grads[4], grads[5], grads[6], grads[7], grads[8], grads[9], grads[10], grads[11])
```

```python
import functools
import math

import jax
import jax.numpy as jnp
from jax import lax
from jax.experimental import pallas as pl
from jax.experimental.pallas import tpu as pltpu
from jax.sharding import PartitionSpec as P

HEAD_DIM = 72
GROUP_HEADS = 4
PAD = 768
EPS = 1e-06
VMEM_BYTES = 60 * 1024 * 1024
BF16 = jnp.bfloat16
F32 = jnp.float32
LOG2E = math.log2(math.e)


def nn(a, b):
    return lax.dot_general(a, b, (((1,), (0,)), ((), ())), preferred_element_type=F32)


def nt(a, b):
    return lax.dot_general(a, b, (((1,), (1,)), ((), ())), preferred_element_type=F32)


def tn(a, b):
    return lax.dot_general(a, b, (((0,), (0,)), ((), ())), preferred_element_type=F32)


def params(**kw):
    return pltpu.CompilerParams(vmem_limit_bytes=VMEM_BYTES, **kw)


def cost(flops, bytes_):
    return pl.CostEstimate(flops=int(flops), bytes_accessed=int(bytes_), transcendentals=0)


def whole(shape):
    zeros = (0,) * len(shape)
    return pl.BlockSpec(shape, lambda *_: zeros)


class Plan:
    def __init__(self, entries, columns):
        self.entries = entries
        self.columns = columns

    def copies(self, slot, pieces, table, dst, sems):
        for number, (piece, src, rows, to, entry, column) in enumerate(self.entries):
            if to != slot:
                continue
            row = pl.multiple_of(table[entry], 16)
            yield pltpu.make_async_copy(
                pieces[piece].at[pl.ds(src, rows), :],
                dst.at[pl.ds(row, rows), pl.ds(column, self.columns)],
                sems.at[number],
            )


def attn_fwd_kernel(plan, pieces_total, has_acc, seq, groups, *refs):
    table, x, bias = refs[:3]
    pieces = refs[3 : 3 + pieces_total]
    rest = refs[3 + pieces_total :]
    if has_acc:
        acc_in, rest = rest[0], rest[1:]
    proj, mixed, lse, acc, w_out, w, mixed_t, sems, out_sems = rest
    g = pl.program_id(0)
    width = GROUP_HEADS * HEAD_DIM
    keys = -(-seq // 16) * 16
    low = seq // 8 * 8
    scale = HEAD_DIM**-0.5 * LOG2E

    @pl.when(g == 0)
    def _():
        for slot in range(groups):
            for c in plan.copies(slot, pieces, table, w.at[slot], sems):
                c.start()

    for slot in range(groups):

        @pl.when(g == slot)
        def _(slot=slot):
            for c in plan.copies(slot, pieces, table, w.at[slot], sems):
                c.wait()
            pltpu.make_async_copy(w.at[slot], w_out.at[slot], out_sems.at[slot]).start()

    proj[0] = (nn(x[...], w[g, :, 0 : 3 * width]) + bias[0]).astype(BF16)
    for h in range(GROUP_HEADS):
        q = proj[0, :, h * HEAD_DIM : (h + 1) * HEAD_DIM]
        k = proj[0, 0:keys, width + h * HEAD_DIM : width + (h + 1) * HEAD_DIM]
        v = proj[0, 0:keys, 2 * width + h * HEAD_DIM : 2 * width + (h + 1) * HEAD_DIM]
        for c in range(0, PAD, QCHUNK):
            s = nt(k, q[c : c + QCHUNK])
            tail_rows = lax.broadcasted_iota(jnp.int32, (keys - low, QCHUNK), 0)
            tail = jnp.where(tail_rows < seq - low, s[low:keys], -1e30)
            top = jnp.maximum(
                jnp.max(s[0:low], axis=0, keepdims=True), jnp.max(tail, axis=0, keepdims=True)
            )
            shift = top * scale
            p = jnp.exp2(jnp.concatenate([s[0:low], tail], axis=0) * scale - shift)
            total = jnp.sum(p, axis=0, keepdims=True)
            o = tn(v, p.astype(BF16)) / total
            mixed_t[h * HEAD_DIM : (h + 1) * HEAD_DIM, c : c + QCHUNK] = o
            lse[0, h : h + 1, c : c + QCHUNK] = shift + jnp.log2(total)
    mixed[0] = mixed_t[...].T.astype(BF16)
    part = nt(mixed[0], w[g, :, 3 * width : 4 * width])

    @pl.when(g == 0)
    def _():
        acc[...] = part + acc_in[...] if has_acc else part

    @pl.when(g > 0)
    def _():
        acc[...] += part

    @pl.when(g == groups - 1)
    def _():
        for slot in range(groups):
            pltpu.make_async_copy(w.at[slot], w_out.at[slot], out_sems.at[slot]).wait()


QCHUNK = 768


def attn_fwd(table, x, bias, pieces, plan, acc_in, seq, groups):
    d = x.shape[1]
    gw = plan.columns
    width = GROUP_HEADS * HEAD_DIM
    has_acc = acc_in is not None
    args = [table, x, bias, *pieces] + ([acc_in] if has_acc else [])
    return pl.pallas_call(
        functools.partial(attn_fwd_kernel, plan, len(pieces), has_acc, seq, groups),
        grid=(groups,),
        in_specs=[
            pl.BlockSpec(memory_space=pltpu.SMEM),
            whole((PAD, d)),
            pl.BlockSpec((1, 1, 3 * width), lambda g: (g, 0, 0)),
            *[pl.BlockSpec(memory_space=pl.ANY) for _ in pieces],
            *([whole((PAD, d))] if has_acc else []),
        ],
        out_specs=[
            pl.BlockSpec((1, PAD, 3 * width), lambda g: (g, 0, 0)),
            pl.BlockSpec((1, PAD, width), lambda g: (g, 0, 0)),
            pl.BlockSpec((1, 8, PAD), lambda g: (g, 0, 0)),
            whole((PAD, d)),
            pl.BlockSpec(memory_space=pl.ANY),
        ],
        out_shape=[
            jax.ShapeDtypeStruct((groups, PAD, 3 * width), BF16),
            jax.ShapeDtypeStruct((groups, PAD, width), BF16),
            jax.ShapeDtypeStruct((groups, 8, PAD), F32),
            jax.ShapeDtypeStruct((PAD, d), F32),
            jax.ShapeDtypeStruct((groups, d, gw), BF16),
        ],
        scratch_shapes=[
            pltpu.VMEM((groups, d, gw), BF16),
            pltpu.VMEM((width, PAD), F32),
            pltpu.SemaphoreType.DMA((len(plan.entries),)),
            pltpu.SemaphoreType.DMA((groups,)),
        ],
        compiler_params=params(),
        cost_estimate=cost(
            groups * 2 * PAD * (d * 4 * width + 8 * PAD * 256), groups * (d * gw * 4 + PAD * d * 4)
        ),
        name="attn_fwd",
    )(*args)


def attn_bwd_kernel(has_acc, seq, groups, *refs):
    proj, lse, ga, w = refs[:4]
    rest = refs[4:]
    if has_acc:
        acc_in, rest = rest[0], rest[1:]
    dproj, acc, sums, gm, dq_t = rest
    g = pl.program_id(0)
    width = GROUP_HEADS * HEAD_DIM
    keys = -(-seq // 16) * 16
    low = seq // 8 * 8
    factor = HEAD_DIM**-0.5
    scale = factor * LOG2E
    gm[...] = nn(ga[...], w[0, :, 3 * width : 4 * width]).astype(BF16)
    for h in range(GROUP_HEADS):
        sl = slice(h * HEAD_DIM, (h + 1) * HEAD_DIM)
        q = proj[0, :, h * HEAD_DIM : (h + 1) * HEAD_DIM]
        k = proj[0, 0:keys, width + h * HEAD_DIM : width + (h + 1) * HEAD_DIM]
        v = proj[0, 0:keys, 2 * width + h * HEAD_DIM : 2 * width + (h + 1) * HEAD_DIM]
        do = gm[:, sl]
        dk = jnp.zeros((keys, HEAD_DIM), F32)
        dv = jnp.zeros((keys, HEAD_DIM), F32)
        for c in range(0, PAD, QCHUNK):
            qc, doc = q[c : c + QCHUNK], do[c : c + QCHUNK]
            s = nt(k, qc)
            e = s * scale - lse[0, h : h + 1, c : c + QCHUNK]
            tail_rows = lax.broadcasted_iota(jnp.int32, (keys - low, QCHUNK), 0)
            tail = jnp.where(tail_rows < seq - low, e[low:keys], -1e30)
            p = jnp.exp2(jnp.concatenate([e[0:low], tail], axis=0))
            dp = nt(v, doc)
            delta = jnp.sum(p * dp, axis=0, keepdims=True)
            ds = (p * (dp - delta)).astype(BF16)
            dv += nn(p.astype(BF16), doc)
            dk += nn(ds, qc)
            dq_t[sl, c : c + QCHUNK] = tn(k, ds)
        dproj[0, 0:keys, width + h * HEAD_DIM : width + (h + 1) * HEAD_DIM] = (dk * factor).astype(BF16)
        dproj[0, 0:keys, 2 * width + h * HEAD_DIM : 2 * width + (h + 1) * HEAD_DIM] = dv.astype(BF16)
    dproj[0, keys:PAD, width : 3 * width] = jnp.zeros((PAD - keys, 2 * width), BF16)
    dproj[0, :, 0:width] = (dq_t[...] * factor).T.astype(BF16)
    sums[0] = jnp.sum(dproj[0].astype(F32), axis=0, keepdims=True)
    part = nt(dproj[0], w[0, :, 0 : 3 * width])

    @pl.when(g == 0)
    def _():
        acc[...] = part + acc_in[...] if has_acc else part

    @pl.when(g > 0)
    def _():
        acc[...] += part


def attn_bwd(proj, lse, ga, w, acc_in, seq):
    groups, _, gw = w.shape
    d = ga.shape[1]
    width = GROUP_HEADS * HEAD_DIM
    has_acc = acc_in is not None
    args = [proj, lse, ga, w] + ([acc_in] if has_acc else [])
    return pl.pallas_call(
        functools.partial(attn_bwd_kernel, has_acc, seq, groups),
        grid=(groups,),
        in_specs=[
            pl.BlockSpec((1, PAD, 3 * width), lambda g: (g, 0, 0)),
            pl.BlockSpec((1, 8, PAD), lambda g: (g, 0, 0)),
            whole((PAD, d)),
            pl.BlockSpec((1, d, gw), lambda g: (g, 0, 0)),
            *([whole((PAD, d))] if has_acc else []),
        ],
        out_specs=[
            pl.BlockSpec((1, PAD, 3 * width), lambda g: (g, 0, 0)),
            whole((PAD, d)),
            pl.BlockSpec((1, 1, 3 * width), lambda g: (g, 0, 0)),
        ],
        out_shape=[
            jax.ShapeDtypeStruct((groups, PAD, 3 * width), BF16),
            jax.ShapeDtypeStruct((PAD, d), F32),
            jax.ShapeDtypeStruct((groups, 1, 3 * width), F32),
        ],
        scratch_shapes=[pltpu.VMEM((PAD, width), BF16), pltpu.VMEM((width, PAD), F32)],
        compiler_params=params(),
        cost_estimate=cost(
            groups * 2 * PAD * (d * 4 * width + 20 * PAD * 256), groups * (d * gw * 2 + PAD * d * 4)
        ),
        name="attn_bwd",
    )(*args)


def tile_of(units):
    return next(t for t in (1024, 768, 512, 256, 128) if units % t == 0)


def first_need(tile, columns, slots):
    return [slot * columns // tile for slot in range(slots)]


def ff_up_kernel(plan, pieces_total, slots, tile, *refs):
    table, x, bias = refs[:3]
    pieces = refs[3 : 3 + pieces_total]
    active, slope, w_out, w, sems, out_sems = refs[3 + pieces_total :]
    n = pl.program_id(0)
    cols = plan.columns

    @pl.when(n == 0)
    def _():
        for slot in range(slots):
            for c in plan.copies(slot, pieces, table, w, sems):
                c.start()

    def out_copy(slot):
        part = pl.ds(slot * cols, cols)
        return pltpu.make_async_copy(w.at[:, part], w_out.at[:, part], out_sems.at[slot])

    for slot, step in enumerate(first_need(tile, cols, slots)):

        @pl.when(n == step)
        def _(slot=slot):
            for c in plan.copies(slot, pieces, table, w, sems):
                c.wait()
            out_copy(slot).start()

    u = nn(x[...], w[:, pl.ds(pl.multiple_of(n * tile, tile), tile)]) + bias[...]
    root = math.sqrt(2.0 / math.pi)
    square = u * u
    t = jnp.tanh(u * (root + (root * 0.044715) * square))
    half = 0.5 * (1.0 + t)
    active[...] = (u * half).astype(BF16)
    slope[...] = (
        half + (0.5 * u) * (1.0 - t * t) * (root + (3.0 * root * 0.044715) * square)
    ).astype(BF16)

    @pl.when(n == pl.num_programs(0) - 1)
    def _():
        for slot in range(slots):
            out_copy(slot).wait()


def ff_up(table, x, bias, pieces, plan, slots):
    d = x.shape[1]
    units = slots * plan.columns
    tile = tile_of(units)
    return pl.pallas_call(
        functools.partial(ff_up_kernel, plan, len(pieces), slots, tile),
        grid=(units // tile,),
        in_specs=[
            pl.BlockSpec(memory_space=pltpu.SMEM),
            whole((PAD, d)),
            pl.BlockSpec((1, tile), lambda n: (0, n)),
            *[pl.BlockSpec(memory_space=pl.ANY) for _ in pieces],
        ],
        out_specs=[
            pl.BlockSpec((PAD, tile), lambda n: (0, n)),
            pl.BlockSpec((PAD, tile), lambda n: (0, n)),
            pl.BlockSpec(memory_space=pl.ANY),
        ],
        out_shape=[
            jax.ShapeDtypeStruct((PAD, units), BF16),
            jax.ShapeDtypeStruct((PAD, units), BF16),
            jax.ShapeDtypeStruct((d, units), BF16),
        ],
        scratch_shapes=[
            pltpu.VMEM((d, units), BF16),
            pltpu.SemaphoreType.DMA((len(plan.entries),)),
            pltpu.SemaphoreType.DMA((slots,)),
        ],
        compiler_params=params(),
        cost_estimate=cost(2 * PAD * d * units, 4 * d * units + 4 * PAD * units),
        name="ff_up",
    )(table, x, bias, *pieces)


def ff_down_kernel(plan, pieces_total, slots, tile, *refs):
    table, gl, active, slope = refs[:4]
    pieces = refs[4 : 4 + pieces_total]
    acc, gu, sums, w, sems = refs[4 + pieces_total :]
    n = pl.program_id(0)
    cols = plan.columns

    @pl.when(n == 0)
    def _():
        for slot in range(slots):
            for c in plan.copies(slot, pieces, table, w, sems):
                c.start()

    for slot, step in enumerate(first_need(tile, cols, slots)):

        @pl.when(n == step)
        def _(slot=slot):
            for c in plan.copies(slot, pieces, table, w, sems):
                c.wait()

    wt = w[:, pl.ds(pl.multiple_of(n * tile, tile), tile)]
    grad = (nn(gl[...], wt) * slope[...].astype(F32)).astype(BF16)
    gu[...] = grad
    sums[...] = jnp.sum(grad.astype(F32), axis=0, keepdims=True)
    part = nt(active[...], wt)

    @pl.when(n == 0)
    def _():
        acc[...] = part

    @pl.when(n > 0)
    def _():
        acc[...] += part


def ff_down(table, gl, active, slope, pieces, plan, slots):
    d = gl.shape[1]
    units = slots * plan.columns
    tile = tile_of(units)
    return pl.pallas_call(
        functools.partial(ff_down_kernel, plan, len(pieces), slots, tile),
        grid=(units // tile,),
        in_specs=[
            pl.BlockSpec(memory_space=pltpu.SMEM),
            whole((PAD, d)),
            pl.BlockSpec((PAD, tile), lambda n: (0, n)),
            pl.BlockSpec((PAD, tile), lambda n: (0, n)),
            *[pl.BlockSpec(memory_space=pl.ANY) for _ in pieces],
        ],
        out_specs=[
            whole((PAD, d)),
            pl.BlockSpec((PAD, tile), lambda n: (0, n)),
            pl.BlockSpec((1, tile), lambda n: (0, n)),
        ],
        out_shape=[
            jax.ShapeDtypeStruct((PAD, d), F32),
            jax.ShapeDtypeStruct((PAD, units), BF16),
            jax.ShapeDtypeStruct((1, units), F32),
        ],
        scratch_shapes=[
            pltpu.VMEM((d, units), BF16),
            pltpu.SemaphoreType.DMA((len(plan.entries),)),
        ],
        compiler_params=params(),
        cost_estimate=cost(4 * PAD * d * units, 2 * d * units + 6 * PAD * units),
        name="ff_down",
    )(table, gl, active, slope, *pieces)


def ff_back_kernel(gu, w, acc):
    part = nt(gu[...], w[...])

    @pl.when(pl.program_id(0) == 0)
    def _():
        acc[...] = part

    @pl.when(pl.program_id(0) > 0)
    def _():
        acc[...] += part


def ff_back(gu, w):
    d, units = w.shape
    tile = tile_of(units)
    return pl.pallas_call(
        ff_back_kernel,
        grid=(units // tile,),
        in_specs=[
            pl.BlockSpec((PAD, tile), lambda n: (0, n)),
            pl.BlockSpec((d, tile), lambda n: (0, n)),
        ],
        out_specs=whole((PAD, d)),
        out_shape=jax.ShapeDtypeStruct((PAD, d), F32),
        compiler_params=params(),
        cost_estimate=cost(2 * PAD * d * units, 2 * d * units + 2 * PAD * units),
        name="ff_back",
    )(gu, w)


def turn_kernel(blocks, table, x, out):
    rows = x.shape[1] // blocks
    t = x[...].T
    for b in range(blocks):
        out[pl.ds(pl.multiple_of(table[b], 16), rows), :] = t[b * rows : (b + 1) * rows, :]


def turn(table, x):
    blocks = table.shape[0]
    d = x.shape[1]
    return pl.pallas_call(
        functools.partial(turn_kernel, blocks),
        in_specs=[pl.BlockSpec(memory_space=pltpu.SMEM), pl.BlockSpec(memory_space=pltpu.VMEM)],
        out_specs=pl.BlockSpec(memory_space=pltpu.VMEM),
        out_shape=jax.ShapeDtypeStruct((d, PAD), BF16),
        compiler_params=params(),
        cost_estimate=cost(PAD * d * 8, PAD * d * 4),
        name="turn",
    )(table, x)


def ff_grad_kernel(total, parts, rows, *refs):
    lhs, rhs, outs = refs[:total], refs[total : 2 * total], refs[2 * total :]
    value = nn(lhs[0][...], rhs[0][...])
    for a, b in zip(lhs[1:], rhs[1:]):
        value += nn(a[...], b[...])
    for number in range(parts):
        outs[number][0] = value[number * rows : (number + 1) * rows].astype(BF16)


def ff_grad(lhs, rhs, slots, parts):
    total = len(lhs)
    height = lhs[0].shape[0]
    rows = height // parts
    cols = rhs[0].shape[1] // slots
    return pl.pallas_call(
        functools.partial(ff_grad_kernel, total, parts, rows),
        grid=(slots,),
        in_specs=[
            *[whole((height, PAD)) for _ in lhs],
            *[pl.BlockSpec((PAD, cols), lambda n: (0, n)) for _ in rhs],
        ],
        out_specs=[pl.BlockSpec((1, rows, cols), lambda n: (n, 0, 0)) for _ in range(parts)],
        out_shape=[jax.ShapeDtypeStruct((slots, rows, cols), BF16) for _ in range(parts)],
        compiler_params=params(),
        cost_estimate=cost(
            2 * total * PAD * height * slots * cols, 2 * slots * cols * (total * PAD + height)
        ),
        name="ff_grad",
    )(*lhs, *rhs)


def attn_grad_kernel(total, parts, slots, rows, *refs):
    na, dp = refs[:total], refs[total : 2 * total]
    ga, mx = refs[2 * total : 3 * total], refs[3 * total : 4 * total]
    outs = refs[4 * total :]
    left = nn(na[0][...], dp[0][0])
    right = nn(ga[0][...], mx[0][0])
    for i in range(1, total):
        left += nn(na[i][...], dp[i][0])
        right += nn(ga[i][...], mx[i][0])
    cut = left.shape[1]
    for part in range(parts):
        for slot in range(slots):
            block = slice((part * slots + slot) * rows, (part * slots + slot + 1) * rows)
            outs[part][slot, 0, :, 0:cut] = left[block].astype(BF16)
            outs[part][slot, 0, :, cut:] = right[block].astype(BF16)


def attn_grad(na, dp, ga, mx, parts, slots):
    total = len(na)
    height = na[0].shape[0]
    rows = height // (parts * slots)
    groups, _, cut = dp[0].shape
    cols = cut + mx[0].shape[2]
    return pl.pallas_call(
        functools.partial(attn_grad_kernel, total, parts, slots, rows),
        grid=(groups,),
        in_specs=[
            *[whole((height, PAD)) for _ in na],
            *[pl.BlockSpec((1, PAD, cut), lambda g: (g, 0, 0)) for _ in dp],
            *[whole((height, PAD)) for _ in ga],
            *[pl.BlockSpec((1, PAD, cols - cut), lambda g: (g, 0, 0)) for _ in mx],
        ],
        out_specs=[
            pl.BlockSpec((slots, 1, rows, cols), lambda g: (0, g, 0, 0)) for _ in range(parts)
        ],
        out_shape=[jax.ShapeDtypeStruct((slots, groups, rows, cols), BF16) for _ in range(parts)],
        compiler_params=params(),
        cost_estimate=cost(
            2 * total * PAD * height * groups * cols, 2 * groups * cols * (total * PAD + height)
        ),
        name="attn_grad",
    )(*na, *dp, *ga, *mx)


def layer_norm(values, scaling, offset):
    center = values - jnp.mean(values, axis=-1, keepdims=True)
    spread = jnp.mean(center * center, axis=-1, keepdims=True)
    return center * lax.rsqrt(spread + EPS) * scaling + offset


def hop(x, axis, n, step):
    return lax.ppermute(x, axis, [(i, (i + step) % n) for i in range(n)])


def cat(*arrays):
    return jnp.concatenate(arrays, axis=0)


def total_sum(value, sizes):
    for axis, n in sizes.items():
        step = 1
        while step < n:
            value = value + lax.ppermute(value, axis, [(i, i ^ step) for i in range(n)])
            step *= 2
    return value


class Links:
    def __init__(self, sizes, rows):
        self.nz = sizes["z"]
        nz = self.nz
        self.rows = rows
        blocks = [(dy, dz) for dy in range(2) for dz in range(nz)]
        self.attn_plans = []
        for dc in range(2):
            entries = []
            for dx in range(2):
                for dy, dz in blocks:
                    if dc == 1:
                        piece, at = dy, dz * 2 + dx
                    elif dy == 0:
                        piece, at = dz, dx
                    else:
                        piece, at = nz + dz // 2, dz % 2 * 2 + dx
                    entries.append((piece, at * rows, rows, dx, dy * nz + dz, 0))
            self.attn_plans.append(entries)
        self.ff_entries = []
        for dz in range(nz):
            for dc in range(2):
                for dy in range(2):
                    for dx in range(2):
                        if dc == 0:
                            piece, at = dx * 2 + dy, dz
                        else:
                            piece, at = 4 + dx, dy * nz + dz
                        self.ff_entries.append((piece, at * rows, rows, dz, dc * 4 + dy * 2 + dx))

    def gather_attn(self, own):
        s = [cat(own, hop(own, "x", 2, 1))]
        for _ in range(self.nz - 1):
            s.append(hop(s[-1], "z", self.nz, 1))
        y = [hop(cat(*s[i : i + 2]), "y", 2, 1) for i in range(0, self.nz, 2)]
        far = [hop(cat(*s), "c", 2, 1), hop(cat(*y), "c", 2, 1)]
        return [s + y, far]

    def gather_ff(self, own):
        u = [own]
        for _ in range(self.nz - 1):
            u.append(hop(u[-1], "z", self.nz, 1))
        y = [hop(cat(*u[i : i + 2]), "y", 2, 1) for i in range(0, self.nz, 2)]
        a, b = cat(*u), cat(*y)
        xa, xb = hop(a, "x", 2, 1), hop(b, "x", 2, 1)
        return [a, b, xa, xb, hop(cat(a, b), "c", 2, 1), hop(cat(xa, xb), "c", 2, 1)]

    def line(self, part):
        value = part[self.nz - 1]
        for k in range(self.nz - 2, -1, -1):
            value = hop(value, "z", self.nz, -1) + part[k]
        return value

    def scatter_ff(self, parts):
        p00, p01, p10, p11 = parts
        far = p10 + hop(p11, "x", 2, 1)
        near = p00 + hop(p01, "x", 2, 1) + hop(far, "y", 2, 1)
        return self.line(near)

    def scatter_attn(self, parts):
        pair = self.line(parts[0] + hop(parts[1], "y", 2, 1))
        return pair[0] + hop(pair[1], "x", 2, 1)


def on_device(
    sizes,
    inputs,
    slot_mask,
    ln1_gain,
    ln1_bias,
    qkv_weight,
    qv_bias,
    out_weight,
    out_bias,
    ln2_gain,
    ln2_bias,
    up_weight,
    up_bias,
    down_weight,
    down_bias,
    out_grad,
):
    seq, d = inputs.shape[1:]
    ny, nx, nc, nz = (sizes[a] for a in ("y", "x", "c", "z"))
    yi, xi, ci, zi = (lax.axis_index(a) for a in ("y", "x", "c", "z"))
    width = GROUP_HEADS * HEAD_DIM
    unit_width = up_weight.shape[1]
    cols = -(-unit_width // 128) * 128
    a_rows, f_rows = qkv_weight.shape[0], up_weight.shape[0]
    linked = ny == nx == nc == 2 and nz % 2 == 0 and a_rows % 16 == 0 and f_rows % 16 == 0

    attn_own = jnp.concatenate(
        [qkv_weight.reshape(a_rows, 3 * width).astype(BF16), out_weight.T.astype(BF16)], axis=1
    )
    spare = ((0, 0), (0, cols - unit_width))
    up_own = jnp.pad(up_weight.astype(BF16), spare)
    down_own = jnp.pad(down_weight.T.astype(BF16), spare)

    if linked:
        links = Links(sizes, a_rows)
        ffl = Links(sizes, f_rows)
        attn_pieces = links.gather_attn(attn_own)
        up_pieces, down_pieces = ffl.gather_ff(up_own), ffl.gather_ff(down_own)
        attn_plans = [Plan(e, attn_own.shape[1]) for e in links.attn_plans]
        ff_plan = Plan([e + (e[3] * cols,) for e in ffl.ff_entries], cols)
        attn_table = jnp.stack(
            [((yi ^ dy) * nz + (zi - dz) % nz) * a_rows for dy in range(2) for dz in range(nz)]
        )
        ff_table = jnp.stack(
            [
                (((yi ^ dy) * 2 + (xi ^ dx)) * 2 + (ci ^ dc)) * f_rows
                for dc in range(2)
                for dy in range(2)
                for dx in range(2)
            ]
        )
        turn_attn = jnp.stack(
            [((yi ^ b // nz) * nz + (zi - b % nz) % nz) * a_rows for b in range(2 * nz)]
        )
        turn_ff = jnp.stack(
            [
                ((ci ^ b % 2) * 4 + (yi ^ b // 4) * 2 + (xi ^ b // 2 % 2)) * f_rows
                for b in range(8)
            ]
        )
        halves = [[(xi ^ dx) * 2 + (ci ^ dc) for dx in range(2)] for dc in range(2)]
        zones = [(zi - dz) % nz for dz in range(nz)]
    else:
        heads = ("x", "c")
        whole_attn = lax.all_gather(attn_own, ("y", "z"), axis=0, tiled=True)
        whole_attn = lax.all_gather(whole_attn, heads, axis=0)
        attn_pieces = [[whole_attn[g] for g in range(nx * nc)]]
        spot = ("y", "x", "c")
        up_whole = lax.all_gather(up_own, spot, axis=0, tiled=True)
        up_whole = lax.all_gather(up_whole, "z", axis=0)
        down_whole = lax.all_gather(down_own, spot, axis=0, tiled=True)
        down_whole = lax.all_gather(down_whole, "z", axis=0)
        up_pieces = [up_whole[k] for k in range(nz)]
        down_pieces = [down_whole[k] for k in range(nz)]
        attn_plans = [Plan([(g, 0, d, g, 0, 0) for g in range(nx * nc)], attn_own.shape[1])]
        ff_plan = Plan([(k, 0, d, k, 0, k * cols) for k in range(nz)], cols)
        attn_table = ff_table = turn_attn = turn_ff = jnp.zeros((1,), jnp.int32)
        halves = [list(range(nx * nc))]
        zones = list(range(nz))

    valid = slot_mask[0].astype(F32)
    token_pad = ((0, PAD - seq), (0, 0))
    residual = jnp.pad(inputs[0], token_pad).astype(F32)
    real = lax.broadcasted_iota(jnp.int32, (PAD, 1), 0) < seq

    def norm(v, g, b):
        return jnp.where(real, layer_norm(v, g, b), 0.0)

    normed_a, back_a = jax.vjp(norm, residual, ln1_gain, ln1_bias)
    normed_a = normed_a.astype(BF16)

    def bias_rows(group):
        part = lax.dynamic_slice_in_dim(qv_bias, group * width, width, 1)
        return jnp.concatenate([part[0], jnp.zeros_like(part[0]), part[1]])[None]

    acc = None
    kept = []
    for pieces, plan, groups in zip(attn_pieces, attn_plans, halves):
        bias = jnp.stack([bias_rows(g) for g in groups])
        proj, mixed, lse, acc, w = attn_fwd(
            attn_table, normed_a, bias, pieces, plan, acc, seq, len(groups)
        )
        kept.append((proj, mixed, lse, w))
    hidden = residual + (acc + out_bias)

    normed_b, back_b = jax.vjp(norm, hidden, ln2_gain, ln2_bias)
    normed_b = normed_b.astype(BF16)
    grad_low = (valid * jnp.pad(out_grad[0], token_pad).astype(F32)).astype(BF16)
    shift = jnp.concatenate(
        [
            jnp.pad(lax.dynamic_slice_in_dim(up_bias, k * unit_width, unit_width), spare[1])
            for k in zones
        ]
    )[None]
    active, slope, up_full = ff_up(ff_table, normed_b, shift, up_pieces, ff_plan, nz)
    mlp, grad_upper, upper_sums = ff_down(
        ff_table, grad_low, active, slope, down_pieces, ff_plan, nz
    )
    output = (valid * (hidden + (mlp + down_bias)))[:seq].astype(BF16)[None]

    def swap(x):
        return hop(x, "c", 2, 1)

    nb_t, gl_t = turn(turn_ff, normed_b), turn(turn_ff, grad_low)
    if linked:
        half = d // 2
        down_lhs = [gl_t[:half], swap(gl_t[half:])]
        up_lhs = [nb_t[:half], swap(nb_t[half:])]
        down_parts = ff_grad(down_lhs, [active, swap(active)], nz, 4)
        down_sum = ffl.scatter_ff(down_parts)
        up_parts = ff_grad(up_lhs, [grad_upper, swap(grad_upper)], nz, 4)
        up_sum = ffl.scatter_ff(up_parts)
    else:
        spot = ("y", "x", "c")

        def spread(parts):
            part = lax.psum_scatter(parts[0], "z", scatter_dimension=0, tiled=True)[0]
            part = lax.psum_scatter(part, spot, scatter_dimension=0, tiled=True)
            return lax.optimization_barrier(part)

        down_sum = spread(ff_grad([gl_t], [active], nz, 1))
        up_sum = spread(ff_grad([nb_t], [grad_upper], nz, 1))

    grad_normed_b = ff_back(grad_upper, up_full)
    through, ln2_gain_grad, ln2_bias_grad = back_b(grad_normed_b)
    grad_hidden = grad_low.astype(F32) + through
    grad_attn = grad_hidden.astype(BF16)

    na_t, ga_t = turn(turn_attn, normed_a), turn(turn_attn, grad_attn)
    acc = None
    grads, sums = [], []
    for proj, mixed, lse, w in kept[::-1]:
        dproj, acc, part_sums = attn_bwd(proj, lse, grad_attn, w, acc, seq)
        grads.insert(0, dproj)
        sums.insert(0, part_sums)
    if linked:
        parts = attn_grad(
            [na_t, swap(na_t)],
            [grads[0], swap(grads[1])],
            [ga_t, swap(ga_t)],
            [kept[0][1], swap(kept[1][1])],
            2,
            nz,
        )
        attn_sum = links.scatter_attn(parts)
    else:
        part = attn_grad([na_t], grads, [ga_t], [kept[0][1]], 1, 1)[0][0]
        part = lax.psum_scatter(part, ("x", "c"), scatter_dimension=0, tiled=True)[0]
        attn_sum = lax.psum_scatter(part, ("y", "z"), scatter_dimension=0, tiled=True)
        attn_sum = lax.optimization_barrier(attn_sum)
    through, ln1_gain_grad, ln1_bias_grad = back_a(acc)
    input_grad = (grad_hidden + through)[:seq][None]

    qv_sum = jnp.zeros_like(qv_bias)
    for groups, part_sums in zip(halves, sums):
        for k, g in enumerate(groups):
            row = part_sums[k, 0]
            pair = jnp.stack([row[:width], row[2 * width :]])
            qv_sum = lax.dynamic_update_slice_in_dim(qv_sum, pair, g * width, 1)
    up_shift = jnp.zeros_like(up_bias)
    for slot, k in enumerate(zones):
        piece = upper_sums[0, slot * cols : slot * cols + unit_width]
        up_shift = lax.dynamic_update_slice_in_dim(up_shift, piece, k * unit_width, 0)
    vectors = [
        ln1_gain_grad,
        ln1_bias_grad,
        qv_sum.reshape(-1),
        jnp.sum(grad_attn.astype(F32), axis=0),
        ln2_gain_grad,
        ln2_bias_grad,
        up_shift,
        jnp.sum(grad_low.astype(F32), axis=0),
    ]
    lengths = [v.shape[0] for v in vectors]
    flat = jnp.concatenate(vectors)
    fill = -flat.shape[0] % 1024
    flat = total_sum(jnp.pad(flat, (0, fill)).reshape(-1, 128), sizes).reshape(-1)
    out = []
    start = 0
    for n in lengths:
        out.append(flat[start : start + n])
        start += n

    qkv_grad = attn_sum[:, : 3 * width].astype(F32).reshape(a_rows, 3, width)
    out_weight_grad = attn_sum[:, 3 * width :].astype(F32).T
    up_grad = up_sum[:, :unit_width].astype(F32)
    down_grad = down_sum[:, :unit_width].astype(F32).T
    return (
        output,
        input_grad,
        out[0],
        out[1],
        qkv_grad,
        out[2].reshape(qv_bias.shape),
        out_weight_grad,
        out[3],
        out[4],
        out[5],
        up_grad,
        out[6],
        down_grad,
        out[7],
    )


def solution(mesh):
    heads = mesh.shape["heads"]
    sizes = {"y": mesh.shape["fsdp"], "x": heads // 2, "c": 2, "z": mesh.shape["tensor"]}
    split = jax.sharding.Mesh(mesh.devices.reshape(tuple(sizes.values())), tuple(sizes))
    images = P(("y", "x", "c", "z"), None, None)
    attn_in = P(("y", "z"), None, ("x", "c"))
    attn_out = P(("x", "c"), ("y", "z"))
    up, down = P(("y", "x", "c"), "z"), P("z", ("y", "x", "c"))
    in_specs = (
        images,
        P(("y", "x", "c", "z")),
        P(),
        P(),
        attn_in,
        P(),
        attn_out,
        P(),
        P(),
        P(),
        up,
        P(),
        down,
        P(),
        images,
    )
    out_specs = (
        images,
        images,
        P(),
        P(),
        attn_in,
        P(),
        attn_out,
        P(),
        P(),
        P(),
        up,
        P(),
        down,
        P(),
    )
    return jax.shard_map(
        functools.partial(on_device, sizes),
        mesh=split,
        in_specs=in_specs,
        out_specs=out_specs,
        check_vma=False,
    )
```

```python
import functools
import math

import jax
import jax.numpy as jnp
from jax import lax
from jax.experimental import pallas as pl
from jax.experimental.pallas import tpu as pltpu
from jax.sharding import PartitionSpec as P

HEAD_DIM = 72
GROUP_HEADS = 4
PAD = 768
EPS = 1e-06
VMEM_BYTES = 60 * 1024 * 1024
BF16 = jnp.bfloat16
F32 = jnp.float32
LOG2E = math.log2(math.e)


def nn(a, b):
    return lax.dot_general(a, b, (((1,), (0,)), ((), ())), preferred_element_type=F32)


def nt(a, b):
    return lax.dot_general(a, b, (((1,), (1,)), ((), ())), preferred_element_type=F32)


def tn(a, b):
    return lax.dot_general(a, b, (((0,), (0,)), ((), ())), preferred_element_type=F32)


def params(**kw):
    return pltpu.CompilerParams(vmem_limit_bytes=VMEM_BYTES, **kw)


def cost(flops, bytes_, scale=64):
    return pl.CostEstimate(
        flops=int(flops * scale), bytes_accessed=int(bytes_ * scale), transcendentals=0
    )


def whole(shape):
    zeros = (0,) * len(shape)
    return pl.BlockSpec(shape, lambda *_: zeros)


class Plan:
    def __init__(self, entries, columns):
        self.entries = entries
        self.columns = columns

    def copies(self, slot, pieces, table, dst, sems):
        for number, (piece, src, rows, to, entry, inside, column) in enumerate(self.entries):
            if to != slot:
                continue
            row = pl.multiple_of(table[entry] + inside, 16)
            yield pltpu.make_async_copy(
                pieces[piece].at[pl.ds(src, rows), :],
                dst.at[pl.ds(row, rows), pl.ds(column, self.columns)],
                sems.at[number],
            )


class ZonePlan:
    def __init__(self, slots, rows, columns):
        self.entries = range(slots)
        self.rows = rows
        self.columns = columns

    def copies(self, slot, pieces, table, dst, sems):
        row = pl.multiple_of(table[slot], 16)
        yield pltpu.make_async_copy(
            pieces[0].at[pl.ds(row, self.rows), :],
            dst.at[:, pl.ds(slot * self.columns, self.columns)],
            sems.at[slot],
        )


def masked_tail(values, low, seq):
    tail = values[low:]
    rows = lax.broadcasted_iota(jnp.int32, tail.shape, 0)
    return jnp.where(rows < seq - low, tail, -1e30)


def attn_fwd_kernel(plan, pieces_total, has_acc, seq, *refs):
    table, x, bias = refs[:3]
    pieces = refs[3 : 3 + pieces_total]
    rest = refs[3 + pieces_total :]
    if has_acc:
        acc_in, rest = rest[0], rest[1:]
    proj, mixed, lse, acc, w, mixed_t, sems = rest
    width = GROUP_HEADS * HEAD_DIM
    keys = -(-seq // 16) * 16
    low = seq // 8 * 8
    scale = HEAD_DIM**-0.5 * LOG2E

    for c in plan.copies(0, pieces, table, w, sems):
        c.start()
    for c in plan.copies(0, pieces, table, w, sems):
        c.wait()

    proj[...] = (nn(x[...], w[:, 0 : 3 * width]) + bias[...]).astype(BF16)
    for h in range(GROUP_HEADS):
        q = proj[:, h * HEAD_DIM : (h + 1) * HEAD_DIM]
        k = proj[0:keys, width + h * HEAD_DIM : width + (h + 1) * HEAD_DIM]
        v = proj[0:keys, 2 * width + h * HEAD_DIM : 2 * width + (h + 1) * HEAD_DIM]
        s = nt(k, q)
        tail = masked_tail(s, low, seq)
        top = jnp.maximum(
            jnp.max(s[0:low], axis=0, keepdims=True), jnp.max(tail, axis=0, keepdims=True)
        )
        shift = top * scale
        p = jnp.exp2(jnp.concatenate([s[0:low], tail], axis=0) * scale - shift)
        total = jnp.sum(p, axis=0, keepdims=True)
        mixed_t[h * HEAD_DIM : (h + 1) * HEAD_DIM, :] = tn(v, p.astype(BF16)) / total
        lse[h : h + 1, :] = shift + jnp.log2(total)
    mixed[...] = mixed_t[...].T.astype(BF16)
    part = nt(mixed[...], w[:, 3 * width : 4 * width])
    acc[...] = part + acc_in[...] if has_acc else part


def attn_fwd(table, x, bias, pieces, plan, acc_in, seq):
    d = x.shape[1]
    gw = plan.columns
    width = GROUP_HEADS * HEAD_DIM
    has_acc = acc_in is not None
    vmem = pl.BlockSpec(memory_space=pltpu.VMEM)
    return pl.pallas_call(
        functools.partial(attn_fwd_kernel, plan, len(pieces), has_acc, seq),
        in_specs=[
            pl.BlockSpec(memory_space=pltpu.SMEM),
            vmem,
            vmem,
            *[pl.BlockSpec(memory_space=pl.ANY) for _ in pieces],
            *([vmem] if has_acc else []),
        ],
        out_specs=[vmem] * 5,
        out_shape=[
            jax.ShapeDtypeStruct((PAD, 3 * width), BF16),
            jax.ShapeDtypeStruct((PAD, width), BF16),
            jax.ShapeDtypeStruct((8, PAD), F32),
            jax.ShapeDtypeStruct((PAD, d), F32),
            jax.ShapeDtypeStruct((d, gw), BF16),
        ],
        scratch_shapes=[
            pltpu.VMEM((width, PAD), F32),
            pltpu.SemaphoreType.DMA((len(plan.entries),)),
        ],
        compiler_params=params(),
        cost_estimate=cost(
            2 * PAD * (d * 4 * width + 8 * PAD * 256), d * gw * 4 + PAD * d * 8, 0.05),
        name="attn_fwd",
    )(table, x, bias, *pieces, *([acc_in] if has_acc else []))


def attn_bwd_kernel(has_acc, seq, *refs):
    proj, mixed, lse, ga, w = refs[:5]
    rest = refs[5:]
    if has_acc:
        acc_in, rest = rest[0], rest[1:]
    grads, acc, sums, gm, dq_t = rest
    width = GROUP_HEADS * HEAD_DIM
    keys = -(-seq // 16) * 16
    low = seq // 8 * 8
    factor = HEAD_DIM**-0.5
    scale = factor * LOG2E
    gm[...] = nn(ga[...], w[:, 3 * width : 4 * width]).astype(BF16)
    for h in range(GROUP_HEADS):
        sl = slice(h * HEAD_DIM, (h + 1) * HEAD_DIM)
        q = proj[:, h * HEAD_DIM : (h + 1) * HEAD_DIM]
        k = proj[0:keys, width + h * HEAD_DIM : width + (h + 1) * HEAD_DIM]
        v = proj[0:keys, 2 * width + h * HEAD_DIM : 2 * width + (h + 1) * HEAD_DIM]
        do = gm[:, sl]
        e = nt(k, q) * scale - lse[h : h + 1, :]
        p = jnp.exp2(jnp.concatenate([e[0:low], masked_tail(e, low, seq)], axis=0))
        dp = nt(v, do)
        delta = jnp.sum(p * dp, axis=0, keepdims=True)
        ds = (p * (dp - delta)).astype(BF16)
        dv = nn(p.astype(BF16), do)
        dk = nn(ds, q)
        dq_t[sl, :] = tn(k, ds)
        grads[0:keys, width + h * HEAD_DIM : width + (h + 1) * HEAD_DIM] = (dk * factor).astype(
            BF16
        )
        grads[0:keys, 2 * width + h * HEAD_DIM : 2 * width + (h + 1) * HEAD_DIM] = dv.astype(BF16)
    grads[keys:PAD, width : 3 * width] = jnp.zeros((PAD - keys, 2 * width), BF16)
    grads[:, 0:width] = (dq_t[...] * factor).T.astype(BF16)
    value = grads[:, 0 : 3 * width]
    sums[...] = jnp.sum(value.astype(F32), axis=0, keepdims=True)
    part = nt(value, w[:, 0 : 3 * width])
    grads[:, 3 * width : 4 * width] = mixed[...]
    acc[...] = part + acc_in[...] if has_acc else part


def attn_bwd(proj, mixed, lse, ga, w, acc_in, seq):
    d, gw = w.shape
    width = GROUP_HEADS * HEAD_DIM
    has_acc = acc_in is not None
    vmem = pl.BlockSpec(memory_space=pltpu.VMEM)
    return pl.pallas_call(
        functools.partial(attn_bwd_kernel, has_acc, seq),
        in_specs=[vmem] * (6 if has_acc else 5),
        out_specs=[vmem] * 3,
        out_shape=[
            jax.ShapeDtypeStruct((PAD, gw), BF16),
            jax.ShapeDtypeStruct((PAD, d), F32),
            jax.ShapeDtypeStruct((1, 3 * width), F32),
        ],
        scratch_shapes=[pltpu.VMEM((PAD, width), BF16), pltpu.VMEM((width, PAD), F32)],
        compiler_params=params(),
        cost_estimate=cost(
            2 * PAD * (d * 4 * width + 20 * PAD * 256), d * gw * 2 + PAD * d * 8
        ),
        name="attn_bwd",
    )(proj, mixed, lse, ga, w, *([acc_in] if has_acc else []))


def tile_of(units):
    return next(t for t in (1024, 768, 512, 256, 128) if units % t == 0)


def first_need(tile, columns, slots):
    return [slot * columns // tile for slot in range(slots)]


def ff_up_kernel(plan, pieces_total, slots, tile, *refs):
    table, x, bias = refs[:3]
    pieces = refs[3 : 3 + pieces_total]
    active, slope, w_out, w, sems, out_sems = refs[3 + pieces_total :]
    n = pl.program_id(0)
    cols = plan.columns

    @pl.when(n == 0)
    def _():
        for slot in range(slots):
            for c in plan.copies(slot, pieces, table, w, sems):
                c.start()

    def out_copy(slot):
        part = pl.ds(slot * cols, cols)
        return pltpu.make_async_copy(w.at[:, part], w_out.at[:, part], out_sems.at[slot])

    for slot, step in enumerate(first_need(tile, cols, slots)):

        @pl.when(n == step)
        def _(slot=slot):
            for c in plan.copies(slot, pieces, table, w, sems):
                c.wait()
            out_copy(slot).start()

    u = nn(x[...], w[:, pl.ds(pl.multiple_of(n * tile, tile), tile)]) + bias[...]
    root = math.sqrt(2.0 / math.pi)
    square = u * u
    t = jnp.tanh(u * (root + (root * 0.044715) * square))
    half = 0.5 * (1.0 + t)
    active[...] = (u * half).astype(BF16)
    slope[...] = (
        half + (0.5 * u) * (1.0 - t * t) * (root + (3.0 * root * 0.044715) * square)
    ).astype(BF16)

    @pl.when(n == pl.num_programs(0) - 1)
    def _():
        for slot in range(slots):
            out_copy(slot).wait()


def ff_up(table, x, bias, pieces, plan, slots):
    d = x.shape[1]
    units = slots * plan.columns
    tile = tile_of(units)
    return pl.pallas_call(
        functools.partial(ff_up_kernel, plan, len(pieces), slots, tile),
        grid=(units // tile,),
        in_specs=[
            pl.BlockSpec(memory_space=pltpu.SMEM),
            whole((PAD, d)),
            pl.BlockSpec((1, tile), lambda n: (0, n)),
            *[pl.BlockSpec(memory_space=pl.ANY) for _ in pieces],
        ],
        out_specs=[
            pl.BlockSpec((PAD, tile), lambda n: (0, n)),
            pl.BlockSpec((PAD, tile), lambda n: (0, n)),
            pl.BlockSpec(memory_space=pl.ANY),
        ],
        out_shape=[
            jax.ShapeDtypeStruct((PAD, units), BF16),
            jax.ShapeDtypeStruct((PAD, units), BF16),
            jax.ShapeDtypeStruct((d, units), BF16),
        ],
        scratch_shapes=[
            pltpu.VMEM((d, units), BF16),
            pltpu.SemaphoreType.DMA((len(plan.entries),)),
            pltpu.SemaphoreType.DMA((slots,)),
        ],
        compiler_params=params(),
        cost_estimate=cost(2 * PAD * d * units, 4 * d * units + 4 * PAD * units, 0.05),
        name="ff_up",
    )(table, x, bias, *pieces)


def ff_down_kernel(plan, pieces_total, slots, tile, *refs):
    table, gl, active, slope = refs[:4]
    pieces = refs[4 : 4 + pieces_total]
    acc, gu, sums, w, sems = refs[4 + pieces_total :]
    n = pl.program_id(0)
    cols = plan.columns

    @pl.when(n == 0)
    def _():
        for slot in range(slots):
            for c in plan.copies(slot, pieces, table, w, sems):
                c.start()

    for slot, step in enumerate(first_need(tile, cols, slots)):

        @pl.when(n == step)
        def _(slot=slot):
            for c in plan.copies(slot, pieces, table, w, sems):
                c.wait()

    wt = w[:, pl.ds(pl.multiple_of(n * tile, tile), tile)]
    grad = (nn(gl[...], wt) * slope[...].astype(F32)).astype(BF16)
    gu[...] = grad
    sums[...] = jnp.sum(grad.astype(F32), axis=0, keepdims=True)
    part = nt(active[...], wt)

    @pl.when(n == 0)
    def _():
        acc[...] = part

    @pl.when(n > 0)
    def _():
        acc[...] += part


def ff_down(table, gl, active, slope, pieces, plan, slots):
    d = gl.shape[1]
    units = slots * plan.columns
    tile = tile_of(units)
    return pl.pallas_call(
        functools.partial(ff_down_kernel, plan, len(pieces), slots, tile),
        grid=(units // tile,),
        in_specs=[
            pl.BlockSpec(memory_space=pltpu.SMEM),
            whole((PAD, d)),
            pl.BlockSpec((PAD, tile), lambda n: (0, n)),
            pl.BlockSpec((PAD, tile), lambda n: (0, n)),
            *[pl.BlockSpec(memory_space=pl.ANY) for _ in pieces],
        ],
        out_specs=[
            whole((PAD, d)),
            pl.BlockSpec((PAD, tile), lambda n: (0, n)),
            pl.BlockSpec((1, tile), lambda n: (0, n)),
        ],
        out_shape=[
            jax.ShapeDtypeStruct((PAD, d), F32),
            jax.ShapeDtypeStruct((PAD, units), BF16),
            jax.ShapeDtypeStruct((1, units), F32),
        ],
        scratch_shapes=[
            pltpu.VMEM((d, units), BF16),
            pltpu.SemaphoreType.DMA((len(plan.entries),)),
        ],
        compiler_params=params(),
        cost_estimate=cost(4 * PAD * d * units, 2 * d * units + 6 * PAD * units, 0.05),
        name="ff_down",
    )(table, gl, active, slope, *pieces)


def ff_back_kernel(gu, w, acc):
    part = nt(gu[...], w[...])

    @pl.when(pl.program_id(0) == 0)
    def _():
        acc[...] = part

    @pl.when(pl.program_id(0) > 0)
    def _():
        acc[...] += part


def ff_back(gu, w):
    d, units = w.shape
    tile = tile_of(units)
    return pl.pallas_call(
        ff_back_kernel,
        grid=(units // tile,),
        in_specs=[
            pl.BlockSpec((PAD, tile), lambda n: (0, n)),
            pl.BlockSpec((d, tile), lambda n: (0, n)),
        ],
        out_specs=whole((PAD, d)),
        out_shape=jax.ShapeDtypeStruct((PAD, d), F32),
        compiler_params=params(),
        cost_estimate=cost(2 * PAD * d * units, 2 * d * units + 2 * PAD * units),
        name="ff_back",
    )(gu, w)


def put_turned(table, blocks, value, out):
    t = value.T
    rows = t.shape[0] // blocks
    for b in range(blocks):
        out[pl.ds(pl.multiple_of(table[b], 16), rows), :] = t[b * rows : (b + 1) * rows, :]


def turn_kernel(blocks, table, x, out, sums):
    value = x[...]
    put_turned(table, blocks, value, out)
    sums[...] = jnp.sum(value.astype(F32), axis=0, keepdims=True)


def specs(total):
    return [pl.BlockSpec(memory_space=pltpu.SMEM)] + [pl.BlockSpec(memory_space=pltpu.VMEM)] * total


def turn(table, x):
    d = x.shape[1]
    return pl.pallas_call(
        functools.partial(turn_kernel, table.shape[0]),
        in_specs=specs(1),
        out_specs=specs(2)[1:],
        out_shape=[jax.ShapeDtypeStruct((d, PAD), BF16), jax.ShapeDtypeStruct((1, d), F32)],
        compiler_params=params(),
        cost_estimate=cost(PAD * d * 8, PAD * d * 4, 0.05),
        name="turn",
    )(table, x)


def centered(v):
    c = v - jnp.mean(v, axis=-1, keepdims=True)
    return c, lax.rsqrt(jnp.mean(c * c, axis=-1, keepdims=True) + EPS)


def norm_kernel(blocks, seq, has_acc, *refs):
    if has_acc:
        table, base, acc, extra, gain, bias, hidden, normed, turned = refs
        v = base[...].astype(F32) + (acc[...] + extra[...])
        hidden[...] = v
    else:
        table, base, gain, bias, normed, turned = refs
        v = base[...].astype(F32)
    c, r = centered(v)
    value = c * r * gain[...] + bias[...]
    rows = lax.broadcasted_iota(jnp.int32, value.shape, 0)
    low = jnp.where(rows < seq, value, 0.0).astype(BF16)
    normed[...] = low
    put_turned(table, blocks, low, turned)


def norm(table, base, acc, extra, gain, bias, seq):
    d = base.shape[1]
    has_acc = acc is not None
    args = [base] + ([acc, extra[None]] if has_acc else []) + [gain[None], bias[None]]
    outs = [jax.ShapeDtypeStruct((PAD, d), BF16), jax.ShapeDtypeStruct((d, PAD), BF16)]
    if has_acc:
        outs = [jax.ShapeDtypeStruct((PAD, d), F32)] + outs
    return pl.pallas_call(
        functools.partial(norm_kernel, table.shape[0], seq, has_acc),
        in_specs=specs(len(args)),
        out_specs=specs(len(outs))[1:],
        out_shape=outs,
        compiler_params=params(),
        cost_estimate=cost(PAD * d * 16, PAD * d * 10, 0.05),
        name="norm",
    )(table, *args)


def norm_back_kernel(blocks, seq, with_low, *refs):
    table, v, e, gain, base, grad, gain_sum, bias_sum, *low_refs = refs
    c, r = centered(v[...].astype(F32))
    u = c * r
    scaled = e[...] * gain[...]
    inner = jnp.mean(scaled * u, axis=-1, keepdims=True)
    value = base[...].astype(F32) + r * (
        scaled - jnp.mean(scaled, axis=-1, keepdims=True) - u * inner
    )
    gain_sum[...] = jnp.sum(e[...] * u, axis=0, keepdims=True)
    bias_sum[...] = jnp.sum(e[...], axis=0, keepdims=True)
    if with_low:
        grad[...] = value
        low, turned, low_sum = low_refs
        rounded = value.astype(BF16)
        low[...] = rounded
        put_turned(table, blocks, rounded, turned)
        low_sum[...] = jnp.sum(rounded.astype(F32), axis=0, keepdims=True)
    else:
        grad[...] = value[0:seq]


def norm_back(table, v, e, gain, base, seq, with_low):
    d = v.shape[1]
    row = jax.ShapeDtypeStruct((1, d), F32)
    outs = [jax.ShapeDtypeStruct((PAD if with_low else seq, d), F32), row, row]
    if with_low:
        outs += [
            jax.ShapeDtypeStruct((PAD, d), BF16),
            jax.ShapeDtypeStruct((d, PAD), BF16),
            row,
        ]
    return pl.pallas_call(
        functools.partial(norm_back_kernel, table.shape[0], seq, with_low),
        in_specs=specs(4),
        out_specs=specs(len(outs))[1:],
        out_shape=outs,
        compiler_params=params(),
        cost_estimate=cost(PAD * d * 24, PAD * d * 18),
        name="norm_back",
    )(table, v, e, gain[None], base)


def ff_grad_kernel(total, parts, rows, *refs):
    lhs, rhs, outs = refs[:total], refs[total : 2 * total], refs[2 * total :]
    value = nn(lhs[0][...], rhs[0][...])
    for a, b in zip(lhs[1:], rhs[1:]):
        value += nn(a[...], b[...])
    for number in range(parts):
        outs[number][0] = value[number * rows : (number + 1) * rows].astype(BF16)


def ff_grad(lhs, rhs, slots, parts):
    total = len(lhs)
    height = lhs[0].shape[0]
    rows = height // parts
    cols = rhs[0].shape[1] // slots
    return pl.pallas_call(
        functools.partial(ff_grad_kernel, total, parts, rows),
        grid=(slots,),
        in_specs=[
            *[whole((height, PAD)) for _ in lhs],
            *[pl.BlockSpec((PAD, cols), lambda n: (0, n)) for _ in rhs],
        ],
        out_specs=[pl.BlockSpec((1, rows, cols), lambda n: (n, 0, 0)) for _ in range(parts)],
        out_shape=[jax.ShapeDtypeStruct((slots, rows, cols), BF16) for _ in range(parts)],
        compiler_params=params(),
        cost_estimate=cost(
            2 * total * PAD * height * slots * cols, 2 * slots * cols * (total * PAD + height)
        ),
        name="ff_grad",
    )(*lhs, *rhs)


def attn_grad_kernel(total, parts, has_more, *refs):
    na, ga, g = refs[:total], refs[total : 2 * total], refs[2 * total : 3 * total]
    more, outs = refs[3 * total : -parts], refs[-parts:]
    cut = 3 * GROUP_HEADS * HEAD_DIM
    rows = na[0].shape[0] // parts
    for part in range(parts):
        block = slice(part * rows, (part + 1) * rows)
        for lhs, columns in ((na, slice(0, cut)), (ga, slice(cut, None))):
            value = nn(lhs[0][block, :], g[0][:, columns])
            for i in range(1, total):
                value += nn(lhs[i][block, :], g[i][:, columns])
            if has_more:
                value += more[part][:, columns].astype(F32)
            outs[part][:, columns] = value.astype(BF16)


def attn_grad(na, ga, grads, parts, more=()):
    total = len(na)
    d = na[0].shape[0]
    cols = grads[0].shape[1]
    args = [*na, *ga, *grads, *more]
    return pl.pallas_call(
        functools.partial(attn_grad_kernel, total, parts, len(more) > 0),
        in_specs=specs(len(args))[1:],
        out_specs=specs(parts)[1:],
        out_shape=[jax.ShapeDtypeStruct((d // parts, cols), BF16) for _ in range(parts)],
        compiler_params=params(),
        cost_estimate=cost(2 * total * PAD * d * cols, 2 * cols * (total * PAD + 2 * d)),
        name="attn_grad",
    )(*args)


def hop(x, axis, n, step):
    return lax.ppermute(x, axis, [(i, (i + step) % n) for i in range(n)])


def cat(*arrays):
    return jnp.concatenate(arrays, axis=0)


def after(x, *others):
    return lax.optimization_barrier((x, others))[0]


def total_sum(value, sizes):
    for axis, n in sizes.items():
        step = 1
        while step < n:
            value = value + lax.ppermute(value, axis, [(i, i ^ step) for i in range(n)])
            step *= 2
    return value


def attn_entries(nz, rows, h):
    g = rows - h
    plans = {}
    for dc in range(2):
        for dx in range(2):
            entries = []
            for dy in range(2):
                for dz in range(nz):
                    if dy == 0:
                        one = (dz, dz * 2 * rows, dx * h)
                    else:
                        one = (nz + dz // 2, dz // 2 * 4 * h, dz % 2 * 2 * h + dx * h)
                    if dx == 0:
                        two = (dz, dz * 2 * rows, 2 * h + dy * g)
                    else:
                        two = (
                            nz + nz // 2 + dz // 2,
                            2 * nz * h + dz // 2 * 4 * g,
                            dz % 2 * 2 * g + dy * g,
                        )
                    for (piece, base, at), size, inside in ((one, h, 0), (two, g, h)):
                        if dc == 1:
                            piece, at = (0 if piece < nz else 1), base + at
                        entries.append((piece, at, size, 0, dy * nz + dz, inside, 0))
            plans[dc, dx] = entries
    return plans


def ff_entries(nz, rows, cols):
    entries = []
    for dz in range(nz):
        for dy in range(2):
            for dx in range(2):
                if dy == 0:
                    if dx == 0:
                        near = dz, 0
                    elif dz == 0:
                        near = nz, 0
                    else:
                        near = nz + 1, dz - 1
                    far = nz + 5, dx * nz + dz
                elif dz == 0:
                    near = nz + 2, dx
                    far = nz + 6, dx
                elif dx == 0:
                    near = nz + 3, dz - 1
                    far = nz + 6, 1 + dz
                else:
                    near = nz + 4, dz - 1
                    far = nz + 7, dz - 1
                for dc, (piece, at) in enumerate((near, far)):
                    entries.append(
                        (piece, at * rows, rows, dz, dc * 4 + dy * 2 + dx, 0, dz * cols)
                    )
    return entries


def on_device(
    sizes,
    inputs,
    slot_mask,
    ln1_gain,
    ln1_bias,
    qkv_weight,
    qv_bias,
    out_weight,
    out_bias,
    ln2_gain,
    ln2_bias,
    up_weight,
    up_bias,
    down_weight,
    down_bias,
    out_grad,
):
    seq, d = inputs.shape[1:]
    ny, nx, nc, nz = (sizes[a] for a in ("y", "x", "c", "z"))
    yi, xi, ci, zi = (lax.axis_index(a) for a in ("y", "x", "c", "z"))
    width = GROUP_HEADS * HEAD_DIM
    unit_width = up_weight.shape[1]
    cols = -(-unit_width // 128) * 128
    a_rows, f_rows = qkv_weight.shape[0], up_weight.shape[0]
    linked = ny == nx == nc == 2 and nz % 2 == 0 and a_rows % 16 == 0 and f_rows % 16 == 0

    attn_own = jnp.concatenate(
        [qkv_weight.reshape(a_rows, 3 * width).astype(BF16), out_weight.T.astype(BF16)], axis=1
    )
    spare = ((0, 0), (0, cols - unit_width))
    up_own = jnp.pad(up_weight.astype(BF16), spare)
    down_own = jnp.pad(down_weight.T.astype(BF16), spare)

    def swap(x, axis="c"):
        return hop(x, axis, 2, 1)

    if linked:
        h = -(-a_rows // 32) * 16
        order = [(dc, dx) for dc in range(2) for dx in range(2)]
        entries = attn_entries(nz, a_rows, h)
        attn_plans = [Plan(entries[o], 4 * width) for o in order]
        groups = [(xi ^ dx) * 2 + (ci ^ dc) for dc, dx in order]
        down_plan = Plan(ff_entries(nz, f_rows, cols), cols)
        zones = [(zi - dz) % nz for dz in range(nz)]
        attn_table = jnp.stack(
            [((yi ^ dy) * nz + (zi - dz) % nz) * a_rows for dy in range(2) for dz in range(nz)]
        )
        ff_table = jnp.stack(
            [
                (((yi ^ dy) * 2 + (xi ^ dx)) * 2 + (ci ^ dc)) * f_rows
                for dc in range(2)
                for dy in range(2)
                for dx in range(2)
            ]
        )
        turn_attn = jnp.stack(
            [((yi ^ b // nz) * nz + (zi - b % nz) % nz) * a_rows for b in range(2 * nz)]
        )
        turn_ff = jnp.stack(
            [
                ((ci ^ b % 2) * 4 + (yi ^ b // 4) * 2 + (xi ^ b // 2 % 2)) * f_rows
                for b in range(8)
            ]
        )
    else:
        whole_attn = lax.all_gather(attn_own, ("y", "z"), axis=0, tiled=True)
        whole_attn = lax.all_gather(whole_attn, ("x", "c"), axis=0)
        down_whole = lax.all_gather(down_own, ("z", "y", "x", "c"), axis=0, tiled=True)
        up_whole = lax.all_gather(up_own, ("z", "y", "x", "c"), axis=0, tiled=True)
        attn_pieces = [[whole_attn[g]] for g in range(nx * nc)]
        attn_plans = [Plan([(0, 0, d, 0, 0, 0, 0)], 4 * width)] * (nx * nc)
        attn_table = ff_table = turn_attn = turn_ff = jnp.zeros((1,), jnp.int32)
        groups = list(range(nx * nc))
        zones = list(range(nz))
    up_plan = ZonePlan(nz, d, cols)
    zone_table = jnp.stack([jnp.asarray(k, jnp.int32) * d for k in zones])

    valid = slot_mask[0].astype(F32)
    token_pad = ((0, PAD - seq), (0, 0))
    base = jnp.pad(inputs[0], token_pad)
    grad_low = (valid * jnp.pad(out_grad[0], token_pad).astype(F32)).astype(BF16)
    bias_rows = []
    for g in groups:
        part = lax.dynamic_slice_in_dim(qv_bias, g * width, width, 1)
        bias_rows.append(jnp.concatenate([part[0], jnp.zeros_like(part[0]), part[1]])[None])
    shift = jnp.concatenate(
        [
            jnp.pad(lax.dynamic_slice_in_dim(up_bias, k * unit_width, unit_width), spare[1])
            for k in zones
        ]
    )[None]
    normed_a, na_t = norm(turn_attn, base, None, None, ln1_gain, ln1_bias, seq)
    gl_t, down_bias_sum = turn(turn_ff, grad_low)

    together = lax.optimization_barrier
    if linked:
        half = d // 2
        px, py, down_xa = together(
            (swap(attn_own[:h], "x"), swap(attn_own[h:], "y"), swap(down_own, "x"))
        )
        s = [cat(attn_own[:h], px, attn_own[h:], py)]
        s1, down_ya, na_far = together(
            (
                hop(s[0], "z", nz, 1),
                swap(cat(down_own, after(down_xa, px)), "y"),
                swap(after(na_t, px)),
            )
        )
        s.append(s1)
        y_parts, x_parts = [], []
        gl_first = gl_t[half:]
        for k in range(2, nz):
            moves = [hop(s[-1], "z", nz, 1)]
            if k % 2 == 0:
                moves.append(swap(cat(s[k - 2][: 2 * h], s[k - 1][: 2 * h]), "y"))
                moves.append(swap(cat(s[k - 2][2 * h :], s[k - 1][2 * h :]), "x"))
            elif k == 3:
                gl_far = swap(after(gl_first, s[-1]))
                moves.append(gl_far)
            moves = together(tuple(moves))
            s.append(moves[0])
            if k % 2 == 0:
                y_parts.append(moves[1])
                x_parts.append(moves[2])
            elif k == 3:
                gl_far = moves[1]
        moves = together(
            (
                swap(cat(s[-2][: 2 * h], s[-1][: 2 * h]), "y"),
                swap(cat(s[-2][2 * h :], s[-1][2 * h :]), "x"),
                swap(cat(*s)),
            )
        )
        y_parts.append(moves[0])
        x_parts.append(moves[1])
        up_whole = lax.all_gather(after(up_own, s[2]), ("z", "y", "x", "c"), axis=0, tiled=True)
        near = [*s, *y_parts, *x_parts]
        far = [moves[2], swap(cat(*y_parts, *x_parts))]
        down_first = after(down_own, moves[2])
        down_z = [down_own] + [hop(down_first, "z", nz, k) for k in range(1, nz)]

        kept = []
        acc = None
        for number in range(4):
            pieces = near if number < 2 else far
            proj, mixed, lse, acc, w = attn_fwd(
                attn_table, normed_a, bias_rows[number], pieces, attn_plans[number], acc, seq
            )
            kept.append((proj, mixed, lse, w))
            if number == 1:
                acc, down_z, far = together((acc, down_z, far))
                down_xb = swap(cat(*down_z[1:]), "x")
                down_yb = swap(cat(*down_z[1:]), "y")
            if number == 3:
                acc, down_xb, down_yb = together((acc, down_xb, down_yb))
                down_yc = swap(down_xb, "y")
                down_c0 = swap(cat(*down_z, down_xa, down_xb))
                down_c1 = swap(cat(down_ya, down_yb))
    else:
        kept = []
        acc = None
        for number, g in enumerate(groups):
            proj, mixed, lse, acc, w = attn_fwd(
                attn_table,
                normed_a,
                bias_rows[number],
                attn_pieces[number],
                attn_plans[number],
                acc,
                seq,
            )
            kept.append((proj, mixed, lse, w))

    hidden, normed_b, nb_t = norm(turn_ff, base, acc, out_bias, ln2_gain, ln2_bias, seq)
    if linked:
        nb_far = swap(nb_t[half:])
    active, slope, up_full = ff_up(zone_table, normed_b, shift, [up_whole], up_plan, nz)
    if linked:
        active, down_yc, down_c0, down_c1, nb_far = together(
            (active, down_yc, down_c0, down_c1, nb_far)
        )
        down_c2 = swap(down_yc)
        down_pieces = [*down_z, down_xa, down_xb, down_ya, down_yb, down_yc]
        down_pieces += [down_c0, down_c1, down_c2]
        active_far = swap(active)
    else:
        down_plan, ff_table, down_pieces = up_plan, zone_table, [down_whole]
    mlp, grad_upper, upper_sums = ff_down(
        ff_table, grad_low, active, slope, down_pieces, down_plan, nz
    )
    output = (valid * (hidden + (mlp + down_bias)))[:seq].astype(BF16)[None]

    def plus(*values):
        return sum(v.astype(F32) for v in values).astype(BF16)

    if linked:
        grad_upper, active_far = together((grad_upper, active_far))
        upper_far = swap(grad_upper)
        down_parts = ff_grad([gl_t[:half], gl_far], [active, active_far], nz, 4)
        down_one, down_two = swap(down_parts[3], "x"), swap(down_parts[1], "x")
        grad_normed_b = ff_back(after(grad_upper, down_parts), up_full)
    else:
        spot = ("y", "x", "c")

        def spread(parts):
            part = lax.psum_scatter(parts[0], "z", scatter_dimension=0, tiled=True)[0]
            part = lax.psum_scatter(part, spot, scatter_dimension=0, tiled=True)
            return lax.optimization_barrier(part).astype(F32)

        down_sum = spread(ff_grad([gl_t], [active], nz, 1))
        up_sum = spread(ff_grad([nb_t], [grad_upper], nz, 1))
        grad_normed_b = ff_back(grad_upper, up_full)

    grad_hidden, ln2_gain_grad, ln2_bias_grad, grad_attn, ga_t, out_bias_sum = norm_back(
        turn_attn, hidden, grad_normed_b, ln2_gain, grad_low, seq, True
    )

    acc = None
    sums = [None] * len(groups)
    if linked:
        grads = {}
        ga_far = swap(ga_t)

        def back(number, acc):
            proj, mixed, lse, w = kept[number]
            grads[number], acc, sums[number] = attn_bwd(proj, mixed, lse, ga_first, w, acc, seq)
            return acc

        ga_first, down_one = together((grad_attn, down_one))
        down_one = plus(down_parts[2], down_one)
        down_other = swap(down_one, "y")
        ga_first = after(ga_first, down_one)
        acc = back(3, None)
        far_grads = swap(grads[3])
        acc = back(1, acc)
        acc, far_grads, ga_far, down_two, down_other = together(
            (acc, far_grads, ga_far, down_two, down_other)
        )
        down_value = plus(down_parts[0], down_two, down_other)
        down_line = hop(down_value[nz - 1], "z", nz, -1)
        more = attn_grad(
            [after(na_t, down_value), na_far], [ga_t, ga_far], [grads[1], far_grads], 2
        )
        more_one, more_two = swap(more[1], "x"), swap(more[0], "x")
        upper_first, upper_far = together((grad_upper, upper_far, more))[:2]
        up_parts = ff_grad([nb_t[:half], nb_far], [upper_first, upper_far], nz, 4)
        up_parts, down_line, acc = together((up_parts, down_line, acc))
        up_one, up_two = swap(up_parts[3], "y"), swap(up_parts[2], "y")
        down_line = hop(plus(down_line, down_value[nz - 2]), "z", nz, -1)
        acc = back(2, acc)
        far_grads = swap(grads[2])
        acc, more_one, down_line = together((acc, more_one, down_line))
        for k in range(nz - 3, 0, -1):
            down_line = hop(plus(down_line, down_value[k]), "z", nz, -1)
        acc = back(0, acc)
        acc, far_grads, up_one, down_line = together((acc, far_grads, up_one, down_line))
        up_one = plus(up_parts[1], up_one)
        up_other = swap(up_one, "x")
        input_grad, ln1_gain_grad, ln1_bias_grad = norm_back(
            turn_attn, base, after(acc, up_one), ln1_gain, grad_hidden, seq, False
        )
        na_first, more_two, up_two, up_other, input_grad = together(
            (na_t, more_two, up_two, up_other, input_grad)
        )
        total = attn_grad(
            [na_first, na_far], [ga_t, ga_far], [grads[0], far_grads], 2, (more_two, more_one)
        )
        far_y = swap(total[1], "y")
        up_value = plus(up_parts[0], up_two, up_other)
        up_line = hop(after(up_value[nz - 1], total[0]), "z", nz, -1)
        for k in range(nz - 2, 0, -1):
            up_line = hop(plus(up_line, up_value[k]), "z", nz, -1)
        far_y, up_line, near_y = together((far_y, up_line, total[0]))
        last = plus(near_y, far_y).reshape(nz, a_rows, 4 * width)
        last_far = [hop(last[k], "z", nz, -k) for k in range(1, nz)]
        down_sum = down_line.astype(F32) + down_value[0].astype(F32)
        up_sum = up_line.astype(F32) + up_value[0].astype(F32)
        attn_sum = sum(v.astype(F32) for v in (last[0], *last_far))
    else:
        parts = []
        for number, (proj, mixed, lse, w) in enumerate(kept):
            g, acc, sums[number] = attn_bwd(proj, mixed, lse, grad_attn, w, acc, seq)
            parts.append(attn_grad([na_t], [ga_t], [g], 1)[0])
        part = lax.psum_scatter(jnp.stack(parts), ("x", "c"), scatter_dimension=0, tiled=True)[0]
        part = lax.psum_scatter(part, ("y", "z"), scatter_dimension=0, tiled=True)
        attn_sum = lax.optimization_barrier(part).astype(F32)
        input_grad, ln1_gain_grad, ln1_bias_grad = norm_back(
            turn_attn, base, acc, ln1_gain, grad_hidden, seq, False
        )

    def in_place(rows, places):
        at = jnp.arange(len(rows))[:, None]
        return sum(jnp.where(at == p, r, 0.0) for r, p in zip(rows, places))

    wide = max(d, 3 * width, cols)

    def fit(x):
        return jnp.pad(x, ((0, 0), (0, wide - x.shape[1])))

    vectors = [
        ln1_gain_grad,
        ln1_bias_grad,
        out_bias_sum,
        ln2_gain_grad,
        ln2_bias_grad,
        down_bias_sum,
        in_place(sums, groups),
        in_place(
            [upper_sums[:, slot * cols : (slot + 1) * cols] for slot in range(nz)], zones
        ),
    ]
    table = cat(*[fit(v) for v in vectors])
    fill = -table.shape[0] % 8
    table = total_sum(jnp.pad(table, ((0, fill), (0, 0))), sizes)
    singles = [table[k, :d] for k in range(6)]
    qv = table[6 : 6 + len(groups)]
    qv_grad = jnp.stack([qv[:, :width].reshape(-1), qv[:, 2 * width : 3 * width].reshape(-1)])
    up_bias_grad = table[6 + len(groups) : 6 + len(groups) + nz, :unit_width].reshape(-1)

    qkv_grad = attn_sum[:, : 3 * width].reshape(a_rows, 3, width)
    out_weight_grad = attn_sum[:, 3 * width :].T
    up_grad = up_sum[:, :unit_width]
    down_grad = down_sum[:, :unit_width].T
    return (
        output,
        input_grad[None],
        singles[0],
        singles[1],
        qkv_grad,
        qv_grad,
        out_weight_grad,
        singles[2],
        singles[3],
        singles[4],
        up_grad,
        up_bias_grad,
        down_grad,
        singles[5],
    )


def solution(mesh):
    heads = mesh.shape["heads"]
    sizes = {"y": mesh.shape["fsdp"], "x": heads // 2, "c": 2, "z": mesh.shape["tensor"]}
    split = jax.sharding.Mesh(mesh.devices.reshape(tuple(sizes.values())), tuple(sizes))
    images = P(("y", "x", "c", "z"), None, None)
    attn_in = P(("y", "z"), None, ("x", "c"))
    attn_out = P(("x", "c"), ("y", "z"))
    up, down = P(("y", "x", "c"), "z"), P("z", ("y", "x", "c"))
    in_specs = (
        images,
        P(("y", "x", "c", "z")),
        P(),
        P(),
        attn_in,
        P(),
        attn_out,
        P(),
        P(),
        P(),
        up,
        P(),
        down,
        P(),
        images,
    )
    out_specs = (
        images,
        images,
        P(),
        P(),
        attn_in,
        P(),
        attn_out,
        P(),
        P(),
        P(),
        up,
        P(),
        down,
        P(),
    )
    return jax.shard_map(
        functools.partial(on_device, sizes),
        mesh=split,
        in_specs=in_specs,
        out_specs=out_specs,
        check_vma=False,
    )
```

```python
import functools
import math

import jax
import jax.numpy as jnp
from jax import lax
from jax.experimental import pallas as pl
from jax.experimental.pallas import tpu as pltpu
from jax.sharding import PartitionSpec as P

HEAD_DIM = 72
GROUP_HEADS = 4
PAD = 768
EPS = 1e-06
VMEM_BYTES = 60 * 1024 * 1024
BF16 = jnp.bfloat16
F32 = jnp.float32
LOG2E = math.log2(math.e)


def nn(a, b):
    return lax.dot_general(a, b, (((1,), (0,)), ((), ())), preferred_element_type=F32)


def nt(a, b):
    return lax.dot_general(a, b, (((1,), (1,)), ((), ())), preferred_element_type=F32)


def tn(a, b):
    return lax.dot_general(a, b, (((0,), (0,)), ((), ())), preferred_element_type=F32)


def params(**kw):
    return pltpu.CompilerParams(vmem_limit_bytes=VMEM_BYTES, **kw)


def cost(flops, bytes_, scale=64):
    return pl.CostEstimate(
        flops=int(flops * scale), bytes_accessed=int(bytes_ * scale), transcendentals=0
    )


def whole(shape):
    zeros = (0,) * len(shape)
    return pl.BlockSpec(shape, lambda *_: zeros)


class Plan:
    def __init__(self, entries, columns):
        self.entries = entries
        self.columns = columns

    def copies(self, slot, pieces, table, dst, sems):
        for number, (piece, src, rows, to, entry, inside, column) in enumerate(self.entries):
            if to != slot:
                continue
            row = pl.multiple_of(table[entry] + inside, 16)
            yield pltpu.make_async_copy(
                pieces[piece].at[pl.ds(src, rows), :],
                dst.at[pl.ds(row, rows), pl.ds(column, self.columns)],
                sems.at[number],
            )


class ZonePlan:
    def __init__(self, slots, rows, columns):
        self.entries = range(slots)
        self.rows = rows
        self.columns = columns

    def copies(self, slot, pieces, table, dst, sems):
        row = pl.multiple_of(table[slot], 16)
        yield pltpu.make_async_copy(
            pieces[0].at[pl.ds(row, self.rows), :],
            dst.at[:, pl.ds(slot * self.columns, self.columns)],
            sems.at[slot],
        )


def cut_rows(values, low, seq):
    tail = values[low:]
    rows = lax.broadcasted_iota(jnp.int32, tail.shape, 0)
    return values[0:low], jnp.where(rows < seq - low, tail, -1e30)


def attn_fwd_kernel(plan, pieces_total, seq, *refs):
    table, x, bias = refs[:3]
    pieces = refs[3 : 3 + pieces_total]
    proj, mixed, lse, w_out, wo, w, mixed_t, probs, sems, out_sem = refs[3 + pieces_total :]
    width = GROUP_HEADS * HEAD_DIM
    keys = -(-seq // 16) * 16
    low = seq // 16 * 16
    scale = HEAD_DIM**-0.5 * LOG2E

    for c in plan.copies(0, pieces, table, w, sems):
        c.start()
    for c in plan.copies(0, pieces, table, w, sems):
        c.wait()
    keep = pltpu.make_async_copy(w, w_out, out_sem)
    keep.start()

    proj[...] = (nn(x[...], w[:, 0 : 3 * width]) + bias[...]).astype(BF16)
    wo[...] = w[:, 3 * width : 4 * width]
    for h in range(GROUP_HEADS):
        q = proj[:, h * HEAD_DIM : (h + 1) * HEAD_DIM]
        k = proj[0:keys, width + h * HEAD_DIM : width + (h + 1) * HEAD_DIM]
        v = proj[0:keys, 2 * width + h * HEAD_DIM : 2 * width + (h + 1) * HEAD_DIM]
        parts = cut_rows(nt(k, q), low, seq)
        top = functools.reduce(jnp.maximum, [jnp.max(t, axis=0, keepdims=True) for t in parts])
        shift = top * scale
        total = jnp.zeros_like(top)
        for t, rows in zip(parts, (slice(0, low), slice(low, keys))):
            p = jnp.exp2(t * scale - shift)
            total += jnp.sum(p, axis=0, keepdims=True)
            probs[rows, :] = p.astype(BF16)
        mixed_t[h * HEAD_DIM : (h + 1) * HEAD_DIM, :] = tn(v, probs[...]) / total
        lse[h : h + 1, :] = shift + jnp.log2(total)
    mixed[...] = mixed_t[...].T.astype(BF16)
    keep.wait()


def attn_fwd(table, x, bias, pieces, plan, seq):
    d = x.shape[1]
    gw = plan.columns
    width = GROUP_HEADS * HEAD_DIM
    keys = -(-seq // 16) * 16
    vmem = pl.BlockSpec(memory_space=pltpu.VMEM)
    anywhere = pl.BlockSpec(memory_space=pl.ANY)
    return pl.pallas_call(
        functools.partial(attn_fwd_kernel, plan, len(pieces), seq),
        in_specs=[pl.BlockSpec(memory_space=pltpu.SMEM), vmem, vmem, *[anywhere for _ in pieces]],
        out_specs=[vmem, vmem, vmem, anywhere, vmem],
        out_shape=[
            jax.ShapeDtypeStruct((PAD, 3 * width), BF16),
            jax.ShapeDtypeStruct((PAD, width), BF16),
            jax.ShapeDtypeStruct((8, PAD), F32),
            jax.ShapeDtypeStruct((d, gw), BF16),
            jax.ShapeDtypeStruct((d, width), BF16),
        ],
        scratch_shapes=[
            pltpu.VMEM((d, gw), BF16),
            pltpu.VMEM((width, PAD), F32),
            pltpu.VMEM((keys, PAD), BF16),
            pltpu.SemaphoreType.DMA((len(plan.entries),)),
            pltpu.SemaphoreType.DMA,
        ],
        compiler_params=params(),
        cost_estimate=cost(2 * PAD * (d * 4 * width + 8 * PAD * 256), d * gw * 4, 0.05),
        name="attn_fwd",
    )(table, x, bias, *pieces)


def attn_bwd_kernel(seq, proj, mixed, lse, ga, wo, grads, sums, gm, dq_t, probs, slopes):
    width = GROUP_HEADS * HEAD_DIM
    keys = -(-seq // 16) * 16
    low = seq // 16 * 16
    factor = HEAD_DIM**-0.5
    scale = factor * LOG2E
    gm[...] = nn(ga[...], wo[...]).astype(BF16)
    for h in range(GROUP_HEADS):
        sl = slice(h * HEAD_DIM, (h + 1) * HEAD_DIM)
        q = proj[:, h * HEAD_DIM : (h + 1) * HEAD_DIM]
        k = proj[0:keys, width + h * HEAD_DIM : width + (h + 1) * HEAD_DIM]
        v = proj[0:keys, 2 * width + h * HEAD_DIM : 2 * width + (h + 1) * HEAD_DIM]
        do = gm[:, sl]
        parts = cut_rows(nt(k, q) * scale - lse[h : h + 1, :], low, seq)
        dp = nt(v, do)
        cuts = (slice(0, low), slice(low, keys))
        p = [jnp.exp2(t) for t in parts]
        delta = sum(
            jnp.sum(t * dp[rows], axis=0, keepdims=True) for t, rows in zip(p, cuts)
        )
        for t, rows in zip(p, cuts):
            probs[rows, :] = t.astype(BF16)
            slopes[rows, :] = (t * (dp[rows] - delta)).astype(BF16)
        dv = nn(probs[...], do)
        dk = nn(slopes[...], q)
        dq_t[sl, :] = tn(k, slopes[...])
        grads[0:keys, width + h * HEAD_DIM : width + (h + 1) * HEAD_DIM] = (dk * factor).astype(
            BF16
        )
        grads[0:keys, 2 * width + h * HEAD_DIM : 2 * width + (h + 1) * HEAD_DIM] = dv.astype(BF16)
    grads[keys:PAD, width : 3 * width] = jnp.zeros((PAD - keys, 2 * width), BF16)
    grads[:, 0:width] = (dq_t[...] * factor).T.astype(BF16)
    sums[...] = jnp.sum(grads[:, 0 : 3 * width].astype(F32), axis=0, keepdims=True)
    grads[:, 3 * width : 4 * width] = mixed[...]


def attn_bwd(proj, mixed, lse, ga, wo, seq):
    d, width = wo.shape
    keys = -(-seq // 16) * 16
    return pl.pallas_call(
        functools.partial(attn_bwd_kernel, seq),
        in_specs=specs(5)[1:],
        out_specs=specs(2)[1:],
        out_shape=[
            jax.ShapeDtypeStruct((PAD, 4 * width), BF16),
            jax.ShapeDtypeStruct((1, 3 * width), F32),
        ],
        scratch_shapes=[
            pltpu.VMEM((PAD, width), BF16),
            pltpu.VMEM((width, PAD), F32),
            pltpu.VMEM((keys, PAD), BF16),
            pltpu.VMEM((keys, PAD), BF16),
        ],
        compiler_params=params(),
        cost_estimate=cost(2 * PAD * (d * width + 20 * PAD * 256), d * width * 2 + PAD * d * 8),
        name="attn_bwd",
    )(proj, mixed, lse, ga, wo)


def tile_of(units):
    return next(t for t in (1024, 768, 512, 256, 128) if units % t == 0)


def first_need(tile, columns, slots):
    return [slot * columns // tile for slot in range(slots)]


def ff_up_kernel(plan, pieces_total, slots, tile, *refs):
    table, x, bias = refs[:3]
    pieces = refs[3 : 3 + pieces_total]
    active, slope, w_out, w, sems, out_sems = refs[3 + pieces_total :]
    n = pl.program_id(0)
    cols = plan.columns

    @pl.when(n == 0)
    def _():
        for slot in range(slots):
            for c in plan.copies(slot, pieces, table, w, sems):
                c.start()

    def out_copy(slot):
        part = pl.ds(slot * cols, cols)
        return pltpu.make_async_copy(w.at[:, part], w_out.at[:, part], out_sems.at[slot])

    for slot, step in enumerate(first_need(tile, cols, slots)):

        @pl.when(n == step)
        def _(slot=slot):
            for c in plan.copies(slot, pieces, table, w, sems):
                c.wait()
            out_copy(slot).start()

    root = math.sqrt(2.0 / math.pi)
    for r in range(0, PAD, PAD // 3):
        rows = slice(r, r + PAD // 3)
        u = nn(x[rows, :], w[:, pl.ds(pl.multiple_of(n * tile, tile), tile)]) + bias[...]
        square = u * u
        t = jnp.tanh(u * (root + (root * 0.044715) * square))
        half = 0.5 + 0.5 * t
        value = u * half
        active[rows, :] = value.astype(BF16)
        slope[rows, :] = (
            half + (value * (1.0 - half)) * (2.0 * root + (6.0 * root * 0.044715) * square)
        ).astype(BF16)

    @pl.when(n == pl.num_programs(0) - 1)
    def _():
        for slot in range(slots):
            out_copy(slot).wait()


def ff_up(table, x, bias, pieces, plan, slots):
    d = x.shape[1]
    units = slots * plan.columns
    tile = tile_of(units)
    return pl.pallas_call(
        functools.partial(ff_up_kernel, plan, len(pieces), slots, tile),
        grid=(units // tile,),
        in_specs=[
            pl.BlockSpec(memory_space=pltpu.SMEM),
            whole((PAD, d)),
            pl.BlockSpec((1, tile), lambda n: (0, n)),
            *[pl.BlockSpec(memory_space=pl.ANY) for _ in pieces],
        ],
        out_specs=[
            pl.BlockSpec((PAD, tile), lambda n: (0, n)),
            pl.BlockSpec((PAD, tile), lambda n: (0, n)),
            pl.BlockSpec(memory_space=pl.ANY),
        ],
        out_shape=[
            jax.ShapeDtypeStruct((PAD, units), BF16),
            jax.ShapeDtypeStruct((PAD, units), BF16),
            jax.ShapeDtypeStruct((d, units), BF16),
        ],
        scratch_shapes=[
            pltpu.VMEM((d, units), BF16),
            pltpu.SemaphoreType.DMA((len(plan.entries),)),
            pltpu.SemaphoreType.DMA((slots,)),
        ],
        compiler_params=params(),
        cost_estimate=cost(2 * PAD * d * units, 4 * d * units + 4 * PAD * units, 0.05),
        name="ff_up",
    )(table, x, bias, *pieces)


def ff_down_kernel(plan, pieces_total, slots, tile, *refs):
    table, gl, active, slope = refs[:4]
    pieces = refs[4 : 4 + pieces_total]
    acc, gu, sums, w, sems = refs[4 + pieces_total :]
    n = pl.program_id(0)
    cols = plan.columns

    @pl.when(n == 0)
    def _():
        for slot in range(slots):
            for c in plan.copies(slot, pieces, table, w, sems):
                c.start()

    for slot, step in enumerate(first_need(tile, cols, slots)):

        @pl.when(n == step)
        def _(slot=slot):
            for c in plan.copies(slot, pieces, table, w, sems):
                c.wait()

    wt = w[:, pl.ds(pl.multiple_of(n * tile, tile), tile)]
    grad = (nn(gl[...], wt) * slope[...].astype(F32)).astype(BF16)
    gu[...] = grad
    sums[...] = jnp.sum(grad.astype(F32), axis=0, keepdims=True)
    part = nt(active[...], wt)

    @pl.when(n == 0)
    def _():
        acc[...] = part

    @pl.when(n > 0)
    def _():
        acc[...] += part


def ff_down(table, gl, active, slope, pieces, plan, slots):
    d = gl.shape[1]
    units = slots * plan.columns
    tile = tile_of(units)
    return pl.pallas_call(
        functools.partial(ff_down_kernel, plan, len(pieces), slots, tile),
        grid=(units // tile,),
        in_specs=[
            pl.BlockSpec(memory_space=pltpu.SMEM),
            whole((PAD, d)),
            pl.BlockSpec((PAD, tile), lambda n: (0, n)),
            pl.BlockSpec((PAD, tile), lambda n: (0, n)),
            *[pl.BlockSpec(memory_space=pl.ANY) for _ in pieces],
        ],
        out_specs=[
            whole((PAD, d)),
            pl.BlockSpec((PAD, tile), lambda n: (0, n)),
            pl.BlockSpec((1, tile), lambda n: (0, n)),
        ],
        out_shape=[
            jax.ShapeDtypeStruct((PAD, d), F32),
            jax.ShapeDtypeStruct((PAD, units), BF16),
            jax.ShapeDtypeStruct((1, units), F32),
        ],
        scratch_shapes=[
            pltpu.VMEM((d, units), BF16),
            pltpu.SemaphoreType.DMA((len(plan.entries),)),
        ],
        compiler_params=params(),
        cost_estimate=cost(4 * PAD * d * units, 2 * d * units + 6 * PAD * units, 0.05),
        name="ff_down",
    )(table, gl, active, slope, *pieces)


def put_turned(table, blocks, value, out):
    t = value.T
    rows = t.shape[0] // blocks
    for b in range(blocks):
        out[pl.ds(pl.multiple_of(table[b], 16), rows), :] = t[b * rows : (b + 1) * rows, :]


def turn_kernel(blocks, table, x, out, sums):
    value = x[...]
    put_turned(table, blocks, value, out)
    sums[...] = jnp.sum(value.astype(F32), axis=0, keepdims=True)


def specs(total):
    return [pl.BlockSpec(memory_space=pltpu.SMEM)] + [pl.BlockSpec(memory_space=pltpu.VMEM)] * total


def turn(table, x):
    d = x.shape[1]
    return pl.pallas_call(
        functools.partial(turn_kernel, table.shape[0]),
        in_specs=specs(1),
        out_specs=specs(2)[1:],
        out_shape=[jax.ShapeDtypeStruct((d, PAD), BF16), jax.ShapeDtypeStruct((1, d), F32)],
        compiler_params=params(),
        cost_estimate=cost(PAD * d * 8, PAD * d * 4, 0.05),
        name="turn",
    )(table, x)


def centered(v):
    c = v - jnp.mean(v, axis=-1, keepdims=True)
    return c, lax.rsqrt(jnp.mean(c * c, axis=-1, keepdims=True) + EPS)


def norm_kernel(blocks, seq, groups, *refs):
    if groups:
        table, base, extra, gain, bias = refs[:5]
        mixed, wo = refs[5 : 5 + groups], refs[5 + groups : 5 + 2 * groups]
        hidden, normed, turned = refs[5 + 2 * groups :]
        v = base[...].astype(F32) + extra[...]
        for m, o in zip(mixed, wo):
            v += nt(m[...], o[...])
        hidden[...] = v
    else:
        table, base, gain, bias, normed, turned = refs
        v = base[...].astype(F32)
    c, r = centered(v)
    value = c * r * gain[...] + bias[...]
    rows = lax.broadcasted_iota(jnp.int32, value.shape, 0)
    low = jnp.where(rows < seq, value, 0.0).astype(BF16)
    normed[...] = low
    put_turned(table, blocks, low, turned)


def norm(table, base, extra, gain, bias, seq, mixed=(), wo=()):
    d = base.shape[1]
    args = [base] + ([extra[None]] if mixed else []) + [gain[None], bias[None], *mixed, *wo]
    outs = [jax.ShapeDtypeStruct((PAD, d), BF16), jax.ShapeDtypeStruct((d, PAD), BF16)]
    if mixed:
        outs = [jax.ShapeDtypeStruct((PAD, d), F32)] + outs
    return pl.pallas_call(
        functools.partial(norm_kernel, table.shape[0], seq, len(mixed)),
        in_specs=specs(len(args)),
        out_specs=specs(len(outs))[1:],
        out_shape=outs,
        compiler_params=params(),
        cost_estimate=cost(PAD * d * 16, PAD * d * 10, 0.05),
        name="norm",
    )(table, *args)


def through_norm(v, e, gain, base):
    c, r = centered(v)
    u = c * r
    scaled = e * gain
    inner = jnp.mean(scaled * u, axis=-1, keepdims=True)
    value = base + r * (scaled - jnp.mean(scaled, axis=-1, keepdims=True) - u * inner)
    return value, jnp.sum(e * u, axis=0, keepdims=True), jnp.sum(e, axis=0, keepdims=True)


def ff_back_kernel(blocks, *refs):
    table, gu, w, v, gain, base, grad, gain_sum, bias_sum, low, turned, low_sum, acc = refs
    n = pl.program_id(0)
    part = nt(gu[...], w[...])

    @pl.when(n == 0)
    def _():
        acc[...] = part

    @pl.when(n > 0)
    def _():
        acc[...] += part

    @pl.when(n == pl.num_programs(0) - 1)
    def _():
        value, gain_sum[...], bias_sum[...] = through_norm(
            v[...], acc[...], gain[...], base[...].astype(F32)
        )
        grad[...] = value
        rounded = value.astype(BF16)
        low[...] = rounded
        put_turned(table, blocks, rounded, turned)
        low_sum[...] = jnp.sum(rounded.astype(F32), axis=0, keepdims=True)


def ff_back(table, gu, w, v, gain, base):
    d, units = w.shape
    tile = tile_of(units)
    row = jax.ShapeDtypeStruct((1, d), F32)
    outs = [
        jax.ShapeDtypeStruct((PAD, d), F32),
        row,
        row,
        jax.ShapeDtypeStruct((PAD, d), BF16),
        jax.ShapeDtypeStruct((d, PAD), BF16),
        row,
    ]
    return pl.pallas_call(
        functools.partial(ff_back_kernel, table.shape[0]),
        grid=(units // tile,),
        in_specs=[
            pl.BlockSpec(memory_space=pltpu.SMEM),
            pl.BlockSpec((PAD, tile), lambda n: (0, n)),
            pl.BlockSpec((d, tile), lambda n: (0, n)),
            *specs(3)[1:],
        ],
        out_specs=specs(len(outs))[1:],
        out_shape=outs,
        scratch_shapes=[pltpu.VMEM((PAD, d), F32)],
        compiler_params=params(),
        cost_estimate=cost(2 * PAD * d * units, 2 * d * units + 2 * PAD * units),
        name="ff_back",
    )(table, gu, w, v, gain[None], base)


def attn_back_kernel(seq, groups, *refs):
    grads, ws = refs[:groups], refs[groups : 2 * groups]
    v, gain, base, grad, gain_sum, bias_sum = refs[2 * groups :]
    cut = 3 * GROUP_HEADS * HEAD_DIM
    e = nt(grads[0][:, 0:cut], ws[0][:, 0:cut])
    for g, w in zip(grads[1:], ws[1:]):
        e += nt(g[:, 0:cut], w[:, 0:cut])
    value, gain_sum[...], bias_sum[...] = through_norm(
        v[...].astype(F32), e, gain[...], base[...]
    )
    grad[...] = value[0:seq]


def attn_back(grads, ws, v, gain, base, seq):
    d = v.shape[1]
    row = jax.ShapeDtypeStruct((1, d), F32)
    args = [*grads, *ws, v, gain[None], base]
    return pl.pallas_call(
        functools.partial(attn_back_kernel, seq, len(grads)),
        in_specs=specs(len(args))[1:],
        out_specs=specs(3)[1:],
        out_shape=[jax.ShapeDtypeStruct((seq, d), F32), row, row],
        compiler_params=params(),
        cost_estimate=cost(6 * PAD * d * d, PAD * d * 18),
        name="attn_back",
    )(*args)


def ff_grad_kernel(total, parts, rows, *refs):
    lhs, rhs, outs = refs[:total], refs[total : 2 * total], refs[2 * total :]
    value = nn(lhs[0][...], rhs[0][...])
    for a, b in zip(lhs[1:], rhs[1:]):
        value += nn(a[...], b[...])
    for number in range(parts):
        outs[number][0] = value[number * rows : (number + 1) * rows].astype(BF16)


def ff_grad(lhs, rhs, slots, parts):
    total = len(lhs)
    height = lhs[0].shape[0]
    rows = height // parts
    cols = rhs[0].shape[1] // slots
    return pl.pallas_call(
        functools.partial(ff_grad_kernel, total, parts, rows),
        grid=(slots,),
        in_specs=[
            *[whole((height, PAD)) for _ in lhs],
            *[pl.BlockSpec((PAD, cols), lambda n: (0, n)) for _ in rhs],
        ],
        out_specs=[pl.BlockSpec((1, rows, cols), lambda n: (n, 0, 0)) for _ in range(parts)],
        out_shape=[jax.ShapeDtypeStruct((slots, rows, cols), BF16) for _ in range(parts)],
        compiler_params=params(),
        cost_estimate=cost(
            2 * total * PAD * height * slots * cols, 2 * slots * cols * (total * PAD + height)
        ),
        name="ff_grad",
    )(*lhs, *rhs)


def attn_grad_kernel(total, parts, has_more, *refs):
    na, ga, g = refs[:total], refs[total : 2 * total], refs[2 * total : 3 * total]
    more, outs = refs[3 * total : -parts], refs[-parts:]
    cut = 3 * GROUP_HEADS * HEAD_DIM
    rows = na[0].shape[0] // parts
    for part in range(parts):
        block = slice(part * rows, (part + 1) * rows)
        for lhs, columns in ((na, slice(0, cut)), (ga, slice(cut, None))):
            value = nn(lhs[0][block, :], g[0][:, columns])
            for i in range(1, total):
                value += nn(lhs[i][block, :], g[i][:, columns])
            if has_more:
                value += more[part][:, columns].astype(F32)
            outs[part][:, columns] = value.astype(BF16)


def attn_grad(na, ga, grads, parts, more=()):
    total = len(na)
    d = na[0].shape[0]
    cols = grads[0].shape[1]
    args = [*na, *ga, *grads, *more]
    return pl.pallas_call(
        functools.partial(attn_grad_kernel, total, parts, len(more) > 0),
        in_specs=specs(len(args))[1:],
        out_specs=specs(parts)[1:],
        out_shape=[jax.ShapeDtypeStruct((d // parts, cols), BF16) for _ in range(parts)],
        compiler_params=params(),
        cost_estimate=cost(2 * total * PAD * d * cols, 2 * cols * (total * PAD + 2 * d)),
        name="attn_grad",
    )(*args)


def hop(x, axis, n, step):
    return lax.ppermute(x, axis, [(i, (i + step) % n) for i in range(n)])


def cat(*arrays):
    return jnp.concatenate(arrays, axis=0)


def after(x, *others):
    others = [o for o in others if o is not None]
    return lax.optimization_barrier((x, others))[0] if others else x


def total_sum(value, sizes):
    for axis, n in sizes.items():
        step = 1
        while step < n:
            value = value + lax.ppermute(value, axis, [(i, i ^ step) for i in range(n)])
            step *= 2
    return value


def attn_entries(nz, rows, h):
    g = rows - h
    plans = []
    for dx in range(2):
        entries = []
        for dy in range(2):
            for dz in range(nz):
                one = (dz, dx * h) if dy == 0 else (nz + dz // 2, dz % 2 * 2 * h + dx * h)
                if dx == 0:
                    two = dz, 2 * h + dy * g
                else:
                    two = nz + nz // 2 + dz // 2, dz % 2 * 2 * g + dy * g
                for (piece, at), size, inside in ((one, h, 0), (two, g, h)):
                    entries.append((piece, at, size, 0, dy * nz + dz, inside, 0))
        plans.append(entries)
    return plans


def ff_entries(nz, rows, cols):
    entries = []
    for dz in range(nz):
        for dy in range(2):
            for dx in range(2):
                piece, at = (dx * nz + dz, 0) if dy == 0 else (2 * nz + dz, dx)
                far = 3 * nz + dz // 2, dz % 2 * 4 + dy * 2 + dx
                for dc, (p, block) in enumerate(((piece, at), far)):
                    entries.append(
                        (p, block * rows, rows, dz, dc * 4 + dy * 2 + dx, 0, dz * cols)
                    )
    return entries


def on_device(
    sizes,
    inputs,
    slot_mask,
    ln1_gain,
    ln1_bias,
    qkv_weight,
    qv_bias,
    out_weight,
    out_bias,
    ln2_gain,
    ln2_bias,
    up_weight,
    up_bias,
    down_weight,
    down_bias,
    out_grad,
):
    seq, d = inputs.shape[1:]
    ny, nx, nc, nz = (sizes[a] for a in ("y", "x", "c", "z"))
    yi, xi, ci, zi = (lax.axis_index(a) for a in ("y", "x", "c", "z"))
    width = GROUP_HEADS * HEAD_DIM
    unit_width = up_weight.shape[1]
    cols = -(-unit_width // 128) * 128
    a_rows, f_rows = qkv_weight.shape[0], up_weight.shape[0]
    linked = ny == nx == nc == 2 and nz % 2 == 0 and a_rows % 16 == 0 and f_rows % 16 == 0

    attn_own = jnp.concatenate(
        [qkv_weight.reshape(a_rows, 3 * width).astype(BF16), out_weight.T.astype(BF16)], axis=1
    )
    spare = ((0, 0), (0, cols - unit_width))
    up_own = jnp.pad(up_weight.astype(BF16), spare)
    down_own = jnp.pad(down_weight.T.astype(BF16), spare)

    def swap(x, axis="c"):
        return hop(x, axis, 2, 1)

    if linked:
        h = -(-a_rows // 32) * 16
        order = [(dc, dx) for dc in range(2) for dx in range(2)]
        attn_plans = [Plan(e, 4 * width) for e in attn_entries(nz, a_rows, h)] * 2
        groups = [(xi ^ dx) * 2 + (ci ^ dc) for dc, dx in order]
        down_plan = Plan(ff_entries(nz, f_rows, cols), cols)
        zones = [(zi - dz) % nz for dz in range(nz)]
        attn_table = jnp.stack(
            [((yi ^ dy) * nz + (zi - dz) % nz) * a_rows for dy in range(2) for dz in range(nz)]
        )
        ff_table = jnp.stack(
            [
                (((yi ^ dy) * 2 + (xi ^ dx)) * 2 + (ci ^ dc)) * f_rows
                for dc in range(2)
                for dy in range(2)
                for dx in range(2)
            ]
        )
        turn_attn = jnp.stack(
            [((yi ^ b // nz) * nz + (zi - b % nz) % nz) * a_rows for b in range(2 * nz)]
        )
        turn_ff = jnp.stack(
            [
                ((ci ^ b % 2) * 4 + (yi ^ b // 4) * 2 + (xi ^ b // 2 % 2)) * f_rows
                for b in range(8)
            ]
        )
    else:
        whole_attn = lax.all_gather(attn_own, ("y", "z"), axis=0, tiled=True)
        whole_attn = lax.all_gather(whole_attn, ("x", "c"), axis=0)
        down_whole = lax.all_gather(down_own, ("z", "y", "x", "c"), axis=0, tiled=True)
        up_whole = lax.all_gather(up_own, ("z", "y", "x", "c"), axis=0, tiled=True)
        attn_pieces = [[whole_attn[g]] for g in range(nx * nc)]
        attn_plans = [Plan([(0, 0, d, 0, 0, 0, 0)], 4 * width)] * (nx * nc)
        attn_table = ff_table = turn_attn = turn_ff = jnp.zeros((1,), jnp.int32)
        groups = list(range(nx * nc))
        zones = list(range(nz))
    up_plan = ZonePlan(nz, d, cols)
    zone_table = jnp.stack([jnp.asarray(k, jnp.int32) * d for k in zones])

    valid = slot_mask[0].astype(F32)
    token_pad = ((0, PAD - seq), (0, 0))
    base = jnp.pad(inputs[0], token_pad)
    grad_low = (valid * jnp.pad(out_grad[0], token_pad).astype(F32)).astype(BF16)
    bias_rows = []
    for g in groups:
        part = lax.dynamic_slice_in_dim(qv_bias, g * width, width, 1)
        bias_rows.append(jnp.concatenate([part[0], jnp.zeros_like(part[0]), part[1]])[None])
    shift = jnp.concatenate(
        [
            jnp.pad(lax.dynamic_slice_in_dim(up_bias, k * unit_width, unit_width), spare[1])
            for k in zones
        ]
    )[None]
    normed_a, na_t = norm(turn_attn, base, None, ln1_gain, ln1_bias, seq)
    gl_t, down_bias_sum = turn(turn_ff, grad_low)

    together = lax.optimization_barrier
    spots = ("z", "y", "x", "c")
    if linked:
        half = d // 2
        down_z, down_x, down_y, down_c = [down_own], [], [], []

        def down_pair(k):
            return swap(cat(down_z[k], down_x[k]), "y")

        def down_core(k):
            return swap(
                cat(*[t for j in (k, k + 1) for t in (down_z[j], down_x[j], down_y[j])])
            )

        px, py, dx0, dz1, normed_a = together(
            (
                swap(attn_own[:h], "x"),
                swap(attn_own[h:], "y"),
                swap(down_own, "x"),
                hop(down_own, "z", nz, 1),
                normed_a,
            )
        )
        down_x.append(dx0)
        down_z.append(dz1)
        s = [cat(attn_own[:h], px, attn_own[h:], py)]
        s1, dy0, dx1, na_far, sc0, gl_t, na_t = together(
            (
                hop(s[0], "z", nz, 1),
                down_pair(0),
                swap(down_z[1], "x"),
                swap(after(na_t, px)),
                swap(s[0]),
                gl_t,
                na_t,
            )
        )
        down_y.append(dy0)
        down_x.append(dx1)
        s.append(s1)
        s_far = [sc0]
        y_parts, x_parts, y_far, x_far = [], [], [], []
        for k in range(2, nz):
            moves = [hop(s[-1], "z", nz, 1), swap(s[-1])]
            if k % 2 == 0:
                moves.append(swap(cat(s[k - 2][: 2 * h], s[k - 1][: 2 * h]), "y"))
                moves.append(swap(cat(s[k - 2][2 * h :], s[k - 1][2 * h :]), "x"))
                if k == 2:
                    moves.append(swap(after(gl_t, s1)[half:]))
            else:
                moves += [swap(y_parts[-1]), swap(x_parts[-1])]
                if k == 3:
                    moves.append(down_pair(1))
            moves = together(tuple(moves))
            s.append(moves[0])
            s_far.append(moves[1])
            if k % 2 == 0:
                y_parts.append(moves[2])
                x_parts.append(moves[3])
                if k == 2:
                    gl_far = moves[4]
            else:
                y_far.append(moves[2])
                x_far.append(moves[3])
                if k == 3:
                    down_y.append(moves[4])
        up_whole = lax.all_gather(after(up_own, s[-1]), spots, axis=0, tiled=True)
        y1, x1, sc3, dz2 = together(
            (
                swap(cat(s[-2][: 2 * h], s[-1][: 2 * h]), "y"),
                swap(cat(s[-2][2 * h :], s[-1][2 * h :]), "x"),
                swap(s[-1]),
                hop(after(down_z[1], s[-1]), "z", nz, 1),
            )
        )
        y_parts.append(y1)
        x_parts.append(x1)
        s_far.append(sc3)
        down_z.append(dz2)
        near = [*s, *y_parts, *x_parts]
        y_far.append(swap(y1))
        x_far.append(swap(x1))
        far = [*s_far, *y_far, *x_far]

        kept = []
        for number in range(4):
            pieces = near if number < 2 else far
            out = attn_fwd(
                attn_table, normed_a, bias_rows[number], pieces, attn_plans[number], seq
            )
            kept.append(out)
            if number == 0:
                dz3 = hop(down_z[2], "z", nz, 1)
                dx2 = swap(down_z[2], "x")
                normed_a, dz3, dx2, far, _ = together((normed_a, dz3, dx2, far, out))
                down_z.append(dz3)
                down_x.append(dx2)
            if number == 1:
                dx3, dy2 = swap(down_z[3], "x"), down_pair(2)
                down_c.append(down_core(0))
                normed_a = after(normed_a, out)
            if number == 2:
                normed_a, dx3, dy2, down_c[0], _ = together(
                    (normed_a, dx3, dy2, down_c[0], out)
                )
                down_x.append(dx3)
                down_y.append(dy2)
                down_y.append(down_pair(3))
    else:
        kept = []
        for number, g in enumerate(groups):
            kept.append(
                attn_fwd(
                    attn_table,
                    normed_a,
                    bias_rows[number],
                    attn_pieces[number],
                    attn_plans[number],
                    seq,
                )
            )

    hidden, normed_b, nb_t = norm(
        turn_ff,
        base,
        out_bias,
        ln2_gain,
        ln2_bias,
        seq,
        [out[1] for out in kept],
        [out[4] for out in kept],
    )
    if linked:
        normed_b, down_y[3] = together((normed_b, down_y[3]))
        down_c.append(down_core(2))
        nb_far = swap(nb_t[half:])
    active, slope, up_full = ff_up(zone_table, normed_b, shift, [up_whole], up_plan, nz)
    if linked:
        active, down_c[1], nb_far = together((active, down_c[1], nb_far))
        down_pieces = [*down_z, *down_x, *down_y, *down_c]
        active_far = swap(active)
    else:
        down_plan, ff_table, down_pieces = up_plan, zone_table, [down_whole]
    mlp, grad_upper, upper_sums = ff_down(
        ff_table, grad_low, active, slope, down_pieces, down_plan, nz
    )
    output = (valid * (hidden + (mlp + down_bias)))[:seq].astype(BF16)[None]

    def plus(*values):
        return sum(v.astype(F32) for v in values).astype(BF16)

    if linked:
        grad_upper, active_far = together((grad_upper, active_far))
        upper_far = swap(grad_upper)
        down_parts = ff_grad([gl_t[:half], gl_far], [active, active_far], nz, 4)
        down_one, down_two = swap(down_parts[3], "x"), swap(down_parts[1], "x")
        grad_upper_first = after(grad_upper, down_parts)
    else:
        spot = ("y", "x", "c")

        def spread(parts):
            part = lax.psum_scatter(parts[0], "z", scatter_dimension=0, tiled=True)[0]
            part = lax.psum_scatter(part, spot, scatter_dimension=0, tiled=True)
            return lax.optimization_barrier(part).astype(F32)

        down_sum = spread(ff_grad([gl_t], [active], nz, 1))
        up_sum = spread(ff_grad([nb_t], [grad_upper], nz, 1))
        grad_upper_first = grad_upper

    grad_hidden, ln2_gain_grad, ln2_bias_grad, grad_attn, ga_t, out_bias_sum = ff_back(
        turn_attn, grad_upper_first, up_full, hidden, ln2_gain, grad_low
    )

    sums = [None] * len(groups)
    if linked:
        grads = {}
        ga_far = swap(ga_t)

        def back(number):
            proj, mixed, lse, _, wo = kept[number]
            grads[number], sums[number] = attn_bwd(proj, mixed, lse, ga_first, wo, seq)

        ga_first, upper_far = together((grad_attn, upper_far))
        back(3)
        far_grads = swap(grads[3])
        ga_first, down_one, _ = together((ga_first, down_one, grads[3]))
        down_one = plus(down_parts[2], down_one)
        down_other = swap(down_one, "y")
        back(1)
        grads[1], far_grads, ga_far, down_one = together((grads[1], far_grads, ga_far, down_one))
        more = attn_grad([na_t, na_far], [ga_t, ga_far], [grads[1], far_grads], 2)
        more_one, more_two = swap(more[1], "x"), swap(more[0], "x")
        upper_first, upper_far = together((grad_upper, upper_far, more))[:2]
        up_parts = ff_grad([nb_t[:half], nb_far], [upper_first, upper_far], nz, 4)
        up_parts, down_two, down_other, ga_first = together(
            (up_parts, down_two, down_other, ga_first)
        )
        up_one, up_two = swap(up_parts[3], "y"), swap(up_parts[2], "y")
        down_value = plus(down_parts[0], down_two, down_other)
        down_line = hop(down_value[nz - 1], "z", nz, -1)
        ga_first = after(ga_first, down_value)
        back(2)
        far_grads = swap(grads[2])
        grads[2], down_line, ga_first = together((grads[2], down_line, ga_first))
        for k in range(nz - 2, 0, -1):
            down_line = hop(plus(down_line, down_value[k]), "z", nz, -1)
        back(0)
        grads[0], far_grads, more_one = together((grads[0], far_grads, more_one))
        input_grad, ln1_gain_grad, ln1_bias_grad = attn_back(
            [grads[k] for k in range(4)],
            [out[3] for out in kept],
            base,
            ln1_gain,
            grad_hidden,
            seq,
        )
        input_grad, up_one, more_two, down_line = together(
            (input_grad, up_one, more_two, down_line)
        )
        up_one = plus(up_parts[1], up_one)
        up_other = swap(up_one, "x")
        na_first = after(na_t, up_one)
        total = attn_grad(
            [na_first, na_far], [ga_t, ga_far], [grads[0], far_grads], 2, (more_two, more_one)
        )
        far_y = swap(total[1], "y")
        up_two, up_other, near_y = together((up_two, up_other, total[0]))
        up_value = plus(up_parts[0], up_two, up_other)
        up_line = hop(up_value[nz - 1], "z", nz, -1)
        far_y, up_line, near_y = together((far_y, up_line, near_y))
        last = plus(near_y, far_y).reshape(nz, a_rows, 4 * width)
        last_far = [hop(last[k], "z", nz, -k) for k in range(1, nz)]
        for k in range(nz - 2, 0, -1):
            up_line = hop(plus(up_line, up_value[k]), "z", nz, -1)
        down_sum = down_line.astype(F32) + down_value[0].astype(F32)
        up_sum = up_line.astype(F32) + up_value[0].astype(F32)
        attn_sum = sum(v.astype(F32) for v in (last[0], *last_far))
    else:
        parts = []
        grads = {}
        for number, (proj, mixed, lse, _, wo) in enumerate(kept):
            grads[number], sums[number] = attn_bwd(proj, mixed, lse, grad_attn, wo, seq)
            parts.append(attn_grad([na_t], [ga_t], [grads[number]], 1)[0])
        part = lax.psum_scatter(jnp.stack(parts), ("x", "c"), scatter_dimension=0, tiled=True)[0]
        part = lax.psum_scatter(part, ("y", "z"), scatter_dimension=0, tiled=True)
        attn_sum = lax.optimization_barrier(part).astype(F32)
        input_grad, ln1_gain_grad, ln1_bias_grad = attn_back(
            [grads[k] for k in range(len(groups))],
            [out[3] for out in kept],
            base,
            ln1_gain,
            grad_hidden,
            seq,
        )

    def in_place(rows, places):
        at = jnp.arange(len(rows))[:, None]
        return sum(jnp.where(at == p, r, 0.0) for r, p in zip(rows, places))

    wide = max(d, 3 * width, cols)

    def fit(x):
        return jnp.pad(x, ((0, 0), (0, wide - x.shape[1])))

    vectors = [
        ln1_gain_grad,
        ln1_bias_grad,
        out_bias_sum,
        ln2_gain_grad,
        ln2_bias_grad,
        down_bias_sum,
        in_place(sums, groups),
        in_place(
            [upper_sums[:, slot * cols : (slot + 1) * cols] for slot in range(nz)], zones
        ),
    ]
    table = cat(*[fit(v) for v in vectors])
    fill = -table.shape[0] % 8
    table = total_sum(jnp.pad(table, ((0, fill), (0, 0))), sizes)
    singles = [table[k, :d] for k in range(6)]
    qv = table[6 : 6 + len(groups)]
    qv_grad = jnp.stack([qv[:, :width].reshape(-1), qv[:, 2 * width : 3 * width].reshape(-1)])
    up_bias_grad = table[6 + len(groups) : 6 + len(groups) + nz, :unit_width].reshape(-1)

    qkv_grad = attn_sum[:, : 3 * width].reshape(a_rows, 3, width)
    out_weight_grad = attn_sum[:, 3 * width :].T
    up_grad = up_sum[:, :unit_width]
    down_grad = down_sum[:, :unit_width].T
    return (
        output,
        input_grad[None],
        singles[0],
        singles[1],
        qkv_grad,
        qv_grad,
        out_weight_grad,
        singles[2],
        singles[3],
        singles[4],
        up_grad,
        up_bias_grad,
        down_grad,
        singles[5],
    )


def solution(mesh):
    heads = mesh.shape["heads"]
    sizes = {"y": mesh.shape["fsdp"], "x": heads // 2, "c": 2, "z": mesh.shape["tensor"]}
    split = jax.sharding.Mesh(mesh.devices.reshape(tuple(sizes.values())), tuple(sizes))
    images = P(("y", "x", "c", "z"), None, None)
    attn_in = P(("y", "z"), None, ("x", "c"))
    attn_out = P(("x", "c"), ("y", "z"))
    up, down = P(("y", "x", "c"), "z"), P("z", ("y", "x", "c"))
    in_specs = (
        images,
        P(("y", "x", "c", "z")),
        P(),
        P(),
        attn_in,
        P(),
        attn_out,
        P(),
        P(),
        P(),
        up,
        P(),
        down,
        P(),
        images,
    )
    out_specs = (
        images,
        images,
        P(),
        P(),
        attn_in,
        P(),
        attn_out,
        P(),
        P(),
        P(),
        up,
        P(),
        down,
        P(),
    )
    return jax.shard_map(
        functools.partial(on_device, sizes),
        mesh=split,
        in_specs=in_specs,
        out_specs=out_specs,
        check_vma=False,
    )
```

```python
import functools
import math

import jax
import jax.numpy as jnp
from jax import lax
from jax.experimental import pallas as pl
from jax.experimental.pallas import tpu as pltpu
from jax.sharding import PartitionSpec as P

HEAD_DIM = 72
GROUP_HEADS = 4
PAD = 768
EPS = 1e-06
VMEM_BYTES = 60 * 1024 * 1024
BF16 = jnp.bfloat16
F32 = jnp.float32
LOG2E = math.log2(math.e)


def nn(a, b):
    return lax.dot_general(a, b, (((1,), (0,)), ((), ())), preferred_element_type=F32)


def nt(a, b):
    return lax.dot_general(a, b, (((1,), (1,)), ((), ())), preferred_element_type=F32)


def tn(a, b):
    return lax.dot_general(a, b, (((0,), (0,)), ((), ())), preferred_element_type=F32)


def params(**kw):
    return pltpu.CompilerParams(vmem_limit_bytes=VMEM_BYTES, **kw)


def cost(flops, bytes_, scale=64):
    return pl.CostEstimate(
        flops=int(flops * scale), bytes_accessed=int(bytes_ * scale), transcendentals=0
    )


def whole(shape):
    zeros = (0,) * len(shape)
    return pl.BlockSpec(shape, lambda *_: zeros)


class Plan:
    def __init__(self, entries, columns):
        self.entries = entries
        self.columns = columns

    def copies(self, slot, pieces, table, dst, sems):
        for number, (piece, src, rows, to, entry, inside, column) in enumerate(self.entries):
            if to != slot:
                continue
            row = pl.multiple_of(table[entry] + inside, 16)
            yield pltpu.make_async_copy(
                pieces[piece].at[pl.ds(src, rows), :],
                dst.at[pl.ds(row, rows), pl.ds(column, self.columns)],
                sems.at[number],
            )


class ZonePlan:
    def __init__(self, slots, rows, columns):
        self.entries = range(slots)
        self.rows = rows
        self.columns = columns

    def copies(self, slot, pieces, table, dst, sems):
        row = pl.multiple_of(table[slot], 16)
        yield pltpu.make_async_copy(
            pieces[0].at[pl.ds(row, self.rows), :],
            dst.at[:, pl.ds(slot * self.columns, self.columns)],
            sems.at[slot],
        )


def cut_rows(values, low, seq):
    tail = values[low:]
    rows = lax.broadcasted_iota(jnp.int32, tail.shape, 0)
    return values[0:low], jnp.where(rows < seq - low, tail, -1e30)


def attn_fwd_kernel(plan, pieces_total, seq, *refs):
    table, x, bias = refs[:3]
    pieces = refs[3 : 3 + pieces_total]
    proj, mixed, lse, w_out, wo, w, mixed_t, probs, sems, out_sem = refs[3 + pieces_total :]
    width = GROUP_HEADS * HEAD_DIM
    keys = -(-seq // 16) * 16
    low = seq // 16 * 16
    scale = HEAD_DIM**-0.5 * LOG2E

    for c in plan.copies(0, pieces, table, w, sems):
        c.start()
    for c in plan.copies(0, pieces, table, w, sems):
        c.wait()
    keep = pltpu.make_async_copy(w, w_out, out_sem)
    keep.start()

    proj[...] = (nn(x[...], w[:, 0 : 3 * width]) + bias[...]).astype(BF16)
    wo[...] = w[:, 3 * width : 4 * width]
    for h in range(GROUP_HEADS):
        q = proj[:, h * HEAD_DIM : (h + 1) * HEAD_DIM]
        k = proj[0:keys, width + h * HEAD_DIM : width + (h + 1) * HEAD_DIM]
        v = proj[0:keys, 2 * width + h * HEAD_DIM : 2 * width + (h + 1) * HEAD_DIM]
        parts = cut_rows(nt(k, q), low, seq)
        top = functools.reduce(jnp.maximum, [jnp.max(t, axis=0, keepdims=True) for t in parts])
        shift = top * scale
        total = jnp.zeros_like(top)
        for t, rows in zip(parts, (slice(0, low), slice(low, keys))):
            p = jnp.exp2(t * scale - shift)
            total += jnp.sum(p, axis=0, keepdims=True)
            probs[rows, :] = p.astype(BF16)
        mixed_t[h * HEAD_DIM : (h + 1) * HEAD_DIM, :] = tn(v, probs[...]) / total
        lse[h : h + 1, :] = shift + jnp.log2(total)
    mixed[...] = mixed_t[...].T.astype(BF16)
    keep.wait()


def attn_fwd(table, x, bias, pieces, plan, seq):
    d = x.shape[1]
    gw = plan.columns
    width = GROUP_HEADS * HEAD_DIM
    keys = -(-seq // 16) * 16
    vmem = pl.BlockSpec(memory_space=pltpu.VMEM)
    anywhere = pl.BlockSpec(memory_space=pl.ANY)
    return pl.pallas_call(
        functools.partial(attn_fwd_kernel, plan, len(pieces), seq),
        in_specs=[pl.BlockSpec(memory_space=pltpu.SMEM), vmem, vmem, *[anywhere for _ in pieces]],
        out_specs=[vmem, vmem, vmem, anywhere, vmem],
        out_shape=[
            jax.ShapeDtypeStruct((PAD, 3 * width), BF16),
            jax.ShapeDtypeStruct((PAD, width), BF16),
            jax.ShapeDtypeStruct((8, PAD), F32),
            jax.ShapeDtypeStruct((d, gw), BF16),
            jax.ShapeDtypeStruct((d, width), BF16),
        ],
        scratch_shapes=[
            pltpu.VMEM((d, gw), BF16),
            pltpu.VMEM((width, PAD), F32),
            pltpu.VMEM((keys, PAD), BF16),
            pltpu.SemaphoreType.DMA((len(plan.entries),)),
            pltpu.SemaphoreType.DMA,
        ],
        compiler_params=params(),
        cost_estimate=cost(2 * PAD * (d * 4 * width + 8 * PAD * 256), d * gw * 4, 0.05),
        name="attn_fwd",
    )(table, x, bias, *pieces)


def attn_bwd_kernel(seq, proj, mixed, lse, ga, wo, grads, sums, gm, dq_t, probs, slopes):
    width = GROUP_HEADS * HEAD_DIM
    keys = -(-seq // 16) * 16
    low = seq // 16 * 16
    factor = HEAD_DIM**-0.5
    scale = factor * LOG2E
    gm[...] = nn(ga[...], wo[...]).astype(BF16)
    for h in range(GROUP_HEADS):
        sl = slice(h * HEAD_DIM, (h + 1) * HEAD_DIM)
        q = proj[:, h * HEAD_DIM : (h + 1) * HEAD_DIM]
        k = proj[0:keys, width + h * HEAD_DIM : width + (h + 1) * HEAD_DIM]
        v = proj[0:keys, 2 * width + h * HEAD_DIM : 2 * width + (h + 1) * HEAD_DIM]
        do = gm[:, sl]
        parts = cut_rows(nt(k, q) * scale - lse[h : h + 1, :], low, seq)
        dp = nt(v, do)
        cuts = (slice(0, low), slice(low, keys))
        p = [jnp.exp2(t) for t in parts]
        delta = sum(
            jnp.sum(t * dp[rows], axis=0, keepdims=True) for t, rows in zip(p, cuts)
        )
        for t, rows in zip(p, cuts):
            probs[rows, :] = t.astype(BF16)
            slopes[rows, :] = (t * (dp[rows] - delta)).astype(BF16)
        dv = nn(probs[...], do)
        dk = nn(slopes[...], q)
        dq_t[sl, :] = tn(k, slopes[...])
        grads[0:keys, width + h * HEAD_DIM : width + (h + 1) * HEAD_DIM] = (dk * factor).astype(
            BF16
        )
        grads[0:keys, 2 * width + h * HEAD_DIM : 2 * width + (h + 1) * HEAD_DIM] = dv.astype(BF16)
    grads[keys:PAD, width : 3 * width] = jnp.zeros((PAD - keys, 2 * width), BF16)
    grads[:, 0:width] = (dq_t[...] * factor).T.astype(BF16)
    sums[...] = jnp.sum(grads[:, 0 : 3 * width].astype(F32), axis=0, keepdims=True)
    grads[:, 3 * width : 4 * width] = mixed[...]


def attn_bwd(proj, mixed, lse, ga, wo, seq):
    d, width = wo.shape
    keys = -(-seq // 16) * 16
    return pl.pallas_call(
        functools.partial(attn_bwd_kernel, seq),
        in_specs=specs(5)[1:],
        out_specs=specs(2)[1:],
        out_shape=[
            jax.ShapeDtypeStruct((PAD, 4 * width), BF16),
            jax.ShapeDtypeStruct((1, 3 * width), F32),
        ],
        scratch_shapes=[
            pltpu.VMEM((PAD, width), BF16),
            pltpu.VMEM((width, PAD), F32),
            pltpu.VMEM((keys, PAD), BF16),
            pltpu.VMEM((keys, PAD), BF16),
        ],
        compiler_params=params(),
        cost_estimate=cost(2 * PAD * (d * width + 20 * PAD * 256), d * width * 2 + PAD * d * 8),
        name="attn_bwd",
    )(proj, mixed, lse, ga, wo)


def tile_of(units, most=1024):
    return next(t for t in (1536, 1024, 768, 512, 256, 128) if units % t == 0 and t <= most)


def first_need(tile, columns, slots):
    return [slot * columns // tile for slot in range(slots)]


def ff_up_kernel(plan, pieces_total, slots, tile, *refs):
    table, x, bias = refs[:3]
    pieces = refs[3 : 3 + pieces_total]
    active, slope, w_out, w, sems, out_sems = refs[3 + pieces_total :]
    n = pl.program_id(0)
    cols = plan.columns

    @pl.when(n == 0)
    def _():
        for slot in range(slots):
            for c in plan.copies(slot, pieces, table, w, sems):
                c.start()

    def out_copy(slot):
        part = pl.ds(slot * cols, cols)
        return pltpu.make_async_copy(w.at[:, part], w_out.at[:, part], out_sems.at[slot])

    for slot, step in enumerate(first_need(tile, cols, slots)):

        @pl.when(n == step)
        def _(slot=slot):
            for c in plan.copies(slot, pieces, table, w, sems):
                c.wait()
            out_copy(slot).start()

    root = math.sqrt(2.0 / math.pi)
    for r in range(0, PAD, PAD // 3):
        rows = slice(r, r + PAD // 3)
        u = nn(x[rows, :], w[:, pl.ds(pl.multiple_of(n * tile, tile), tile)]) + bias[...]
        square = u * u
        t = jnp.tanh(u * (root + (root * 0.044715) * square))
        half = 0.5 + 0.5 * t
        value = u * half
        active[rows, :] = value.astype(BF16)
        slope[rows, :] = (
            half + (value * (1.0 - half)) * (2.0 * root + (6.0 * root * 0.044715) * square)
        ).astype(BF16)

    @pl.when(n == pl.num_programs(0) - 1)
    def _():
        for slot in range(slots):
            out_copy(slot).wait()


def ff_up(table, x, bias, pieces, plan, slots):
    d = x.shape[1]
    units = slots * plan.columns
    tile = tile_of(units)
    return pl.pallas_call(
        functools.partial(ff_up_kernel, plan, len(pieces), slots, tile),
        grid=(units // tile,),
        in_specs=[
            pl.BlockSpec(memory_space=pltpu.SMEM),
            whole((PAD, d)),
            pl.BlockSpec((1, tile), lambda n: (0, n)),
            *[pl.BlockSpec(memory_space=pl.ANY) for _ in pieces],
        ],
        out_specs=[
            pl.BlockSpec((PAD, tile), lambda n: (0, n)),
            pl.BlockSpec((PAD, tile), lambda n: (0, n)),
            pl.BlockSpec(memory_space=pl.ANY),
        ],
        out_shape=[
            jax.ShapeDtypeStruct((PAD, units), BF16),
            jax.ShapeDtypeStruct((PAD, units), BF16),
            jax.ShapeDtypeStruct((d, units), BF16),
        ],
        scratch_shapes=[
            pltpu.VMEM((d, units), BF16),
            pltpu.SemaphoreType.DMA((len(plan.entries),)),
            pltpu.SemaphoreType.DMA((slots,)),
        ],
        compiler_params=params(),
        cost_estimate=cost(2 * PAD * d * units, 4 * d * units + 4 * PAD * units, 0.05),
        name="ff_up",
    )(table, x, bias, *pieces)


def ff_down_kernel(plan, pieces_total, slots, tile, *refs):
    table, gl, active, slope = refs[:4]
    pieces = refs[4 : 4 + pieces_total]
    acc, gu, sums, w, sems = refs[4 + pieces_total :]
    n = pl.program_id(0)
    cols = plan.columns

    @pl.when(n == 0)
    def _():
        for slot in range(slots):
            for c in plan.copies(slot, pieces, table, w, sems):
                c.start()

    for slot, step in enumerate(first_need(tile, cols, slots)):

        @pl.when(n == step)
        def _(slot=slot):
            for c in plan.copies(slot, pieces, table, w, sems):
                c.wait()

    wt = w[:, pl.ds(pl.multiple_of(n * tile, tile), tile)]
    grad = (nn(gl[...], wt) * slope[...].astype(F32)).astype(BF16)
    gu[...] = grad
    sums[...] = jnp.sum(grad.astype(F32), axis=0, keepdims=True)
    part = nt(active[...], wt)

    @pl.when(n == 0)
    def _():
        acc[...] = part

    @pl.when(n > 0)
    def _():
        acc[...] += part


def ff_down(table, gl, active, slope, pieces, plan, slots):
    d = gl.shape[1]
    units = slots * plan.columns
    tile = tile_of(units)
    return pl.pallas_call(
        functools.partial(ff_down_kernel, plan, len(pieces), slots, tile),
        grid=(units // tile,),
        in_specs=[
            pl.BlockSpec(memory_space=pltpu.SMEM),
            whole((PAD, d)),
            pl.BlockSpec((PAD, tile), lambda n: (0, n)),
            pl.BlockSpec((PAD, tile), lambda n: (0, n)),
            *[pl.BlockSpec(memory_space=pl.ANY) for _ in pieces],
        ],
        out_specs=[
            whole((PAD, d)),
            pl.BlockSpec((PAD, tile), lambda n: (0, n)),
            pl.BlockSpec((1, tile), lambda n: (0, n)),
        ],
        out_shape=[
            jax.ShapeDtypeStruct((PAD, d), F32),
            jax.ShapeDtypeStruct((PAD, units), BF16),
            jax.ShapeDtypeStruct((1, units), F32),
        ],
        scratch_shapes=[
            pltpu.VMEM((d, units), BF16),
            pltpu.SemaphoreType.DMA((len(plan.entries),)),
        ],
        compiler_params=params(),
        cost_estimate=cost(4 * PAD * d * units, 2 * d * units + 6 * PAD * units, 0.05),
        name="ff_down",
    )(table, gl, active, slope, *pieces)


def put_turned(table, blocks, value, out):
    t = value.T
    rows = t.shape[0] // blocks
    for b in range(blocks):
        out[pl.ds(pl.multiple_of(table[b], 16), rows), :] = t[b * rows : (b + 1) * rows, :]


def turn_kernel(blocks, table, x, out, sums):
    value = x[...]
    put_turned(table, blocks, value, out)
    sums[...] = jnp.sum(value.astype(F32), axis=0, keepdims=True)


def specs(total):
    return [pl.BlockSpec(memory_space=pltpu.SMEM)] + [pl.BlockSpec(memory_space=pltpu.VMEM)] * total


def turn(table, x):
    d = x.shape[1]
    return pl.pallas_call(
        functools.partial(turn_kernel, table.shape[0]),
        in_specs=specs(1),
        out_specs=specs(2)[1:],
        out_shape=[jax.ShapeDtypeStruct((d, PAD), BF16), jax.ShapeDtypeStruct((1, d), F32)],
        compiler_params=params(),
        cost_estimate=cost(PAD * d * 8, PAD * d * 4, 0.05),
        name="turn",
    )(table, x)


def centered(v):
    c = v - jnp.mean(v, axis=-1, keepdims=True)
    return c, lax.rsqrt(jnp.mean(c * c, axis=-1, keepdims=True) + EPS)


def norm_kernel(blocks, seq, groups, *refs):
    if groups:
        table, base, extra, gain, bias = refs[:5]
        mixed, wo = refs[5 : 5 + groups], refs[5 + groups : 5 + 2 * groups]
        hidden, normed, turned = refs[5 + 2 * groups :]
        v = base[...].astype(F32) + extra[...]
        for m, o in zip(mixed, wo):
            v += nt(m[...], o[...])
        hidden[...] = v
    else:
        table, base, gain, bias, normed, turned = refs
        v = base[...].astype(F32)
    c, r = centered(v)
    value = c * r * gain[...] + bias[...]
    rows = lax.broadcasted_iota(jnp.int32, value.shape, 0)
    low = jnp.where(rows < seq, value, 0.0).astype(BF16)
    normed[...] = low
    put_turned(table, blocks, low, turned)


def norm(table, base, extra, gain, bias, seq, mixed=(), wo=()):
    d = base.shape[1]
    args = [base] + ([extra[None]] if mixed else []) + [gain[None], bias[None], *mixed, *wo]
    outs = [jax.ShapeDtypeStruct((PAD, d), BF16), jax.ShapeDtypeStruct((d, PAD), BF16)]
    if mixed:
        outs = [jax.ShapeDtypeStruct((PAD, d), F32)] + outs
    return pl.pallas_call(
        functools.partial(norm_kernel, table.shape[0], seq, len(mixed)),
        in_specs=specs(len(args)),
        out_specs=specs(len(outs))[1:],
        out_shape=outs,
        compiler_params=params(),
        cost_estimate=cost(PAD * d * 16, PAD * d * 10, 0.05),
        name="norm",
    )(table, *args)


def through_norm(v, e, gain, base):
    c, r = centered(v)
    u = c * r
    scaled = e * gain
    inner = jnp.mean(scaled * u, axis=-1, keepdims=True)
    value = base + r * (scaled - jnp.mean(scaled, axis=-1, keepdims=True) - u * inner)
    return value, jnp.sum(e * u, axis=0, keepdims=True), jnp.sum(e, axis=0, keepdims=True)


def ff_back_kernel(blocks, *refs):
    table, gu, w, v, gain, base, grad, gain_sum, bias_sum, low, turned, low_sum, acc = refs
    n = pl.program_id(0)
    part = nt(gu[...], w[...])

    @pl.when(n == 0)
    def _():
        acc[...] = part

    @pl.when(n > 0)
    def _():
        acc[...] += part

    @pl.when(n == pl.num_programs(0) - 1)
    def _():
        value, gain_sum[...], bias_sum[...] = through_norm(
            v[...], acc[...], gain[...], base[...].astype(F32)
        )
        grad[...] = value
        rounded = value.astype(BF16)
        low[...] = rounded
        put_turned(table, blocks, rounded, turned)
        low_sum[...] = jnp.sum(rounded.astype(F32), axis=0, keepdims=True)


def ff_back(table, gu, w, v, gain, base):
    d, units = w.shape
    tile = tile_of(units, 1536)
    row = jax.ShapeDtypeStruct((1, d), F32)
    outs = [
        jax.ShapeDtypeStruct((PAD, d), F32),
        row,
        row,
        jax.ShapeDtypeStruct((PAD, d), BF16),
        jax.ShapeDtypeStruct((d, PAD), BF16),
        row,
    ]
    return pl.pallas_call(
        functools.partial(ff_back_kernel, table.shape[0]),
        grid=(units // tile,),
        in_specs=[
            pl.BlockSpec(memory_space=pltpu.SMEM),
            pl.BlockSpec((PAD, tile), lambda n: (0, n)),
            pl.BlockSpec((d, tile), lambda n: (0, n)),
            *specs(3)[1:],
        ],
        out_specs=specs(len(outs))[1:],
        out_shape=outs,
        scratch_shapes=[pltpu.VMEM((PAD, d), F32)],
        compiler_params=params(),
        cost_estimate=cost(2 * PAD * d * units, 2 * d * units + 2 * PAD * units),
        name="ff_back",
    )(table, gu, w, v, gain[None], base)


def attn_back_kernel(seq, groups, *refs):
    grads, ws = refs[:groups], refs[groups : 2 * groups]
    v, gain, base, grad, gain_sum, bias_sum = refs[2 * groups :]
    cut = 3 * GROUP_HEADS * HEAD_DIM
    e = nt(grads[0][:, 0:cut], ws[0][:, 0:cut])
    for g, w in zip(grads[1:], ws[1:]):
        e += nt(g[:, 0:cut], w[:, 0:cut])
    value, gain_sum[...], bias_sum[...] = through_norm(
        v[...].astype(F32), e, gain[...], base[...]
    )
    grad[...] = value[0:seq]


def attn_back(grads, ws, v, gain, base, seq):
    d = v.shape[1]
    row = jax.ShapeDtypeStruct((1, d), F32)
    args = [*grads, *ws, v, gain[None], base]
    return pl.pallas_call(
        functools.partial(attn_back_kernel, seq, len(grads)),
        in_specs=specs(len(args))[1:],
        out_specs=specs(3)[1:],
        out_shape=[jax.ShapeDtypeStruct((seq, d), F32), row, row],
        compiler_params=params(),
        cost_estimate=cost(6 * PAD * d * d, PAD * d * 18),
        name="attn_back",
    )(*args)


def ff_grad_kernel(total, parts, sets, size, rows, *refs):
    lhs, rhs, outs = refs[:total], refs[total : 2 * total], refs[2 * total :]
    value = nn(lhs[0][...], rhs[0][...])
    for a, b in zip(lhs[1:], rhs[1:]):
        value += nn(a[...], b[...])
    low = value.astype(BF16)
    n = pl.program_id(0)
    for s in range(sets):

        @pl.when((n >= s * size) & (n < (s + 1) * size))
        def _(s=s):
            for number in range(parts):
                outs[number * sets + s][0] = low[number * rows : (number + 1) * rows]


def ff_grad(lhs, rhs, slots, parts, sets):
    total = len(lhs)
    height = lhs[0].shape[0]
    rows = height // parts
    cols = rhs[0].shape[1] // slots
    size = slots // sets

    def place(s):
        return lambda n: (jnp.clip(n - s * size, 0, size - 1), 0, 0)

    outs = pl.pallas_call(
        functools.partial(ff_grad_kernel, total, parts, sets, size, rows),
        grid=(slots,),
        in_specs=[
            *[whole((height, PAD)) for _ in lhs],
            *[pl.BlockSpec((PAD, cols), lambda n: (0, n)) for _ in rhs],
        ],
        out_specs=[
            pl.BlockSpec((1, rows, cols), place(s)) for _ in range(parts) for s in range(sets)
        ],
        out_shape=[jax.ShapeDtypeStruct((size, rows, cols), BF16)] * (parts * sets),
        compiler_params=params(),
        cost_estimate=cost(
            2 * total * PAD * height * slots * cols, 2 * slots * cols * (total * PAD + height)
        ),
        name="ff_grad",
    )(*lhs, *rhs)
    return [outs[p * sets : (p + 1) * sets] for p in range(parts)]


def attn_grad_kernel(total, parts, has_more, *refs):
    na, ga, g = refs[:total], refs[total : 2 * total], refs[2 * total : 3 * total]
    more, outs = refs[3 * total : -parts], refs[-parts:]
    cut = 3 * GROUP_HEADS * HEAD_DIM
    rows = na[0].shape[0] // parts
    for part in range(parts):
        block = slice(part * rows, (part + 1) * rows)
        for lhs, columns in ((na, slice(0, cut)), (ga, slice(cut, None))):
            value = nn(lhs[0][block, :], g[0][:, columns])
            for i in range(1, total):
                value += nn(lhs[i][block, :], g[i][:, columns])
            if has_more:
                value += more[part][:, columns].astype(F32)
            outs[part][:, columns] = value.astype(BF16)


def attn_grad(na, ga, grads, parts, more=()):
    total = len(na)
    d = na[0].shape[0]
    cols = grads[0].shape[1]
    args = [*na, *ga, *grads, *more]
    return pl.pallas_call(
        functools.partial(attn_grad_kernel, total, parts, len(more) > 0),
        in_specs=specs(len(args))[1:],
        out_specs=specs(parts)[1:],
        out_shape=[jax.ShapeDtypeStruct((d // parts, cols), BF16) for _ in range(parts)],
        compiler_params=params(),
        cost_estimate=cost(2 * total * PAD * d * cols, 2 * cols * (total * PAD + 2 * d)),
        name="attn_grad",
    )(*args)


def hop(x, axis, n, step):
    return lax.ppermute(x, axis, [(i, (i + step) % n) for i in range(n)])


def cat(*arrays):
    return jnp.concatenate(arrays, axis=0)


def after(x, *others):
    others = [o for o in others if o is not None]
    return lax.optimization_barrier((x, others))[0] if others else x


def total_sum(value, sizes):
    for axis in ("c", "x", "y", "z"):
        n = sizes[axis]
        step = 1
        while step < n:
            value = value + lax.ppermute(value, axis, [(i, i ^ step) for i in range(n)])
            step *= 2
    return value


def attn_entries(nz, rows, h):
    g = rows - h
    plans = []
    for dx in range(2):
        entries = []
        for dy in range(2):
            for dz in range(nz):
                one = (dz, dx * h) if dy == 0 else (nz + dz // 2, dz % 2 * 2 * h + dx * h)
                if dx == 0:
                    two = dz, 2 * h + dy * g
                else:
                    two = nz + nz // 2 + dz // 2, dz % 2 * 2 * g + dy * g
                for (piece, at), size, inside in ((one, h, 0), (two, g, h)):
                    entries.append((piece, at, size, 0, dy * nz + dz, inside, 0))
        plans.append(entries)
    return plans


def ff_entries(nz, rows, cols):
    entries = []
    for dz in range(nz):
        for dc in range(2):
            for dy in range(2):
                for dx in range(2):
                    piece = (dc * 2 + dy) * nz + dz
                    entries.append(
                        (piece, dx * rows, rows, dz, dc * 4 + dy * 2 + dx, 0, dz * cols)
                    )
    return entries


def on_device(
    sizes,
    inputs,
    slot_mask,
    ln1_gain,
    ln1_bias,
    qkv_weight,
    qv_bias,
    out_weight,
    out_bias,
    ln2_gain,
    ln2_bias,
    up_weight,
    up_bias,
    down_weight,
    down_bias,
    out_grad,
):
    seq, d = inputs.shape[1:]
    ny, nx, nc, nz = (sizes[a] for a in ("y", "x", "c", "z"))
    yi, xi, ci, zi = (lax.axis_index(a) for a in ("y", "x", "c", "z"))
    width = GROUP_HEADS * HEAD_DIM
    unit_width = up_weight.shape[1]
    cols = -(-unit_width // 128) * 128
    a_rows, f_rows = qkv_weight.shape[0], up_weight.shape[0]
    linked = ny == nx == nc == 2 and nz == 4 and a_rows % 16 == 0 and f_rows % 16 == 0

    attn_own = jnp.concatenate(
        [qkv_weight.reshape(a_rows, 3 * width).astype(BF16), out_weight.T.astype(BF16)], axis=1
    )
    spare = ((0, 0), (0, cols - unit_width))
    up_own = jnp.pad(up_weight.astype(BF16), spare)
    down_own = jnp.pad(down_weight.T.astype(BF16), spare)

    def swap(x, axis="c"):
        return hop(x, axis, 2, 1)

    if linked:
        h = -(-a_rows // 32) * 16
        order = [(dc, dx) for dc in range(2) for dx in range(2)]
        attn_plans = [Plan(e, 4 * width) for e in attn_entries(nz, a_rows, h)] * 2
        groups = [(xi ^ dx) * 2 + (ci ^ dc) for dc, dx in order]
        down_plan = Plan(ff_entries(nz, f_rows, cols), cols)
        zones = [(zi - dz) % nz for dz in range(nz)]
        attn_table = jnp.stack(
            [((yi ^ dy) * nz + (zi - dz) % nz) * a_rows for dy in range(2) for dz in range(nz)]
        )
        ff_table = jnp.stack(
            [
                (((yi ^ dy) * 2 + (xi ^ dx)) * 2 + (ci ^ dc)) * f_rows
                for dc in range(2)
                for dy in range(2)
                for dx in range(2)
            ]
        )
        turn_attn = jnp.stack(
            [((yi ^ b // nz) * nz + (zi - b % nz) % nz) * a_rows for b in range(2 * nz)]
        )
        turn_ff = jnp.stack(
            [
                ((ci ^ b % 2) * 4 + (yi ^ b // 4) * 2 + (xi ^ b // 2 % 2)) * f_rows
                for b in range(8)
            ]
        )
    else:
        whole_attn = lax.all_gather(attn_own, ("y", "z"), axis=0, tiled=True)
        whole_attn = lax.all_gather(whole_attn, ("x", "c"), axis=0)
        down_whole = lax.all_gather(down_own, ("z", "y", "x", "c"), axis=0, tiled=True)
        up_whole = lax.all_gather(up_own, ("z", "y", "x", "c"), axis=0, tiled=True)
        attn_pieces = [[whole_attn[g]] for g in range(nx * nc)]
        attn_plans = [Plan([(0, 0, d, 0, 0, 0, 0)], 4 * width)] * (nx * nc)
        attn_table = ff_table = turn_attn = turn_ff = jnp.zeros((1,), jnp.int32)
        groups = list(range(nx * nc))
        zones = list(range(nz))
    up_plan = ZonePlan(nz, d, cols)
    zone_table = jnp.stack([jnp.asarray(k, jnp.int32) * d for k in zones])

    valid = slot_mask[0].astype(F32)
    token_pad = ((0, PAD - seq), (0, 0))
    base = jnp.pad(inputs[0], token_pad)
    grad_low = (valid * jnp.pad(out_grad[0], token_pad).astype(F32)).astype(BF16)
    bias_rows = []
    for g in groups:
        part = lax.dynamic_slice_in_dim(qv_bias, g * width, width, 1)
        bias_rows.append(jnp.concatenate([part[0], jnp.zeros_like(part[0]), part[1]])[None])
    shift = jnp.concatenate(
        [
            jnp.pad(lax.dynamic_slice_in_dim(up_bias, k * unit_width, unit_width), spare[1])
            for k in zones
        ]
    )[None]
    normed_a, na_t = norm(turn_attn, base, None, ln1_gain, ln1_bias, seq)
    gl_t, down_bias_sum = turn(turn_ff, grad_low)

    together = lax.optimization_barrier
    spots = ("z", "y", "x", "c")
    if linked:
        half = d // 2
        down_z, pairs, down_y, pair_far, y_far_down = [down_own], [], [], [], []

        px, py, dx0, dz1 = together(
            (
                swap(attn_own[:h], "x"),
                swap(attn_own[h:], "y"),
                swap(down_own, "x"),
                hop(down_own, "z", nz, 1),
            )
        )
        pairs.append(cat(down_own, dx0))
        down_z.append(dz1)
        s = [cat(attn_own[:h], px, attn_own[h:], py)]
        s1, dy0, dx1, sc0, gl_t, na_t = together(
            (
                hop(s[0], "z", nz, 1),
                swap(pairs[0], "y"),
                swap(down_z[1], "x"),
                swap(s[0]),
                gl_t,
                na_t,
            )
        )
        down_y.append(dy0)
        pairs.append(cat(down_z[1], dx1))
        s.append(s1)
        s_far = [sc0]
        y_parts, x_parts, y_far, x_far = [], [], [], []
        for k in range(2, nz):
            moves = [hop(s[-1], "z", nz, 1), swap(s[-1])]
            if k % 2 == 0:
                moves.append(swap(cat(s[k - 2][: 2 * h], s[k - 1][: 2 * h]), "y"))
                moves.append(swap(cat(s[k - 2][2 * h :], s[k - 1][2 * h :]), "x"))
                if k == 2:
                    moves.append(swap(na_t))
            else:
                moves += [swap(y_parts[-1]), swap(x_parts[-1])]
                if k == 3:
                    moves.append(swap(pairs[1], "y"))
            moves = together(tuple(moves))
            s.append(moves[0])
            s_far.append(moves[1])
            if k % 2 == 0:
                y_parts.append(moves[2])
                x_parts.append(moves[3])
                if k == 2:
                    na_far = moves[4]
            else:
                y_far.append(moves[2])
                x_far.append(moves[3])
                if k == 3:
                    down_y.append(moves[4])
        up_whole = lax.all_gather(after(up_own, s[-1]), spots, axis=0, tiled=True)
        y1, x1, sc3, dz2, dz3 = together(
            (
                swap(cat(s[-2][: 2 * h], s[-1][: 2 * h]), "y"),
                swap(cat(s[-2][2 * h :], s[-1][2 * h :]), "x"),
                swap(s[-1]),
                hop(after(down_z[1], s[-1]), "z", nz, 1),
                hop(after(down_own, s[-1]), "z", nz, -1),
            )
        )
        y_parts.append(y1)
        x_parts.append(x1)
        s_far.append(sc3)
        down_z += [dz2, dz3]
        near = [*s, *y_parts, *x_parts]
        y_far.append(swap(y1))
        x_far.append(swap(x1))
        far = [*s_far, *y_far, *x_far]

        kept = []
        for number in range(4):
            pieces = near if number < 2 else far
            out = attn_fwd(
                attn_table, normed_a, bias_rows[number], pieces, attn_plans[number], seq
            )
            kept.append(out)
            normed_a = after(normed_a, out)
            if number == 0:
                dx2, p0, y0 = swap(down_z[2], "x"), swap(pairs[0]), swap(after(down_y[0], s[-1]))
                normed_a, dx2, far, p0, y0 = together((normed_a, dx2, far, p0, y0))
                pair_far.append(p0)
                y_far_down.append(y0)
                pairs.append(cat(down_z[2], dx2))
            if number == 1:
                dx3, dy2 = swap(down_z[3], "x"), swap(pairs[2], "y")
                p1, y1 = swap(pairs[1]), swap(down_y[1])
            if number == 2:
                normed_a, dx3, dy2, p1, y1 = together((normed_a, dx3, dy2, p1, y1))
                pair_far.append(p1)
                y_far_down.append(y1)
                pairs.append(cat(down_z[3], dx3))
                down_y.append(dy2)
                dy3 = swap(pairs[3], "y")
                p2, y2, gl_far = swap(pairs[2]), swap(dy2), swap(after(gl_t[half:], out))
    else:
        kept = []
        for number, g in enumerate(groups):
            kept.append(
                attn_fwd(
                    attn_table,
                    normed_a,
                    bias_rows[number],
                    attn_pieces[number],
                    attn_plans[number],
                    seq,
                )
            )

    hidden, normed_b, nb_t = norm(
        turn_ff,
        base,
        out_bias,
        ln2_gain,
        ln2_bias,
        seq,
        [out[1] for out in kept],
        [out[4] for out in kept],
    )
    if linked:
        normed_b, dy3, p2, y2, gl_far = together((normed_b, dy3, p2, y2, gl_far))
        down_y.append(dy3)
        p3, y3 = swap(pairs[3]), swap(dy3)
        nb_far = swap(nb_t[half:])
    active, slope, up_full = ff_up(zone_table, normed_b, shift, [up_whole], up_plan, nz)
    if linked:
        active, p3, y3, nb_far = together((active, p3, y3, nb_far))
        down_pieces = [*pairs, *down_y, *pair_far, p2, p3, *y_far_down, y2, y3]
        active_far = swap(active)
    else:
        down_plan, ff_table, down_pieces = up_plan, zone_table, [down_whole]
    mlp, grad_upper, upper_sums = ff_down(
        ff_table, grad_low, active, slope, down_pieces, down_plan, nz
    )

    def finish(rows):
        return (valid * (hidden + (rows + down_bias)))[:seq].astype(BF16)[None]

    def plus(*values):
        return sum(v.astype(F32) for v in values).astype(BF16)

    if linked:
        grad_upper, active_far = together((grad_upper, active_far))
        upper_far = swap(grad_upper)
        down_parts = [
            p[0] for p in ff_grad([gl_t[:half], gl_far], [active, active_far], nz, 4, 1)
        ]
        down_one, down_two = swap(down_parts[3], "x"), swap(down_parts[1], "x")
        grad_upper_first = after(grad_upper, down_parts)
    else:
        spot = ("y", "x", "c")

        def spread(parts):
            part = lax.psum_scatter(parts[0], "z", scatter_dimension=0, tiled=True)[0]
            part = lax.psum_scatter(part, spot, scatter_dimension=0, tiled=True)
            return lax.optimization_barrier(part).astype(F32)

        down_sum = spread(ff_grad([gl_t], [active], nz, 1, 1)[0])
        up_sum = spread(ff_grad([nb_t], [grad_upper], nz, 1, 1)[0])
        grad_upper_first = grad_upper

    grad_hidden, ln2_gain_grad, ln2_bias_grad, grad_attn, ga_t, out_bias_sum = ff_back(
        turn_attn, grad_upper_first, up_full, hidden, ln2_gain, grad_low
    )

    def in_place(rows, places):
        at = jnp.arange(len(rows))[:, None]
        return sum(jnp.where(at == p, r, 0.0) for r, p in zip(rows, places))

    wide = max(d, 3 * width, cols)

    def fit(x):
        return jnp.pad(x, ((0, 0), (0, wide - x.shape[1])))

    def early_rows():
        vectors = [
            out_bias_sum,
            ln2_gain_grad,
            ln2_bias_grad,
            down_bias_sum,
            in_place(sums, groups),
            in_place(
                [upper_sums[:, slot * cols : (slot + 1) * cols] for slot in range(nz)], zones
            ),
        ]
        rows = cat(*[fit(v) for v in vectors])
        return jnp.pad(rows, ((0, -(rows.shape[0] + 2) % 8), (0, 0)))

    def fold(value, axis, step):
        return lax.ppermute(value, axis, [(i, i ^ step) for i in range(sizes[axis])])

    sums = [None] * len(groups)
    if linked:
        grads = {}
        ga_far = swap(ga_t)

        def back(number):
            proj, mixed, lse, _, wo = kept[number]
            grads[number], sums[number] = attn_bwd(proj, mixed, lse, ga_first, wo, seq)

        ga_first, upper_far = together((grad_attn, upper_far))
        back(3)
        far_grads = swap(grads[3])
        ga_first, down_one, _ = together((ga_first, down_one, grads[3]))
        down_one = plus(down_parts[2], down_one)
        down_other = swap(down_one, "y")
        back(1)
        grads[1], far_grads, ga_far, down_one = together((grads[1], far_grads, ga_far, down_one))
        more = attn_grad([na_t, na_far], [ga_t, ga_far], [grads[1], far_grads], 4)
        more_in = [None, None, swap(more[2], "x"), swap(more[3], "x")]
        upper_first, upper_far = together((grad_upper, upper_far, more))[:2]
        up_parts = ff_grad([nb_t[:half], nb_far], [upper_first, upper_far], nz, 4, 2)
        up_parts, down_two, down_other, ga_first = together(
            (up_parts, down_two, down_other, ga_first)
        )
        up_near = [swap(up_parts[3][1], "y")]
        down_value = plus(down_parts[0], down_two, down_other)
        ga_first = after(ga_first, down_value)
        down_line = hop(down_value[nz - 1], "z", nz, -1)
        back(2)
        grads[2], down_line, more_in[2], more_in[3], up_near[0], ga_first = together(
            (grads[2], down_line, more_in[2], more_in[3], up_near[0], ga_first)
        )
        far_grads = swap(grads[2])
        more_in[1] = swap(after(more[1], more_in[3]), "x")
        up_near.append(swap(after(up_parts[2][1], grads[2]), "y"))
        down_line = plus(down_line, down_value[nz - 2])
        up_one = [None, plus(up_parts[1][1], up_near[0])]
        ga_first = after(ga_first, down_line, up_one[1])
        down_line = hop(down_line, "z", nz, -1)
        back(0)
        early = early_rows()
        grads[0], far_grads, up_near[1], down_line, more_in[1], early = together(
            (grads[0], far_grads, up_near[1], down_line, more_in[1], early)
        )
        more_in[0] = swap(after(more[0], grads[0]), "x")
        up_near.append(swap(after(up_parts[3][0], grads[0]), "y"))
        down_line = plus(down_line, down_value[nz - 3])
        grads_first = after(grads[0], down_line)
        down_line = hop(down_line, "z", nz, -1)
        input_grad, ln1_gain_grad, ln1_bias_grad = attn_back(
            [grads_first] + [grads[k] for k in range(1, 4)],
            [out[3] for out in kept],
            base,
            ln1_gain,
            grad_hidden,
            seq,
        )
        na_first, more_in[0], up_near[2], down_line, input_grad = together(
            (na_t, more_in[0], up_near[2], down_line, input_grad)
        )
        up_near.append(swap(after(up_parts[2][0], na_first), "y"))
        up_other = [None, swap(after(up_one[1], na_first), "x")]
        total = attn_grad(
            [na_first, na_far], [ga_t, ga_far], [grads[0], far_grads], 4, more_in
        )
        table = after(cat(fit(ln1_gain_grad), fit(ln1_bias_grad), early), na_first)
        total, up_near[3], up_other[1], other = together(
            (total, up_near[3], up_other[1], fold(table, "z", 1))
        )
        table = table + other
        far_y = [None, swap(total[3], "y")]
        up_one[0] = plus(up_parts[1][0], up_near[2])
        up_other[0] = swap(up_one[0], "x")
        up_high = plus(up_parts[0][1], up_near[1], up_other[1])
        up_line = hop(up_high[1], "z", nz, -1)
        far_y[1], up_line, up_other[0], near_y, other = together(
            (far_y[1], up_line, up_other[0], total[1], fold(table, "z", 2))
        )
        table = table + other
        far_y[0] = swap(after(total[2], near_y), "y")
        high = plus(near_y, far_y[1]).reshape(2, a_rows, 4 * width)
        last_far = [hop(high[k], "z", nz, -2 - k) for k in range(2)]
        up_line = hop(plus(up_line, up_high[0]), "z", nz, -1)
        output = finish(after(mlp, near_y))
        input_grad = after(input_grad, near_y)
        far_y[0], up_line, other, last_far, near_y = together(
            (far_y[0], up_line, fold(table, "x", 1), last_far, after(total[0], near_y))
        )
        table = table + other
        table = table + fold(table, "y", 1)
        table = table + fold(table, "c", 1)
        low = plus(near_y, far_y[0]).reshape(2, a_rows, 4 * width)
        last_far.append(hop(low[1], "z", nz, -1))
        up_low = plus(up_parts[0][0], up_near[3], up_other[0])
        up_line = hop(plus(up_line, up_low[1]), "z", nz, -1)
        down_sum = down_line.astype(F32) + down_value[0].astype(F32)
        up_sum = up_line.astype(F32) + up_low[0].astype(F32)
        attn_sum = sum(v.astype(F32) for v in (low[0], *last_far))
    else:
        output = finish(mlp)
        parts = []
        grads = {}
        for number, (proj, mixed, lse, _, wo) in enumerate(kept):
            grads[number], sums[number] = attn_bwd(proj, mixed, lse, grad_attn, wo, seq)
            parts.append(attn_grad([na_t], [ga_t], [grads[number]], 1)[0])
        part = lax.psum_scatter(jnp.stack(parts), ("x", "c"), scatter_dimension=0, tiled=True)[0]
        part = lax.psum_scatter(part, ("y", "z"), scatter_dimension=0, tiled=True)
        attn_sum = lax.optimization_barrier(part).astype(F32)
        input_grad, ln1_gain_grad, ln1_bias_grad = attn_back(
            [grads[k] for k in range(len(groups))],
            [out[3] for out in kept],
            base,
            ln1_gain,
            grad_hidden,
            seq,
        )


    if not linked:
        table = total_sum(cat(fit(ln1_gain_grad), fit(ln1_bias_grad), early_rows()), sizes)
    singles = [table[k, :d] for k in range(6)]
    qv = table[6 : 6 + len(groups)]
    qv_grad = jnp.stack([qv[:, :width].reshape(-1), qv[:, 2 * width : 3 * width].reshape(-1)])
    up_bias_grad = table[6 + len(groups) : 6 + len(groups) + nz, :unit_width].reshape(-1)

    qkv_grad = attn_sum[:, : 3 * width].reshape(a_rows, 3, width)
    out_weight_grad = attn_sum[:, 3 * width :].T
    up_grad = up_sum[:, :unit_width]
    down_grad = down_sum[:, :unit_width].T
    return (
        output,
        input_grad[None],
        singles[0],
        singles[1],
        qkv_grad,
        qv_grad,
        out_weight_grad,
        singles[2],
        singles[3],
        singles[4],
        up_grad,
        up_bias_grad,
        down_grad,
        singles[5],
    )


def solution(mesh):
    heads = mesh.shape["heads"]
    sizes = {"y": mesh.shape["fsdp"], "x": heads // 2, "c": 2, "z": mesh.shape["tensor"]}
    split = jax.sharding.Mesh(mesh.devices.reshape(tuple(sizes.values())), tuple(sizes))
    images = P(("y", "x", "c", "z"), None, None)
    attn_in = P(("y", "z"), None, ("x", "c"))
    attn_out = P(("x", "c"), ("y", "z"))
    up, down = P(("y", "x", "c"), "z"), P("z", ("y", "x", "c"))
    in_specs = (
        images,
        P(("y", "x", "c", "z")),
        P(),
        P(),
        attn_in,
        P(),
        attn_out,
        P(),
        P(),
        P(),
        up,
        P(),
        down,
        P(),
        images,
    )
    out_specs = (
        images,
        images,
        P(),
        P(),
        attn_in,
        P(),
        attn_out,
        P(),
        P(),
        P(),
        up,
        P(),
        down,
        P(),
    )
    return jax.shard_map(
        functools.partial(on_device, sizes),
        mesh=split,
        in_specs=in_specs,
        out_specs=out_specs,
        check_vma=False,
    )
```

```python
import functools
import math

import jax
import jax.numpy as jnp
from jax import lax
from jax.experimental import pallas as pl
from jax.experimental.pallas import tpu as pltpu
from jax.sharding import PartitionSpec as P

HEAD_DIM = 72
GROUP_HEADS = 4
PAD = 768
EPS = 1e-06
VMEM_BYTES = 60 * 1024 * 1024
BF16 = jnp.bfloat16
F32 = jnp.float32
LOG2E = math.log2(math.e)


def nn(a, b):
    return lax.dot_general(a, b, (((1,), (0,)), ((), ())), preferred_element_type=F32)


def nt(a, b):
    return lax.dot_general(a, b, (((1,), (1,)), ((), ())), preferred_element_type=F32)


def tn(a, b):
    return lax.dot_general(a, b, (((0,), (0,)), ((), ())), preferred_element_type=F32)


def params(**kw):
    return pltpu.CompilerParams(vmem_limit_bytes=VMEM_BYTES, **kw)


def cost(flops, bytes_, scale=64):
    return pl.CostEstimate(
        flops=int(flops * scale), bytes_accessed=int(bytes_ * scale), transcendentals=0
    )


def whole(shape):
    zeros = (0,) * len(shape)
    return pl.BlockSpec(shape, lambda *_: zeros)


class Plan:
    def __init__(self, entries, columns):
        self.entries = entries
        self.columns = columns

    def copies(self, slot, pieces, table, dst, sems):
        for number, (piece, src, rows, to, entry, inside, column) in enumerate(self.entries):
            if to != slot:
                continue
            row = pl.multiple_of(table[entry] + inside, 16)
            yield pltpu.make_async_copy(
                pieces[piece].at[pl.ds(src, rows), :],
                dst.at[pl.ds(row, rows), pl.ds(column, self.columns)],
                sems.at[number],
            )


class ZonePlan:
    def __init__(self, slots, rows, columns):
        self.entries = range(slots)
        self.rows = rows
        self.columns = columns

    def copies(self, slot, pieces, table, dst, sems):
        row = pl.multiple_of(table[slot], 16)
        yield pltpu.make_async_copy(
            pieces[0].at[pl.ds(row, self.rows), :],
            dst.at[:, pl.ds(slot * self.columns, self.columns)],
            sems.at[slot],
        )


def cut_rows(values, low, seq):
    tail = values[low:]
    rows = lax.broadcasted_iota(jnp.int32, tail.shape, 0)
    return values[0:low], jnp.where(rows < seq - low, tail, -1e30)


def attn_fwd_kernel(plan, pieces_total, seq, *refs):
    table, x, bias = refs[:3]
    pieces = refs[3 : 3 + pieces_total]
    proj, mixed, lse, w_out, wo, w, mixed_t, probs, sems, out_sem = refs[3 + pieces_total :]
    width = GROUP_HEADS * HEAD_DIM
    keys = -(-seq // 16) * 16
    low = seq // 16 * 16
    scale = HEAD_DIM**-0.5 * LOG2E

    for c in plan.copies(0, pieces, table, w, sems):
        c.start()
    for c in plan.copies(0, pieces, table, w, sems):
        c.wait()
    keep = pltpu.make_async_copy(w, w_out, out_sem)
    keep.start()

    proj[...] = (nn(x[...], w[:, 0 : 3 * width]) + bias[...]).astype(BF16)
    wo[...] = w[:, 3 * width : 4 * width]
    for h in range(GROUP_HEADS):
        q = proj[:, h * HEAD_DIM : (h + 1) * HEAD_DIM]
        k = proj[0:keys, width + h * HEAD_DIM : width + (h + 1) * HEAD_DIM]
        v = proj[0:keys, 2 * width + h * HEAD_DIM : 2 * width + (h + 1) * HEAD_DIM]
        parts = cut_rows(nt(k, q), low, seq)
        top = functools.reduce(jnp.maximum, [jnp.max(t, axis=0, keepdims=True) for t in parts])
        shift = top * scale
        total = jnp.zeros_like(top)
        for t, rows in zip(parts, (slice(0, low), slice(low, keys))):
            p = jnp.exp2(t * scale - shift)
            total += jnp.sum(p, axis=0, keepdims=True)
            probs[rows, :] = p.astype(BF16)
        mixed_t[h * HEAD_DIM : (h + 1) * HEAD_DIM, :] = tn(v, probs[...]) / total
        lse[h : h + 1, :] = shift + jnp.log2(total)
    mixed[...] = mixed_t[...].T.astype(BF16)
    keep.wait()


def attn_fwd(table, x, bias, pieces, plan, seq):
    d = x.shape[1]
    gw = plan.columns
    width = GROUP_HEADS * HEAD_DIM
    keys = -(-seq // 16) * 16
    vmem = pl.BlockSpec(memory_space=pltpu.VMEM)
    anywhere = pl.BlockSpec(memory_space=pl.ANY)
    return pl.pallas_call(
        functools.partial(attn_fwd_kernel, plan, len(pieces), seq),
        in_specs=[pl.BlockSpec(memory_space=pltpu.SMEM), vmem, vmem, *[anywhere for _ in pieces]],
        out_specs=[vmem, vmem, vmem, anywhere, vmem],
        out_shape=[
            jax.ShapeDtypeStruct((PAD, 3 * width), BF16),
            jax.ShapeDtypeStruct((PAD, width), BF16),
            jax.ShapeDtypeStruct((8, PAD), F32),
            jax.ShapeDtypeStruct((d, gw), BF16),
            jax.ShapeDtypeStruct((d, width), BF16),
        ],
        scratch_shapes=[
            pltpu.VMEM((d, gw), BF16),
            pltpu.VMEM((width, PAD), F32),
            pltpu.VMEM((keys, PAD), BF16),
            pltpu.SemaphoreType.DMA((len(plan.entries),)),
            pltpu.SemaphoreType.DMA,
        ],
        compiler_params=params(),
        cost_estimate=cost(2 * PAD * (d * 4 * width + 8 * PAD * 256), d * gw * 4, 0.05),
        name="attn_fwd",
    )(table, x, bias, *pieces)


def attn_bwd_kernel(seq, proj, mixed, lse, ga, wo, grads, sums, gm, dq_t, probs, slopes):
    width = GROUP_HEADS * HEAD_DIM
    keys = -(-seq // 16) * 16
    low = seq // 16 * 16
    factor = HEAD_DIM**-0.5
    scale = factor * LOG2E
    gm[...] = nn(ga[...], wo[...]).astype(BF16)
    for h in range(GROUP_HEADS):
        sl = slice(h * HEAD_DIM, (h + 1) * HEAD_DIM)
        q = proj[:, h * HEAD_DIM : (h + 1) * HEAD_DIM]
        k = proj[0:keys, width + h * HEAD_DIM : width + (h + 1) * HEAD_DIM]
        v = proj[0:keys, 2 * width + h * HEAD_DIM : 2 * width + (h + 1) * HEAD_DIM]
        do = gm[:, sl]
        parts = cut_rows(nt(k, q) * scale - lse[h : h + 1, :], low, seq)
        dp = nt(v, do)
        cuts = (slice(0, low), slice(low, keys))
        p = [jnp.exp2(t) for t in parts]
        delta = sum(
            jnp.sum(t * dp[rows], axis=0, keepdims=True) for t, rows in zip(p, cuts)
        )
        for t, rows in zip(p, cuts):
            probs[rows, :] = t.astype(BF16)
            slopes[rows, :] = (t * (dp[rows] - delta)).astype(BF16)
        dv = nn(probs[...], do)
        dk = nn(slopes[...], q)
        dq_t[sl, :] = tn(k, slopes[...])
        grads[0:keys, width + h * HEAD_DIM : width + (h + 1) * HEAD_DIM] = (dk * factor).astype(
            BF16
        )
        grads[0:keys, 2 * width + h * HEAD_DIM : 2 * width + (h + 1) * HEAD_DIM] = dv.astype(BF16)
    grads[keys:PAD, width : 3 * width] = jnp.zeros((PAD - keys, 2 * width), BF16)
    grads[:, 0:width] = (dq_t[...] * factor).T.astype(BF16)
    sums[...] = jnp.sum(grads[:, 0 : 3 * width].astype(F32), axis=0, keepdims=True)
    grads[:, 3 * width : 4 * width] = mixed[...]


def attn_bwd(proj, mixed, lse, ga, wo, seq):
    d, width = wo.shape
    keys = -(-seq // 16) * 16
    return pl.pallas_call(
        functools.partial(attn_bwd_kernel, seq),
        in_specs=specs(5)[1:],
        out_specs=specs(2)[1:],
        out_shape=[
            jax.ShapeDtypeStruct((PAD, 4 * width), BF16),
            jax.ShapeDtypeStruct((1, 3 * width), F32),
        ],
        scratch_shapes=[
            pltpu.VMEM((PAD, width), BF16),
            pltpu.VMEM((width, PAD), F32),
            pltpu.VMEM((keys, PAD), BF16),
            pltpu.VMEM((keys, PAD), BF16),
        ],
        compiler_params=params(),
        cost_estimate=cost(2 * PAD * (d * width + 20 * PAD * 256), d * width * 2 + PAD * d * 8),
        name="attn_bwd",
    )(proj, mixed, lse, ga, wo)


def tile_of(units, most=1024):
    return next(t for t in (1536, 1024, 768, 512, 256, 128) if units % t == 0 and t <= most)


def first_need(tile, columns, slots):
    return [slot * columns // tile for slot in range(slots)]


def ff_up_kernel(plan, pieces_total, slots, tile, *refs):
    table, x, bias = refs[:3]
    pieces = refs[3 : 3 + pieces_total]
    active, slope, w_out, w, sems, out_sems = refs[3 + pieces_total :]
    n = pl.program_id(0)
    cols = plan.columns

    @pl.when(n == 0)
    def _():
        for slot in range(slots):
            for c in plan.copies(slot, pieces, table, w, sems):
                c.start()

    def out_copy(slot):
        part = pl.ds(slot * cols, cols)
        return pltpu.make_async_copy(w.at[:, part], w_out.at[:, part], out_sems.at[slot])

    for slot, step in enumerate(first_need(tile, cols, slots)):

        @pl.when(n == step)
        def _(slot=slot):
            for c in plan.copies(slot, pieces, table, w, sems):
                c.wait()
            out_copy(slot).start()

    root = math.sqrt(2.0 / math.pi)
    for r in range(0, PAD, PAD // 3):
        rows = slice(r, r + PAD // 3)
        u = nn(x[rows, :], w[:, pl.ds(pl.multiple_of(n * tile, tile), tile)]) + bias[...]
        square = u * u
        t = jnp.tanh(u * (root + (root * 0.044715) * square))
        half = 0.5 + 0.5 * t
        value = u * half
        active[rows, :] = value.astype(BF16)
        slope[rows, :] = (
            half + (value * (1.0 - half)) * (2.0 * root + (6.0 * root * 0.044715) * square)
        ).astype(BF16)

    @pl.when(n == pl.num_programs(0) - 1)
    def _():
        for slot in range(slots):
            out_copy(slot).wait()


def ff_up(table, x, bias, pieces, plan, slots):
    d = x.shape[1]
    units = slots * plan.columns
    tile = tile_of(units)
    return pl.pallas_call(
        functools.partial(ff_up_kernel, plan, len(pieces), slots, tile),
        grid=(units // tile,),
        in_specs=[
            pl.BlockSpec(memory_space=pltpu.SMEM),
            whole((PAD, d)),
            pl.BlockSpec((1, tile), lambda n: (0, n)),
            *[pl.BlockSpec(memory_space=pl.ANY) for _ in pieces],
        ],
        out_specs=[
            pl.BlockSpec((PAD, tile), lambda n: (0, n)),
            pl.BlockSpec((PAD, tile), lambda n: (0, n)),
            pl.BlockSpec(memory_space=pl.ANY),
        ],
        out_shape=[
            jax.ShapeDtypeStruct((PAD, units), BF16),
            jax.ShapeDtypeStruct((PAD, units), BF16),
            jax.ShapeDtypeStruct((d, units), BF16),
        ],
        scratch_shapes=[
            pltpu.VMEM((d, units), BF16),
            pltpu.SemaphoreType.DMA((len(plan.entries),)),
            pltpu.SemaphoreType.DMA((slots,)),
        ],
        compiler_params=params(),
        cost_estimate=cost(2 * PAD * d * units, 4 * d * units + 4 * PAD * units, 0.05),
        name="ff_up",
    )(table, x, bias, *pieces)


def ff_down_kernel(plan, pieces_total, slots, tile, *refs):
    table, gl, active, slope = refs[:4]
    pieces = refs[4 : 4 + pieces_total]
    acc, gu, sums, w, sems = refs[4 + pieces_total :]
    n = pl.program_id(0)
    cols = plan.columns

    @pl.when(n == 0)
    def _():
        for slot in range(slots):
            for c in plan.copies(slot, pieces, table, w, sems):
                c.start()

    for slot, step in enumerate(first_need(tile, cols, slots)):

        @pl.when(n == step)
        def _(slot=slot):
            for c in plan.copies(slot, pieces, table, w, sems):
                c.wait()

    wt = w[:, pl.ds(pl.multiple_of(n * tile, tile), tile)]
    grad = (nn(gl[...], wt) * slope[...].astype(F32)).astype(BF16)
    gu[...] = grad
    sums[...] = jnp.sum(grad.astype(F32), axis=0, keepdims=True)
    part = nt(active[...], wt)

    @pl.when(n == 0)
    def _():
        acc[...] = part

    @pl.when(n > 0)
    def _():
        acc[...] += part


def ff_down(table, gl, active, slope, pieces, plan, slots):
    d = gl.shape[1]
    units = slots * plan.columns
    tile = tile_of(units)
    return pl.pallas_call(
        functools.partial(ff_down_kernel, plan, len(pieces), slots, tile),
        grid=(units // tile,),
        in_specs=[
            pl.BlockSpec(memory_space=pltpu.SMEM),
            whole((PAD, d)),
            pl.BlockSpec((PAD, tile), lambda n: (0, n)),
            pl.BlockSpec((PAD, tile), lambda n: (0, n)),
            *[pl.BlockSpec(memory_space=pl.ANY) for _ in pieces],
        ],
        out_specs=[
            whole((PAD, d)),
            pl.BlockSpec((PAD, tile), lambda n: (0, n)),
            pl.BlockSpec((1, tile), lambda n: (0, n)),
        ],
        out_shape=[
            jax.ShapeDtypeStruct((PAD, d), F32),
            jax.ShapeDtypeStruct((PAD, units), BF16),
            jax.ShapeDtypeStruct((1, units), F32),
        ],
        scratch_shapes=[
            pltpu.VMEM((d, units), BF16),
            pltpu.SemaphoreType.DMA((len(plan.entries),)),
        ],
        compiler_params=params(),
        cost_estimate=cost(4 * PAD * d * units, 2 * d * units + 6 * PAD * units, 0.05),
        name="ff_down",
    )(table, gl, active, slope, *pieces)


def put_turned(table, blocks, value, out):
    t = value.T
    rows = t.shape[0] // blocks
    for b in range(blocks):
        out[pl.ds(pl.multiple_of(table[b], 16), rows), :] = t[b * rows : (b + 1) * rows, :]


def turn_kernel(blocks, table, x, out, sums):
    value = x[...]
    put_turned(table, blocks, value, out)
    sums[...] = jnp.sum(value.astype(F32), axis=0, keepdims=True)


def specs(total):
    return [pl.BlockSpec(memory_space=pltpu.SMEM)] + [pl.BlockSpec(memory_space=pltpu.VMEM)] * total


def turn(table, x):
    d = x.shape[1]
    return pl.pallas_call(
        functools.partial(turn_kernel, table.shape[0]),
        in_specs=specs(1),
        out_specs=specs(2)[1:],
        out_shape=[jax.ShapeDtypeStruct((d, PAD), BF16), jax.ShapeDtypeStruct((1, d), F32)],
        compiler_params=params(),
        cost_estimate=cost(PAD * d * 8, PAD * d * 4, 0.05),
        name="turn",
    )(table, x)


def centered(v):
    c = v - jnp.mean(v, axis=-1, keepdims=True)
    return c, lax.rsqrt(jnp.mean(c * c, axis=-1, keepdims=True) + EPS)


def norm_kernel(blocks, seq, groups, *refs):
    if groups:
        table, base, extra, gain, bias = refs[:5]
        mixed, wo = refs[5 : 5 + groups], refs[5 + groups : 5 + 2 * groups]
        hidden, normed, turned = refs[5 + 2 * groups :]
        v = base[...].astype(F32) + extra[...]
        for m, o in zip(mixed, wo):
            v += nt(m[...], o[...])
        hidden[...] = v
    else:
        table, base, gain, bias, normed, turned = refs
        v = base[...].astype(F32)
    c, r = centered(v)
    value = c * r * gain[...] + bias[...]
    rows = lax.broadcasted_iota(jnp.int32, value.shape, 0)
    low = jnp.where(rows < seq, value, 0.0).astype(BF16)
    normed[...] = low
    put_turned(table, blocks, low, turned)


def norm(table, base, extra, gain, bias, seq, mixed=(), wo=()):
    d = base.shape[1]
    args = [base] + ([extra] if mixed else []) + [gain, bias, *mixed, *wo]
    outs = [jax.ShapeDtypeStruct((PAD, d), BF16), jax.ShapeDtypeStruct((d, PAD), BF16)]
    if mixed:
        outs = [jax.ShapeDtypeStruct((PAD, d), F32)] + outs
    return pl.pallas_call(
        functools.partial(norm_kernel, table.shape[0], seq, len(mixed)),
        in_specs=specs(len(args)),
        out_specs=specs(len(outs))[1:],
        out_shape=outs,
        compiler_params=params(),
        cost_estimate=cost(PAD * d * 16, PAD * d * 10, 0.05),
        name="norm",
    )(table, *args)


def through_norm(v, e, gain, base):
    c, r = centered(v)
    u = c * r
    scaled = e * gain
    inner = jnp.mean(scaled * u, axis=-1, keepdims=True)
    value = base + r * (scaled - jnp.mean(scaled, axis=-1, keepdims=True) - u * inner)
    return value, jnp.sum(e * u, axis=0, keepdims=True), jnp.sum(e, axis=0, keepdims=True)


def ff_back_kernel(blocks, *refs):
    table, gu, w, v, gain, base, grad, gain_sum, bias_sum, low, turned, low_sum, acc = refs
    n = pl.program_id(0)
    part = nt(gu[...], w[...])

    @pl.when(n == 0)
    def _():
        acc[...] = part

    @pl.when(n > 0)
    def _():
        acc[...] += part

    @pl.when(n == pl.num_programs(0) - 1)
    def _():
        value, gain_sum[...], bias_sum[...] = through_norm(
            v[...], acc[...], gain[...], base[...].astype(F32)
        )
        grad[...] = value
        rounded = value.astype(BF16)
        low[...] = rounded
        put_turned(table, blocks, rounded, turned)
        low_sum[...] = jnp.sum(rounded.astype(F32), axis=0, keepdims=True)


def ff_back(table, gu, w, v, gain, base):
    d, units = w.shape
    tile = tile_of(units, 1536)
    row = jax.ShapeDtypeStruct((1, d), F32)
    outs = [
        jax.ShapeDtypeStruct((PAD, d), F32),
        row,
        row,
        jax.ShapeDtypeStruct((PAD, d), BF16),
        jax.ShapeDtypeStruct((d, PAD), BF16),
        row,
    ]
    return pl.pallas_call(
        functools.partial(ff_back_kernel, table.shape[0]),
        grid=(units // tile,),
        in_specs=[
            pl.BlockSpec(memory_space=pltpu.SMEM),
            pl.BlockSpec((PAD, tile), lambda n: (0, n)),
            pl.BlockSpec((d, tile), lambda n: (0, n)),
            *specs(3)[1:],
        ],
        out_specs=specs(len(outs))[1:],
        out_shape=outs,
        scratch_shapes=[pltpu.VMEM((PAD, d), F32)],
        compiler_params=params(),
        cost_estimate=cost(2 * PAD * d * units, 2 * d * units + 2 * PAD * units),
        name="ff_back",
    )(table, gu, w, v, gain, base)


def attn_back_kernel(seq, groups, *refs):
    grads, ws = refs[:groups], refs[groups : 2 * groups]
    v, gain, base, grad, gain_sum, bias_sum = refs[2 * groups :]
    cut = 3 * GROUP_HEADS * HEAD_DIM
    e = nt(grads[0][:, 0:cut], ws[0][:, 0:cut])
    for g, w in zip(grads[1:], ws[1:]):
        e += nt(g[:, 0:cut], w[:, 0:cut])
    value, gain_sum[...], bias_sum[...] = through_norm(
        v[...].astype(F32), e, gain[...], base[...]
    )
    grad[...] = value[0:seq]


def attn_back(grads, ws, v, gain, base, seq):
    d = v.shape[1]
    row = jax.ShapeDtypeStruct((1, d), F32)
    args = [*grads, *ws, v, gain, base]
    return pl.pallas_call(
        functools.partial(attn_back_kernel, seq, len(grads)),
        in_specs=specs(len(args))[1:],
        out_specs=specs(3)[1:],
        out_shape=[jax.ShapeDtypeStruct((seq, d), F32), row, row],
        compiler_params=params(),
        cost_estimate=cost(6 * PAD * d * d, PAD * d * 18),
        name="attn_back",
    )(*args)


def ff_grad_kernel(total, parts, sets, size, rows, *refs):
    lhs, rhs, outs = refs[:total], refs[total : 2 * total], refs[2 * total :]
    value = nn(lhs[0][...], rhs[0][...])
    for a, b in zip(lhs[1:], rhs[1:]):
        value += nn(a[...], b[...])
    low = value.astype(BF16)
    n = pl.program_id(0)
    for s in range(sets):

        @pl.when((n >= s * size) & (n < (s + 1) * size))
        def _(s=s):
            for number in range(parts):
                outs[number * sets + s][0] = low[number * rows : (number + 1) * rows]


def ff_grad(lhs, blocks, rhs, slots, parts, sets):
    total = len(lhs)
    height = lhs[0].shape[0] // total
    rows = height // parts
    cols = rhs[0].shape[1] // slots
    size = slots // sets

    def place(s):
        return lambda n: (jnp.clip(n - s * size, 0, size - 1), 0, 0)

    outs = pl.pallas_call(
        functools.partial(ff_grad_kernel, total, parts, sets, size, rows),
        grid=(slots,),
        in_specs=[
            *[pl.BlockSpec((height, PAD), lambda n, b=b: (b, 0)) for b in blocks],
            *[pl.BlockSpec((PAD, cols), lambda n: (0, n)) for _ in rhs],
        ],
        out_specs=[
            pl.BlockSpec((1, rows, cols), place(s)) for _ in range(parts) for s in range(sets)
        ],
        out_shape=[jax.ShapeDtypeStruct((size, rows, cols), BF16)] * (parts * sets),
        compiler_params=params(),
        cost_estimate=cost(
            2 * total * PAD * height * slots * cols, 2 * slots * cols * (total * PAD + height)
        ),
        name="ff_grad",
    )(*lhs, *rhs)
    return [outs[p * sets : (p + 1) * sets] for p in range(parts)]


def attn_grad_kernel(total, parts, has_more, *refs):
    na, ga, g = refs[:total], refs[total : 2 * total], refs[2 * total : 3 * total]
    more, outs = refs[3 * total : -parts], refs[-parts:]
    cut = 3 * GROUP_HEADS * HEAD_DIM
    rows = na[0].shape[0] // parts
    for part in range(parts):
        block = slice(part * rows, (part + 1) * rows)
        for lhs, columns in ((na, slice(0, cut)), (ga, slice(cut, None))):
            value = nn(lhs[0][block, :], g[0][:, columns])
            for i in range(1, total):
                value += nn(lhs[i][block, :], g[i][:, columns])
            if has_more:
                value += more[part][:, columns].astype(F32)
            outs[part][:, columns] = value.astype(BF16)


def attn_grad(na, ga, grads, parts, more=()):
    total = len(na)
    d = na[0].shape[0]
    cols = grads[0].shape[1]
    args = [*na, *ga, *grads, *more]
    return pl.pallas_call(
        functools.partial(attn_grad_kernel, total, parts, len(more) > 0),
        in_specs=specs(len(args))[1:],
        out_specs=specs(parts)[1:],
        out_shape=[jax.ShapeDtypeStruct((d // parts, cols), BF16) for _ in range(parts)],
        compiler_params=params(),
        cost_estimate=cost(2 * total * PAD * d * cols, 2 * cols * (total * PAD + 2 * d)),
        name="attn_grad",
    )(*args)


def hop(x, axis, n, step):
    return lax.ppermute(x, axis, [(i, (i + step) % n) for i in range(n)])


def cat(*arrays):
    return jnp.concatenate(arrays, axis=0)


def after(x, *others):
    others = [o for o in others if o is not None]
    return lax.optimization_barrier((x, others))[0] if others else x


def total_sum(value, sizes):
    for axis in ("c", "x", "y", "z"):
        n = sizes[axis]
        step = 1
        while step < n:
            value = value + lax.ppermute(value, axis, [(i, i ^ step) for i in range(n)])
            step *= 2
    return value


def attn_entries(nz, rows, h):
    g = rows - h
    plans = []
    for dx in range(2):
        entries = []
        for dy in range(2):
            for dz in range(nz):
                one = (dz, dx * h) if dy == 0 else (nz + dz // 2, dz % 2 * 2 * h + dx * h)
                if dx == 0:
                    two = dz, 2 * h + dy * g
                else:
                    two = nz + nz // 2 + dz // 2, dz % 2 * 2 * g + dy * g
                for (piece, at), size, inside in ((one, h, 0), (two, g, h)):
                    entries.append((piece, at, size, 0, dy * nz + dz, inside, 0))
        plans.append(entries)
    return plans


def ff_entries(nz, rows, cols):
    entries = []
    for dz in range(nz):
        for dc in range(2):
            for dy in range(2):
                for dx in range(2):
                    piece = (dc * 2 + dy) * nz + dz
                    entries.append(
                        (piece, dx * rows, rows, dz, dc * 4 + dy * 2 + dx, 0, dz * cols)
                    )
    return entries


def on_device(
    sizes,
    inputs,
    slot_mask,
    ln1_gain,
    ln1_bias,
    qkv_weight,
    qv_bias,
    out_weight,
    out_bias,
    ln2_gain,
    ln2_bias,
    up_weight,
    up_bias,
    down_weight,
    down_bias,
    out_grad,
):
    seq, d = inputs.shape[1:]
    ny, nx, nc, nz = (sizes[a] for a in ("y", "x", "c", "z"))
    yi, xi, ci, zi = (lax.axis_index(a) for a in ("y", "x", "c", "z"))
    width = GROUP_HEADS * HEAD_DIM
    unit_width = up_weight.shape[1]
    cols = -(-unit_width // 128) * 128
    a_rows, f_rows = qkv_weight.shape[0], up_weight.shape[0]
    linked = ny == nx == nc == 2 and nz == 4 and a_rows % 16 == 0 and f_rows % 16 == 0

    attn_own = jnp.concatenate(
        [qkv_weight.reshape(a_rows, 3 * width).astype(BF16), out_weight.T.astype(BF16)], axis=1
    )
    spare = ((0, 0), (0, cols - unit_width))
    up_own = jnp.pad(up_weight.astype(BF16), spare)
    down_own = jnp.pad(down_weight.T.astype(BF16), spare)

    def swap(x, axis="c"):
        return hop(x, axis, 2, 1)

    if linked:
        h = -(-a_rows // 32) * 16
        order = [(dc, dx) for dc in range(2) for dx in range(2)]
        attn_plans = [Plan(e, 4 * width) for e in attn_entries(nz, a_rows, h)] * 2
        groups = [(xi ^ dx) * 2 + (ci ^ dc) for dc, dx in order]
        down_plan = Plan(ff_entries(nz, f_rows, cols), cols)
        zones = [(zi - dz) % nz for dz in range(nz)]
        attn_table = jnp.stack(
            [((yi ^ dy) * nz + (zi - dz) % nz) * a_rows for dy in range(2) for dz in range(nz)]
        )
        ff_table = jnp.stack(
            [
                (((yi ^ dy) * 2 + (xi ^ dx)) * 2 + (ci ^ dc)) * f_rows
                for dc in range(2)
                for dy in range(2)
                for dx in range(2)
            ]
        )
        turn_attn = jnp.stack(
            [((yi ^ b // nz) * nz + (zi - b % nz) % nz) * a_rows for b in range(2 * nz)]
        )
        turn_ff = jnp.stack(
            [
                ((ci ^ b % 2) * 4 + (yi ^ b // 4) * 2 + (xi ^ b // 2 % 2)) * f_rows
                for b in range(8)
            ]
        )
    else:
        whole_attn = lax.all_gather(attn_own, ("y", "z"), axis=0, tiled=True)
        whole_attn = lax.all_gather(whole_attn, ("x", "c"), axis=0)
        down_whole = lax.all_gather(down_own, ("z", "y", "x", "c"), axis=0, tiled=True)
        up_whole = lax.all_gather(up_own, ("z", "y", "x", "c"), axis=0, tiled=True)
        attn_pieces = [[whole_attn[g]] for g in range(nx * nc)]
        attn_plans = [Plan([(0, 0, d, 0, 0, 0, 0)], 4 * width)] * (nx * nc)
        attn_table = ff_table = turn_attn = turn_ff = jnp.zeros((1,), jnp.int32)
        groups = list(range(nx * nc))
        zones = list(range(nz))
    up_plan = ZonePlan(nz, d, cols)
    zone_table = jnp.stack([jnp.asarray(k, jnp.int32) * d for k in zones])

    valid = slot_mask[0].astype(F32)
    token_pad = ((0, PAD - seq), (0, 0))
    base = jnp.pad(inputs[0], token_pad)
    grad_low = (valid * jnp.pad(out_grad[0], token_pad).astype(F32)).astype(BF16)
    bias_rows = []
    for g in groups:
        part = lax.dynamic_slice_in_dim(qv_bias, g * width, width, 1)
        bias_rows.append(jnp.concatenate([part[0], jnp.zeros_like(part[0]), part[1]])[None])
    shift = jnp.concatenate(
        [
            jnp.pad(lax.dynamic_slice_in_dim(up_bias, k * unit_width, unit_width), spare[1])
            for k in zones
        ]
    )[None]
    gain_one, gain_two, shift_two, out_row = (
        v[None] for v in (ln1_gain, ln2_gain, ln2_bias, out_bias)
    )
    normed_a, na_t = norm(turn_attn, base, None, gain_one, ln1_bias[None], seq)
    gl_t, down_bias_sum = turn(turn_ff, grad_low)

    together = lax.optimization_barrier
    spots = ("z", "y", "x", "c")
    if linked:
        down_z, pairs, down_y, pair_far, y_far_down = [down_own], [], [], [], []

        px, py, dx0, dz1 = together(
            (
                swap(attn_own[:h], "x"),
                swap(attn_own[h:], "y"),
                swap(down_own, "x"),
                hop(down_own, "z", nz, 1),
            )
        )
        pairs.append(cat(down_own, dx0))
        down_z.append(dz1)
        s = [cat(attn_own[:h], px, attn_own[h:], py)]
        s1, dy0, dx1, sc0, gl_t, na_t = together(
            (
                hop(s[0], "z", nz, 1),
                swap(pairs[0], "y"),
                swap(down_z[1], "x"),
                swap(s[0]),
                gl_t,
                na_t,
            )
        )
        down_y.append(dy0)
        pairs.append(cat(down_z[1], dx1))
        s.append(s1)
        s_far = [sc0]
        y_parts, x_parts, y_far, x_far = [], [], [], []
        for k in range(2, nz):
            moves = [hop(s[-1], "z", nz, 1), swap(s[-1])]
            if k % 2 == 0:
                moves.append(swap(cat(s[k - 2][: 2 * h], s[k - 1][: 2 * h]), "y"))
                moves.append(swap(cat(s[k - 2][2 * h :], s[k - 1][2 * h :]), "x"))
                if k == 2:
                    moves.append(swap(na_t))
                    moves.append(
                        (bias_rows, shift, ff_table, zone_table, turn_ff, gain_two, shift_two)
                    )
            else:
                moves += [swap(y_parts[-1]), swap(x_parts[-1])]
                if k == 3:
                    moves.append(swap(pairs[1], "y"))
            moves = together(tuple(moves))
            s.append(moves[0])
            s_far.append(moves[1])
            if k % 2 == 0:
                y_parts.append(moves[2])
                x_parts.append(moves[3])
                if k == 2:
                    na_far = moves[4]
                    bias_rows, shift, ff_table, zone_table, turn_ff, gain_two, shift_two = moves[5]
            else:
                y_far.append(moves[2])
                x_far.append(moves[3])
                if k == 3:
                    down_y.append(moves[4])
        up_whole = lax.all_gather(after(up_own, s[-1]), spots, axis=0, tiled=True)
        y1, x1, sc3, dz2, p0 = together(
            (
                swap(cat(s[-2][: 2 * h], s[-1][: 2 * h]), "y"),
                swap(cat(s[-2][2 * h :], s[-1][2 * h :]), "x"),
                swap(s[-1]),
                hop(after(down_z[1], s[-1]), "z", nz, 1),
                swap(after(pairs[0], s[-1])),
            )
        )
        y_parts.append(y1)
        x_parts.append(x1)
        s_far.append(sc3)
        down_z.append(dz2)
        pair_far.append(p0)
        near = [*s, *y_parts, *x_parts]
        y_far.append(swap(y1))
        x_far.append(swap(x1))
        far = [*s_far, *y_far, *x_far]

        kept = []
        for number in range(4):
            pieces = near if number < 2 else far
            out = attn_fwd(
                attn_table, normed_a, bias_rows[number], pieces, attn_plans[number], seq
            )
            kept.append(out)
            normed_a = after(normed_a, out)
            if number == 0:
                dx2, dz3 = swap(down_z[2], "x"), hop(after(down_own, dz2), "z", nz, -1)
                y0 = swap(after(down_y[0], dz2))
                normed_a, dx2, dz3, far, y0 = together((normed_a, dx2, dz3, far, y0))
                down_z.append(dz3)
                pairs.append(cat(down_z[2], dx2))
            if number == 1:
                dx3, dy2 = swap(down_z[3], "x"), swap(pairs[2], "y")
                p1, y1 = swap(after(pairs[1], dx2)), swap(after(down_y[1], dx2))
                normed_a, dx3 = together((normed_a, dx3))
            if number == 2:
                normed_a, dx3, dy2, p1, y1 = together((normed_a, dx3, dy2, p1, y1))
                pair_far.append(p1)
                y_far_down += [y0, y1]
                pairs.append(cat(down_z[3], dx3))
                down_y.append(dy2)
                dy3 = swap(pairs[3], "y")
                p2, y2, gl_far = swap(after(pairs[2], out)), swap(dy2), swap(after(gl_t, out))
        mixed_last, dy3 = together((out[1], dy3))
        kept[3] = [out[0], mixed_last, *out[2:]]
    else:
        kept = []
        for number, g in enumerate(groups):
            kept.append(
                attn_fwd(
                    attn_table,
                    normed_a,
                    bias_rows[number],
                    attn_pieces[number],
                    attn_plans[number],
                    seq,
                )
            )

    hidden, normed_b, nb_t = norm(
        turn_ff,
        base,
        out_row,
        gain_two,
        shift_two,
        seq,
        [out[1] for out in kept],
        [out[4] for out in kept],
    )
    if linked:
        normed_b, p2, y2, gl_far = together((normed_b, p2, y2, gl_far))
        down_y.append(dy3)
        p3, y3 = swap(pairs[3]), swap(dy3)
        nb_far = swap(nb_t)
    active, slope, up_full = ff_up(zone_table, normed_b, shift, [up_whole], up_plan, nz)
    if linked:
        active, p3, y3, nb_far = together((active, p3, y3, nb_far))
        down_pieces = [*pairs, *down_y, *pair_far, p2, p3, *y_far_down, y2, y3]
        active_far = swap(active)
    else:
        down_plan, ff_table, down_pieces = up_plan, zone_table, [down_whole]
    mlp, grad_upper, upper_sums = ff_down(
        ff_table, grad_low, active, slope, down_pieces, down_plan, nz
    )

    def finish(rows):
        return (valid * (hidden + (rows + down_bias)))[:seq].astype(BF16)[None]

    def plus(*values):
        return sum(v.astype(F32) for v in values).astype(BF16)

    if linked:
        grad_upper, active_far = together((grad_upper, active_far))
        upper_far = swap(grad_upper)
        down_parts = [
            p[0] for p in ff_grad([gl_t, gl_far], [0, 1], [active, active_far], nz, 4, 1)
        ]
        down_one, down_two = swap(down_parts[3], "x"), swap(down_parts[1], "x")
        grad_upper_first = after(grad_upper, down_parts)
    else:
        spot = ("y", "x", "c")

        def spread(parts):
            part = lax.psum_scatter(parts[0], "z", scatter_dimension=0, tiled=True)[0]
            part = lax.psum_scatter(part, spot, scatter_dimension=0, tiled=True)
            return lax.optimization_barrier(part).astype(F32)

        down_sum = spread(ff_grad([gl_t], [0], [active], nz, 1, 1)[0])
        up_sum = spread(ff_grad([nb_t], [0], [grad_upper], nz, 1, 1)[0])
        grad_upper_first = grad_upper

    grad_hidden, ln2_gain_grad, ln2_bias_grad, grad_attn, ga_t, out_bias_sum = ff_back(
        turn_attn, grad_upper_first, up_full, hidden, gain_two, grad_low
    )

    def in_place(rows, places):
        at = jnp.arange(len(rows))[:, None]
        return sum(jnp.where(at == p, r, 0.0) for r, p in zip(rows, places))

    wide = max(d, 3 * width, cols)

    def fit(x):
        return jnp.pad(x, ((0, 0), (0, wide - x.shape[1])))

    def early_rows(ready):
        upper = after(upper_sums, ready)
        vectors = [
            out_bias_sum,
            ln2_gain_grad,
            ln2_bias_grad,
            down_bias_sum,
            in_place([after(v, ready) for v in sums], [after(k, ready) for k in groups]),
            in_place([upper[:, slot * cols : (slot + 1) * cols] for slot in range(nz)], zones),
        ]
        rows = cat(*[fit(v) for v in vectors])
        return jnp.pad(rows, ((0, -(rows.shape[0] + 2) % 8), (0, 0)))

    def fold(value, axis, step):
        return lax.ppermute(value, axis, [(i, i ^ step) for i in range(sizes[axis])])

    sums = [None] * len(groups)
    if linked:
        grads = {}
        ga_far = swap(ga_t)

        def back(number):
            proj, mixed, lse, _, wo = kept[number]
            grads[number], sums[number] = attn_bwd(proj, mixed, lse, ga_first, wo, seq)

        ga_first, upper_far = together((grad_attn, upper_far))
        back(3)
        far_grads = swap(grads[3])
        ga_first, down_one, _ = together((ga_first, down_one, grads[3]))
        down_one = plus(down_parts[2], down_one)
        down_other = swap(down_one, "y")
        back(1)
        grads[1], far_grads, ga_far, down_one = together((grads[1], far_grads, ga_far, down_one))
        more = attn_grad([na_t, na_far], [ga_t, ga_far], [grads[1], far_grads], 4)
        more_in = [None, None, swap(more[2], "x"), swap(more[3], "x")]
        upper_first, upper_far = together((grad_upper, upper_far, more))[:2]
        up_parts = ff_grad([nb_t, nb_far], [0, 1], [upper_first, upper_far], nz, 4, 2)
        up_parts, down_two, down_other, ga_first = together(
            (up_parts, down_two, down_other, ga_first)
        )
        up_near = [swap(up_parts[3][1], "y")]
        down_value = plus(down_parts[0], down_two, down_other)
        ga_first = after(ga_first, down_value)
        down_line = hop(down_value[nz - 1], "z", nz, -1)
        back(2)
        grads[2], down_line, more_in[2], more_in[3], up_near[0], ga_first = together(
            (grads[2], down_line, more_in[2], more_in[3], up_near[0], ga_first)
        )
        far_grads = swap(grads[2])
        more_in[1] = swap(after(more[1], more_in[3]), "x")
        up_near.append(swap(after(up_parts[2][1], grads[2]), "y"))
        down_line = plus(down_line, down_value[nz - 2])
        up_one = [None, plus(up_parts[1][1], up_near[0])]
        ga_first = after(ga_first, down_line, up_one[1])
        down_line = hop(down_line, "z", nz, -1)
        back(0)
        early = early_rows(None)
        grads[0], far_grads, up_near[1], down_line, more_in[1], early = together(
            (grads[0], far_grads, up_near[1], down_line, more_in[1], early)
        )
        more_in[0] = swap(after(more[0], grads[0]), "x")
        up_near.append(swap(after(up_parts[3][0], grads[0]), "y"))
        down_line = plus(down_line, down_value[nz - 3])
        grads_first = after(grads[0], down_line)
        down_line = hop(down_line, "z", nz, -1)
        input_grad, ln1_gain_grad, ln1_bias_grad = attn_back(
            [grads_first] + [grads[k] for k in range(1, 4)],
            [out[3] for out in kept],
            base,
            gain_one,
            grad_hidden,
            seq,
        )
        na_first, more_in[0], up_near[2], down_line, input_grad = together(
            (na_t, more_in[0], up_near[2], down_line, input_grad)
        )
        up_near.append(swap(after(up_parts[2][0], na_first), "y"))
        up_other = [None, swap(after(up_one[1], na_first), "x")]
        total = attn_grad(
            [na_first, na_far], [ga_t, ga_far], [grads[0], far_grads], 4, more_in
        )
        table = after(cat(fit(ln1_gain_grad), fit(ln1_bias_grad), early), na_first)
        total, up_near[3], up_other[1], other = together(
            (total, up_near[3], up_other[1], fold(table, "z", 1))
        )
        table = table + other
        far_y = [None, swap(total[3], "y")]
        up_one[0] = plus(up_parts[1][0], up_near[2])
        up_other[0] = swap(up_one[0], "x")
        up_high = plus(up_parts[0][1], up_near[1], up_other[1])
        up_line = hop(up_high[1], "z", nz, -1)
        far_y[1], up_line, up_other[0], near_y, other = together(
            (far_y[1], up_line, up_other[0], total[1], fold(table, "z", 2))
        )
        table = table + other
        far_y[0] = swap(after(total[2], near_y), "y")
        high = plus(near_y, far_y[1]).reshape(2, a_rows, 4 * width)
        last_far = [hop(high[k], "z", nz, -2 - k) for k in range(2)]
        up_line = hop(plus(up_line, up_high[0]), "z", nz, -1)
        output = finish(after(mlp, near_y))
        input_grad = after(input_grad, near_y)
        far_y[0], up_line, other, last_far, near_y = together(
            (far_y[0], up_line, fold(table, "x", 1), last_far, after(total[0], near_y))
        )
        table = table + other
        table = table + fold(table, "y", 1)
        table = table + fold(table, "c", 1)
        low = plus(near_y, far_y[0]).reshape(2, a_rows, 4 * width)
        last_far.append(hop(low[1], "z", nz, -1))
        up_low = plus(up_parts[0][0], up_near[3], up_other[0])
        up_line = hop(plus(up_line, up_low[1]), "z", nz, -1)
        down_sum = down_line.astype(F32) + down_value[0].astype(F32)
        up_sum = up_line.astype(F32) + up_low[0].astype(F32)
        attn_sum = sum(v.astype(F32) for v in (low[0], *last_far))
    else:
        output = finish(mlp)
        parts = []
        grads = {}
        for number, (proj, mixed, lse, _, wo) in enumerate(kept):
            grads[number], sums[number] = attn_bwd(proj, mixed, lse, grad_attn, wo, seq)
            parts.append(attn_grad([na_t], [ga_t], [grads[number]], 1)[0])
        part = lax.psum_scatter(jnp.stack(parts), ("x", "c"), scatter_dimension=0, tiled=True)[0]
        part = lax.psum_scatter(part, ("y", "z"), scatter_dimension=0, tiled=True)
        attn_sum = lax.optimization_barrier(part).astype(F32)
        input_grad, ln1_gain_grad, ln1_bias_grad = attn_back(
            [grads[k] for k in range(len(groups))],
            [out[3] for out in kept],
            base,
            gain_one,
            grad_hidden,
            seq,
        )


    if not linked:
        table = total_sum(cat(fit(ln1_gain_grad), fit(ln1_bias_grad), early_rows(None)), sizes)
    singles = [table[k, :d] for k in range(6)]
    qv = table[6 : 6 + len(groups)]
    qv_grad = jnp.stack([qv[:, :width].reshape(-1), qv[:, 2 * width : 3 * width].reshape(-1)])
    up_bias_grad = table[6 + len(groups) : 6 + len(groups) + nz, :unit_width].reshape(-1)

    qkv_grad = attn_sum[:, : 3 * width].reshape(a_rows, 3, width)
    out_weight_grad = attn_sum[:, 3 * width :].T
    up_grad = up_sum[:, :unit_width]
    down_grad = down_sum[:, :unit_width].T
    return (
        output,
        input_grad[None],
        singles[0],
        singles[1],
        qkv_grad,
        qv_grad,
        out_weight_grad,
        singles[2],
        singles[3],
        singles[4],
        up_grad,
        up_bias_grad,
        down_grad,
        singles[5],
    )


def solution(mesh):
    heads = mesh.shape["heads"]
    sizes = {"y": mesh.shape["fsdp"], "x": heads // 2, "c": 2, "z": mesh.shape["tensor"]}
    split = jax.sharding.Mesh(mesh.devices.reshape(tuple(sizes.values())), tuple(sizes))
    images = P(("y", "x", "c", "z"), None, None)
    attn_in = P(("y", "z"), None, ("x", "c"))
    attn_out = P(("x", "c"), ("y", "z"))
    up, down = P(("y", "x", "c"), "z"), P("z", ("y", "x", "c"))
    in_specs = (
        images,
        P(("y", "x", "c", "z")),
        P(),
        P(),
        attn_in,
        P(),
        attn_out,
        P(),
        P(),
        P(),
        up,
        P(),
        down,
        P(),
        images,
    )
    out_specs = (
        images,
        images,
        P(),
        P(),
        attn_in,
        P(),
        attn_out,
        P(),
        P(),
        P(),
        up,
        P(),
        down,
        P(),
    )
    return jax.shard_map(
        functools.partial(on_device, sizes),
        mesh=split,
        in_specs=in_specs,
        out_specs=out_specs,
        check_vma=False,
    )
```

```python
import functools
import math

import jax
import jax.numpy as jnp
from jax import lax
from jax.experimental import pallas as pl
from jax.experimental.pallas import tpu as pltpu
from jax.sharding import PartitionSpec as P

HEAD_DIM = 72
GROUP_HEADS = 4
PAD = 768
EPS = 1e-06
VMEM_BYTES = 60 * 1024 * 1024
BF16 = jnp.bfloat16
F32 = jnp.float32
LOG2E = math.log2(math.e)


def nn(a, b):
    return lax.dot_general(a, b, (((1,), (0,)), ((), ())), preferred_element_type=F32)


def nt(a, b):
    return lax.dot_general(a, b, (((1,), (1,)), ((), ())), preferred_element_type=F32)


def tn(a, b):
    return lax.dot_general(a, b, (((0,), (0,)), ((), ())), preferred_element_type=F32)


def params(**kw):
    return pltpu.CompilerParams(vmem_limit_bytes=VMEM_BYTES, **kw)


def cost(flops, bytes_, scale=64):
    return pl.CostEstimate(
        flops=int(flops * scale), bytes_accessed=int(bytes_ * scale), transcendentals=0
    )


def whole(shape):
    zeros = (0,) * len(shape)
    return pl.BlockSpec(shape, lambda *_: zeros)


class Plan:
    def __init__(self, entries, columns):
        self.entries = entries
        self.columns = columns

    def copies(self, slot, pieces, table, dst, sems):
        for number, (piece, src, rows, to, entry, inside, column) in enumerate(self.entries):
            if to != slot:
                continue
            row = pl.multiple_of(table[entry] + inside, 16)
            yield pltpu.make_async_copy(
                pieces[piece].at[pl.ds(src, rows), :],
                dst.at[pl.ds(row, rows), pl.ds(column, self.columns)],
                sems.at[number],
            )


class ZonePlan:
    def __init__(self, slots, rows, columns):
        self.entries = range(slots)
        self.rows = rows
        self.columns = columns

    def copies(self, slot, pieces, table, dst, sems):
        row = pl.multiple_of(table[slot], 16)
        yield pltpu.make_async_copy(
            pieces[0].at[pl.ds(row, self.rows), :],
            dst.at[:, pl.ds(slot * self.columns, self.columns)],
            sems.at[slot],
        )


def cut_rows(values, low, seq):
    tail = values[low:]
    rows = lax.broadcasted_iota(jnp.int32, tail.shape, 0)
    return values[0:low], jnp.where(rows < seq - low, tail, -1e30)


def attn_fwd_kernel(plan, pieces_total, seq, *refs):
    table, x, bias = refs[:3]
    pieces = refs[3 : 3 + pieces_total]
    proj, mixed, lse, w_out, wo, w, mixed_t, probs, sems, out_sem = refs[3 + pieces_total :]
    width = GROUP_HEADS * HEAD_DIM
    keys = -(-seq // 16) * 16
    low = seq // 16 * 16
    scale = HEAD_DIM**-0.5 * LOG2E

    for c in plan.copies(0, pieces, table, w, sems):
        c.start()
    for c in plan.copies(0, pieces, table, w, sems):
        c.wait()
    keep = pltpu.make_async_copy(w, w_out, out_sem)
    keep.start()

    proj[...] = (nn(x[...], w[:, 0 : 3 * width]) + bias[...]).astype(BF16)
    wo[...] = w[:, 3 * width : 4 * width]
    for h in range(GROUP_HEADS):
        q = proj[:, h * HEAD_DIM : (h + 1) * HEAD_DIM]
        k = proj[0:keys, width + h * HEAD_DIM : width + (h + 1) * HEAD_DIM]
        v = proj[0:keys, 2 * width + h * HEAD_DIM : 2 * width + (h + 1) * HEAD_DIM]
        parts = cut_rows(nt(k, q), low, seq)
        top = functools.reduce(jnp.maximum, [jnp.max(t, axis=0, keepdims=True) for t in parts])
        shift = top * scale
        total = jnp.zeros_like(top)
        for t, rows in zip(parts, (slice(0, low), slice(low, keys))):
            p = jnp.exp2(t * scale - shift)
            total += jnp.sum(p, axis=0, keepdims=True)
            probs[rows, :] = p.astype(BF16)
        mixed_t[h * HEAD_DIM : (h + 1) * HEAD_DIM, :] = tn(v, probs[...]) / total
        lse[h : h + 1, :] = shift + jnp.log2(total)
    mixed[...] = mixed_t[...].T.astype(BF16)
    keep.wait()


def attn_fwd(table, x, bias, pieces, plan, seq):
    d = x.shape[1]
    gw = plan.columns
    width = GROUP_HEADS * HEAD_DIM
    keys = -(-seq // 16) * 16
    vmem = pl.BlockSpec(memory_space=pltpu.VMEM)
    anywhere = pl.BlockSpec(memory_space=pl.ANY)
    return pl.pallas_call(
        functools.partial(attn_fwd_kernel, plan, len(pieces), seq),
        in_specs=[pl.BlockSpec(memory_space=pltpu.SMEM), vmem, vmem, *[anywhere for _ in pieces]],
        out_specs=[vmem, vmem, vmem, anywhere, vmem],
        out_shape=[
            jax.ShapeDtypeStruct((PAD, 3 * width), BF16),
            jax.ShapeDtypeStruct((PAD, width), BF16),
            jax.ShapeDtypeStruct((8, PAD), F32),
            jax.ShapeDtypeStruct((d, gw), BF16),
            jax.ShapeDtypeStruct((d, width), BF16),
        ],
        scratch_shapes=[
            pltpu.VMEM((d, gw), BF16),
            pltpu.VMEM((width, PAD), F32),
            pltpu.VMEM((keys, PAD), BF16),
            pltpu.SemaphoreType.DMA((len(plan.entries),)),
            pltpu.SemaphoreType.DMA,
        ],
        compiler_params=params(),
        cost_estimate=cost(2 * PAD * (d * 4 * width + 8 * PAD * 256), d * gw * 4, 0.05),
        name="attn_fwd",
    )(table, x, bias, *pieces)


def attn_bwd_kernel(seq, proj, mixed, lse, ga, wo, grads, sums, gm, dq_t, probs, slopes):
    width = GROUP_HEADS * HEAD_DIM
    keys = -(-seq // 16) * 16
    low = seq // 16 * 16
    factor = HEAD_DIM**-0.5
    scale = factor * LOG2E
    gm[...] = nn(ga[...], wo[...]).astype(BF16)
    for h in range(GROUP_HEADS):
        sl = slice(h * HEAD_DIM, (h + 1) * HEAD_DIM)
        q = proj[:, h * HEAD_DIM : (h + 1) * HEAD_DIM]
        k = proj[0:keys, width + h * HEAD_DIM : width + (h + 1) * HEAD_DIM]
        v = proj[0:keys, 2 * width + h * HEAD_DIM : 2 * width + (h + 1) * HEAD_DIM]
        do = gm[:, sl]
        parts = cut_rows(nt(k, q) * scale - lse[h : h + 1, :], low, seq)
        dp = nt(v, do)
        cuts = (slice(0, low), slice(low, keys))
        p = [jnp.exp2(t) for t in parts]
        delta = sum(
            jnp.sum(t * dp[rows], axis=0, keepdims=True) for t, rows in zip(p, cuts)
        )
        for t, rows in zip(p, cuts):
            probs[rows, :] = t.astype(BF16)
            slopes[rows, :] = (t * (dp[rows] - delta)).astype(BF16)
        dv = nn(probs[...], do)
        dk = nn(slopes[...], q)
        dq_t[sl, :] = tn(k, slopes[...])
        grads[0:keys, width + h * HEAD_DIM : width + (h + 1) * HEAD_DIM] = (dk * factor).astype(
            BF16
        )
        grads[0:keys, 2 * width + h * HEAD_DIM : 2 * width + (h + 1) * HEAD_DIM] = dv.astype(BF16)
    grads[keys:PAD, width : 3 * width] = jnp.zeros((PAD - keys, 2 * width), BF16)
    grads[:, 0:width] = (dq_t[...] * factor).T.astype(BF16)
    sums[...] = jnp.sum(grads[:, 0 : 3 * width].astype(F32), axis=0, keepdims=True)
    grads[:, 3 * width : 4 * width] = mixed[...]


def attn_bwd(proj, mixed, lse, ga, wo, seq):
    d, width = wo.shape
    keys = -(-seq // 16) * 16
    return pl.pallas_call(
        functools.partial(attn_bwd_kernel, seq),
        in_specs=specs(5)[1:],
        out_specs=specs(2)[1:],
        out_shape=[
            jax.ShapeDtypeStruct((PAD, 4 * width), BF16),
            jax.ShapeDtypeStruct((1, 3 * width), F32),
        ],
        scratch_shapes=[
            pltpu.VMEM((PAD, width), BF16),
            pltpu.VMEM((width, PAD), F32),
            pltpu.VMEM((keys, PAD), BF16),
            pltpu.VMEM((keys, PAD), BF16),
        ],
        compiler_params=params(),
        cost_estimate=cost(2 * PAD * (d * width + 20 * PAD * 256), d * width * 2 + PAD * d * 8),
        name="attn_bwd",
    )(proj, mixed, lse, ga, wo)


def tile_of(units, most=1024):
    return next(t for t in (1536, 1024, 768, 512, 256, 128) if units % t == 0 and t <= most)


def first_need(tile, columns, slots):
    return [slot * columns // tile for slot in range(slots)]


def ff_up_kernel(plan, pieces_total, slots, tile, *refs):
    table, x, bias = refs[:3]
    pieces = refs[3 : 3 + pieces_total]
    active, slope, w_out, w, sems, out_sems = refs[3 + pieces_total :]
    n = pl.program_id(0)
    cols = plan.columns

    @pl.when(n == 0)
    def _():
        for slot in range(slots):
            for c in plan.copies(slot, pieces, table, w, sems):
                c.start()

    def out_copy(slot):
        part = pl.ds(slot * cols, cols)
        return pltpu.make_async_copy(w.at[:, part], w_out.at[:, part], out_sems.at[slot])

    for slot, step in enumerate(first_need(tile, cols, slots)):

        @pl.when(n == step)
        def _(slot=slot):
            for c in plan.copies(slot, pieces, table, w, sems):
                c.wait()
            out_copy(slot).start()

    root = math.sqrt(2.0 / math.pi)
    for r in range(0, PAD, PAD // 3):
        rows = slice(r, r + PAD // 3)
        u = nn(x[rows, :], w[:, pl.ds(pl.multiple_of(n * tile, tile), tile)]) + bias[...]
        square = u * u
        t = jnp.tanh(u * (root + (root * 0.044715) * square))
        half = 0.5 + 0.5 * t
        value = u * half
        active[rows, :] = value.astype(BF16)
        slope[rows, :] = (
            half + (value * (1.0 - half)) * (2.0 * root + (6.0 * root * 0.044715) * square)
        ).astype(BF16)

    @pl.when(n == pl.num_programs(0) - 1)
    def _():
        for slot in range(slots):
            out_copy(slot).wait()


def ff_up(table, x, bias, pieces, plan, slots):
    d = x.shape[1]
    units = slots * plan.columns
    tile = tile_of(units)
    return pl.pallas_call(
        functools.partial(ff_up_kernel, plan, len(pieces), slots, tile),
        grid=(units // tile,),
        in_specs=[
            pl.BlockSpec(memory_space=pltpu.SMEM),
            whole((PAD, d)),
            pl.BlockSpec((1, tile), lambda n: (0, n)),
            *[pl.BlockSpec(memory_space=pl.ANY) for _ in pieces],
        ],
        out_specs=[
            pl.BlockSpec((PAD, tile), lambda n: (0, n)),
            pl.BlockSpec((PAD, tile), lambda n: (0, n)),
            pl.BlockSpec(memory_space=pl.ANY),
        ],
        out_shape=[
            jax.ShapeDtypeStruct((PAD, units), BF16),
            jax.ShapeDtypeStruct((PAD, units), BF16),
            jax.ShapeDtypeStruct((d, units), BF16),
        ],
        scratch_shapes=[
            pltpu.VMEM((d, units), BF16),
            pltpu.SemaphoreType.DMA((len(plan.entries),)),
            pltpu.SemaphoreType.DMA((slots,)),
        ],
        compiler_params=params(),
        cost_estimate=cost(2 * PAD * d * units, 4 * d * units + 4 * PAD * units, 0.05),
        name="ff_up",
    )(table, x, bias, *pieces)


def ff_down_kernel(plan, pieces_total, slots, tile, *refs):
    table, gl, active, slope = refs[:4]
    pieces = refs[4 : 4 + pieces_total]
    acc, gu, sums, w, sems = refs[4 + pieces_total :]
    n = pl.program_id(0)
    cols = plan.columns

    @pl.when(n == 0)
    def _():
        for slot in range(slots):
            for c in plan.copies(slot, pieces, table, w, sems):
                c.start()

    for slot, step in enumerate(first_need(tile, cols, slots)):

        @pl.when(n == step)
        def _(slot=slot):
            for c in plan.copies(slot, pieces, table, w, sems):
                c.wait()

    wt = w[:, pl.ds(pl.multiple_of(n * tile, tile), tile)]
    grad = (nn(gl[...], wt) * slope[...].astype(F32)).astype(BF16)
    gu[...] = grad
    sums[...] = jnp.sum(grad.astype(F32), axis=0, keepdims=True)
    part = nt(active[...], wt)

    @pl.when(n == 0)
    def _():
        acc[...] = part

    @pl.when(n > 0)
    def _():
        acc[...] += part


def ff_down(table, gl, active, slope, pieces, plan, slots):
    d = gl.shape[1]
    units = slots * plan.columns
    tile = tile_of(units)
    return pl.pallas_call(
        functools.partial(ff_down_kernel, plan, len(pieces), slots, tile),
        grid=(units // tile,),
        in_specs=[
            pl.BlockSpec(memory_space=pltpu.SMEM),
            whole((PAD, d)),
            pl.BlockSpec((PAD, tile), lambda n: (0, n)),
            pl.BlockSpec((PAD, tile), lambda n: (0, n)),
            *[pl.BlockSpec(memory_space=pl.ANY) for _ in pieces],
        ],
        out_specs=[
            whole((PAD, d)),
            pl.BlockSpec((PAD, tile), lambda n: (0, n)),
            pl.BlockSpec((1, tile), lambda n: (0, n)),
        ],
        out_shape=[
            jax.ShapeDtypeStruct((PAD, d), F32),
            jax.ShapeDtypeStruct((PAD, units), BF16),
            jax.ShapeDtypeStruct((1, units), F32),
        ],
        scratch_shapes=[
            pltpu.VMEM((d, units), BF16),
            pltpu.SemaphoreType.DMA((len(plan.entries),)),
        ],
        compiler_params=params(),
        cost_estimate=cost(4 * PAD * d * units, 2 * d * units + 6 * PAD * units, 0.05),
        name="ff_down",
    )(table, gl, active, slope, *pieces)


def put_turned(table, blocks, value, out):
    t = value.T
    rows = t.shape[0] // blocks
    for b in range(blocks):
        out[pl.ds(pl.multiple_of(table[b], 16), rows), :] = t[b * rows : (b + 1) * rows, :]


def turn_kernel(blocks, table, x, out, sums):
    value = x[...]
    put_turned(table, blocks, value, out)
    sums[...] = jnp.sum(value.astype(F32), axis=0, keepdims=True)


def specs(total):
    return [pl.BlockSpec(memory_space=pltpu.SMEM)] + [pl.BlockSpec(memory_space=pltpu.VMEM)] * total


def turn(table, x):
    d = x.shape[1]
    return pl.pallas_call(
        functools.partial(turn_kernel, table.shape[0]),
        in_specs=specs(1),
        out_specs=specs(2)[1:],
        out_shape=[jax.ShapeDtypeStruct((d, PAD), BF16), jax.ShapeDtypeStruct((1, d), F32)],
        compiler_params=params(),
        cost_estimate=cost(PAD * d * 8, PAD * d * 4, 0.05),
        name="turn",
    )(table, x)


def centered(v):
    c = v - jnp.mean(v, axis=-1, keepdims=True)
    return c, lax.rsqrt(jnp.mean(c * c, axis=-1, keepdims=True) + EPS)


def norm_kernel(blocks, seq, groups, *refs):
    if groups:
        table, base, extra, gain, bias = refs[:5]
        mixed, wo = refs[5 : 5 + groups], refs[5 + groups : 5 + 2 * groups]
        hidden, normed, turned = refs[5 + 2 * groups :]
        v = base[...].astype(F32) + extra[...]
        for m, o in zip(mixed, wo):
            v += nt(m[...], o[...])
        hidden[...] = v
    else:
        table, base, gain, bias, normed, turned = refs
        v = base[...].astype(F32)
    c, r = centered(v)
    value = c * r * gain[...] + bias[...]
    rows = lax.broadcasted_iota(jnp.int32, value.shape, 0)
    low = jnp.where(rows < seq, value, 0.0).astype(BF16)
    normed[...] = low
    put_turned(table, blocks, low, turned)


def norm(table, base, extra, gain, bias, seq, mixed=(), wo=()):
    d = base.shape[1]
    args = [base] + ([extra] if mixed else []) + [gain, bias, *mixed, *wo]
    outs = [jax.ShapeDtypeStruct((PAD, d), BF16), jax.ShapeDtypeStruct((d, PAD), BF16)]
    if mixed:
        outs = [jax.ShapeDtypeStruct((PAD, d), F32)] + outs
    return pl.pallas_call(
        functools.partial(norm_kernel, table.shape[0], seq, len(mixed)),
        in_specs=specs(len(args)),
        out_specs=specs(len(outs))[1:],
        out_shape=outs,
        compiler_params=params(),
        cost_estimate=cost(PAD * d * 16, PAD * d * 10, 0.05),
        name="norm",
    )(table, *args)


def through_norm(v, e, gain, base):
    c, r = centered(v)
    u = c * r
    scaled = e * gain
    inner = jnp.mean(scaled * u, axis=-1, keepdims=True)
    value = base + r * (scaled - jnp.mean(scaled, axis=-1, keepdims=True) - u * inner)
    return value, jnp.sum(e * u, axis=0, keepdims=True), jnp.sum(e, axis=0, keepdims=True)


def ff_back_kernel(blocks, *refs):
    table, gu, w, v, gain, base, grad, gain_sum, bias_sum, low, turned, low_sum, acc = refs
    n = pl.program_id(0)
    part = nt(gu[...], w[...])

    @pl.when(n == 0)
    def _():
        acc[...] = part

    @pl.when(n > 0)
    def _():
        acc[...] += part

    @pl.when(n == pl.num_programs(0) - 1)
    def _():
        value, gain_sum[...], bias_sum[...] = through_norm(
            v[...], acc[...], gain[...], base[...].astype(F32)
        )
        grad[...] = value
        rounded = value.astype(BF16)
        low[...] = rounded
        put_turned(table, blocks, rounded, turned)
        low_sum[...] = jnp.sum(rounded.astype(F32), axis=0, keepdims=True)


def ff_back(table, gu, w, v, gain, base):
    d, units = w.shape
    tile = tile_of(units, 1536)
    row = jax.ShapeDtypeStruct((1, d), F32)
    outs = [
        jax.ShapeDtypeStruct((PAD, d), F32),
        row,
        row,
        jax.ShapeDtypeStruct((PAD, d), BF16),
        jax.ShapeDtypeStruct((d, PAD), BF16),
        row,
    ]
    return pl.pallas_call(
        functools.partial(ff_back_kernel, table.shape[0]),
        grid=(units // tile,),
        in_specs=[
            pl.BlockSpec(memory_space=pltpu.SMEM),
            pl.BlockSpec((PAD, tile), lambda n: (0, n)),
            pl.BlockSpec((d, tile), lambda n: (0, n)),
            *specs(3)[1:],
        ],
        out_specs=specs(len(outs))[1:],
        out_shape=outs,
        scratch_shapes=[pltpu.VMEM((PAD, d), F32)],
        compiler_params=params(),
        cost_estimate=cost(2 * PAD * d * units, 2 * d * units + 2 * PAD * units),
        name="ff_back",
    )(table, gu, w, v, gain, base)


def attn_back_kernel(seq, groups, *refs):
    grads, ws = refs[:groups], refs[groups : 2 * groups]
    v, gain, base, grad, gain_sum, bias_sum = refs[2 * groups :]
    cut = 3 * GROUP_HEADS * HEAD_DIM
    e = nt(grads[0][:, 0:cut], ws[0][:, 0:cut])
    for g, w in zip(grads[1:], ws[1:]):
        e += nt(g[:, 0:cut], w[:, 0:cut])
    value, gain_sum[...], bias_sum[...] = through_norm(
        v[...].astype(F32), e, gain[...], base[...]
    )
    grad[...] = value[0:seq]


def attn_back(grads, ws, v, gain, base, seq):
    d = v.shape[1]
    row = jax.ShapeDtypeStruct((1, d), F32)
    args = [*grads, *ws, v, gain, base]
    return pl.pallas_call(
        functools.partial(attn_back_kernel, seq, len(grads)),
        in_specs=specs(len(args))[1:],
        out_specs=specs(3)[1:],
        out_shape=[jax.ShapeDtypeStruct((seq, d), F32), row, row],
        compiler_params=params(),
        cost_estimate=cost(6 * PAD * d * d, PAD * d * 18),
        name="attn_back",
    )(*args)


def ff_grad_kernel(total, parts, sets, size, rows, *refs):
    lhs, rhs, outs = refs[:total], refs[total : 2 * total], refs[2 * total :]
    value = nn(lhs[0][...], rhs[0][...])
    for a, b in zip(lhs[1:], rhs[1:]):
        value += nn(a[...], b[...])
    low = value.astype(BF16)
    n = pl.program_id(0)
    for s in range(sets):

        @pl.when((n >= s * size) & (n < (s + 1) * size))
        def _(s=s):
            for number in range(parts):
                outs[number * sets + s][0] = low[number * rows : (number + 1) * rows]


def ff_grad(lhs, blocks, rhs, slots, parts, sets):
    total = len(lhs)
    height = lhs[0].shape[0] // total
    rows = height // parts
    cols = rhs[0].shape[1] // slots
    size = slots // sets

    def place(s):
        return lambda n: (jnp.clip(n - s * size, 0, size - 1), 0, 0)

    outs = pl.pallas_call(
        functools.partial(ff_grad_kernel, total, parts, sets, size, rows),
        grid=(slots,),
        in_specs=[
            *[pl.BlockSpec((height, PAD), lambda n, b=b: (b, 0)) for b in blocks],
            *[pl.BlockSpec((PAD, cols), lambda n: (0, n)) for _ in rhs],
        ],
        out_specs=[
            pl.BlockSpec((1, rows, cols), place(s)) for _ in range(parts) for s in range(sets)
        ],
        out_shape=[jax.ShapeDtypeStruct((size, rows, cols), BF16)] * (parts * sets),
        compiler_params=params(),
        cost_estimate=cost(
            2 * total * PAD * height * slots * cols, 2 * slots * cols * (total * PAD + height)
        ),
        name="ff_grad",
    )(*lhs, *rhs)
    return [outs[p * sets : (p + 1) * sets] for p in range(parts)]


def attn_grad_kernel(total, parts, has_more, *refs):
    na, ga, g = refs[:total], refs[total : 2 * total], refs[2 * total : 3 * total]
    more, outs = refs[3 * total : -parts], refs[-parts:]
    cut = 3 * GROUP_HEADS * HEAD_DIM
    rows = na[0].shape[0] // parts
    for part in range(parts):
        block = slice(part * rows, (part + 1) * rows)
        for lhs, columns in ((na, slice(0, cut)), (ga, slice(cut, None))):
            value = nn(lhs[0][block, :], g[0][:, columns])
            for i in range(1, total):
                value += nn(lhs[i][block, :], g[i][:, columns])
            if has_more:
                value += more[part][:, columns].astype(F32)
            outs[part][:, columns] = value.astype(BF16)


def attn_grad(na, ga, grads, parts, more=()):
    total = len(na)
    d = na[0].shape[0]
    cols = grads[0].shape[1]
    args = [*na, *ga, *grads, *more]
    return pl.pallas_call(
        functools.partial(attn_grad_kernel, total, parts, len(more) > 0),
        in_specs=specs(len(args))[1:],
        out_specs=specs(parts)[1:],
        out_shape=[jax.ShapeDtypeStruct((d // parts, cols), BF16) for _ in range(parts)],
        compiler_params=params(),
        cost_estimate=cost(2 * total * PAD * d * cols, 2 * cols * (total * PAD + 2 * d)),
        name="attn_grad",
    )(*args)


def hop(x, axis, n, step):
    return lax.ppermute(x, axis, [(i, (i + step) % n) for i in range(n)])


def cat(*arrays):
    return jnp.concatenate(arrays, axis=0)


def after(x, *others):
    others = [o for o in others if o is not None]
    return lax.optimization_barrier((x, others))[0] if others else x


def total_sum(value, sizes):
    for axis in ("c", "x", "y", "z"):
        n = sizes[axis]
        step = 1
        while step < n:
            value = value + lax.ppermute(value, axis, [(i, i ^ step) for i in range(n)])
            step *= 2
    return value


def attn_entries(nz, rows, h):
    g = rows - h
    plans = []
    for dx in range(2):
        entries = []
        for dy in range(2):
            for dz in range(nz):
                one = (dz, dx * h) if dy == 0 else (nz + dz // 2, dz % 2 * 2 * h + dx * h)
                if dx == 0:
                    two = dz, 2 * h + dy * g
                else:
                    two = nz + nz // 2 + dz // 2, dz % 2 * 2 * g + dy * g
                for (piece, at), size, inside in ((one, h, 0), (two, g, h)):
                    entries.append((piece, at, size, 0, dy * nz + dz, inside, 0))
        plans.append(entries)
    return plans


def ff_entries(nz, rows, cols):
    entries = []
    for dz in range(nz):
        for dc in range(2):
            for dy in range(2):
                for dx in range(2):
                    piece = (dc * 2 + dy) * nz + dz
                    entries.append(
                        (piece, dx * rows, rows, dz, dc * 4 + dy * 2 + dx, 0, dz * cols)
                    )
    return entries


def on_device(
    sizes,
    inputs,
    slot_mask,
    ln1_gain,
    ln1_bias,
    qkv_weight,
    qv_bias,
    out_weight,
    out_bias,
    ln2_gain,
    ln2_bias,
    up_weight,
    up_bias,
    down_weight,
    down_bias,
    out_grad,
):
    seq, d = inputs.shape[1:]
    ny, nx, nc, nz = (sizes[a] for a in ("y", "x", "c", "z"))
    yi, xi, ci, zi = (lax.axis_index(a) for a in ("y", "x", "c", "z"))
    width = GROUP_HEADS * HEAD_DIM
    unit_width = up_weight.shape[1]
    cols = -(-unit_width // 128) * 128
    a_rows, f_rows = qkv_weight.shape[0], up_weight.shape[0]
    linked = ny == nx == nc == 2 and nz == 4 and a_rows % 16 == 0 and f_rows % 16 == 0

    attn_own = jnp.concatenate(
        [qkv_weight.reshape(a_rows, 3 * width).astype(BF16), out_weight.T.astype(BF16)], axis=1
    )
    spare = ((0, 0), (0, cols - unit_width))
    up_own = jnp.pad(up_weight.astype(BF16), spare)
    down_own = jnp.pad(down_weight.T.astype(BF16), spare)

    def swap(x, axis="c"):
        return hop(x, axis, 2, 1)

    if linked:
        h = -(-a_rows // 32) * 16
        order = [(dc, dx) for dc in range(2) for dx in range(2)]
        attn_plans = [Plan(e, 4 * width) for e in attn_entries(nz, a_rows, h)] * 2
        groups = [(xi ^ dx) * 2 + (ci ^ dc) for dc, dx in order]
        down_plan = Plan(ff_entries(nz, f_rows, cols), cols)
        zones = [(zi - dz) % nz for dz in range(nz)]
        attn_table = jnp.stack(
            [((yi ^ dy) * nz + (zi - dz) % nz) * a_rows for dy in range(2) for dz in range(nz)]
        )
        ff_table = jnp.stack(
            [
                (((yi ^ dy) * 2 + (xi ^ dx)) * 2 + (ci ^ dc)) * f_rows
                for dc in range(2)
                for dy in range(2)
                for dx in range(2)
            ]
        )
        turn_attn = jnp.stack(
            [((yi ^ b // nz) * nz + (zi - b % nz) % nz) * a_rows for b in range(2 * nz)]
        )
        turn_ff = jnp.stack(
            [
                ((ci ^ b % 2) * 4 + (yi ^ b // 4) * 2 + (xi ^ b // 2 % 2)) * f_rows
                for b in range(8)
            ]
        )
    else:
        whole_attn = lax.all_gather(attn_own, ("y", "z"), axis=0, tiled=True)
        whole_attn = lax.all_gather(whole_attn, ("x", "c"), axis=0)
        down_whole = lax.all_gather(down_own, ("z", "y", "x", "c"), axis=0, tiled=True)
        up_whole = lax.all_gather(up_own, ("z", "y", "x", "c"), axis=0, tiled=True)
        attn_pieces = [[whole_attn[g]] for g in range(nx * nc)]
        attn_plans = [Plan([(0, 0, d, 0, 0, 0, 0)], 4 * width)] * (nx * nc)
        attn_table = ff_table = turn_attn = turn_ff = jnp.zeros((1,), jnp.int32)
        groups = list(range(nx * nc))
        zones = list(range(nz))
    up_plan = ZonePlan(nz, d, cols)
    zone_table = jnp.stack([jnp.asarray(k, jnp.int32) * d for k in zones])

    valid = slot_mask[0].astype(F32)
    token_pad = ((0, PAD - seq), (0, 0))
    base = jnp.pad(inputs[0], token_pad)
    grad_low = (valid * jnp.pad(out_grad[0], token_pad).astype(F32)).astype(BF16)
    bias_rows = []
    for g in groups:
        part = lax.dynamic_slice_in_dim(qv_bias, g * width, width, 1)
        bias_rows.append(jnp.concatenate([part[0], jnp.zeros_like(part[0]), part[1]])[None])
    shift = jnp.concatenate(
        [
            jnp.pad(lax.dynamic_slice_in_dim(up_bias, k * unit_width, unit_width), spare[1])
            for k in zones
        ]
    )[None]
    gain_one, gain_two, shift_two, out_row = (
        v[None] for v in (ln1_gain, ln2_gain, ln2_bias, out_bias)
    )
    normed_a, na_t = norm(turn_attn, base, None, gain_one, ln1_bias[None], seq)
    gl_t, down_bias_sum = turn(turn_ff, grad_low)

    together = lax.optimization_barrier
    spots = ("z", "y", "x", "c")
    if linked:
        down_z, pairs, down_y, pair_far, y_far_down = [down_own], [], [], [], []

        px, py, dx0, dz1 = together(
            (
                swap(attn_own[:h], "x"),
                swap(attn_own[h:], "y"),
                swap(down_own, "x"),
                hop(down_own, "z", nz, 1),
            )
        )
        pairs.append(cat(down_own, dx0))
        down_z.append(dz1)
        s = [cat(attn_own[:h], px, attn_own[h:], py)]
        s1, dy0, dx1, sc0, gl_t, na_t = together(
            (
                hop(s[0], "z", nz, 1),
                swap(pairs[0], "y"),
                swap(down_z[1], "x"),
                swap(s[0]),
                gl_t,
                na_t,
            )
        )
        down_y.append(dy0)
        pairs.append(cat(down_z[1], dx1))
        s.append(s1)
        s_far = [sc0]
        y_parts, x_parts, y_far, x_far = [], [], [], []
        for k in range(2, nz):
            moves = [hop(s[-1], "z", nz, 1), swap(s[-1])]
            if k % 2 == 0:
                moves.append(swap(cat(s[k - 2][: 2 * h], s[k - 1][: 2 * h]), "y"))
                moves.append(swap(cat(s[k - 2][2 * h :], s[k - 1][2 * h :]), "x"))
                if k == 2:
                    moves.append(swap(na_t))
                    moves.append(
                        (bias_rows, shift, ff_table, zone_table, turn_ff, gain_two, shift_two)
                    )
            else:
                moves += [swap(y_parts[-1]), swap(x_parts[-1])]
                if k == 3:
                    moves.append(swap(pairs[1], "y"))
            moves = together(tuple(moves))
            s.append(moves[0])
            s_far.append(moves[1])
            if k % 2 == 0:
                y_parts.append(moves[2])
                x_parts.append(moves[3])
                if k == 2:
                    na_far = moves[4]
                    bias_rows, shift, ff_table, zone_table, turn_ff, gain_two, shift_two = moves[5]
            else:
                y_far.append(moves[2])
                x_far.append(moves[3])
                if k == 3:
                    down_y.append(moves[4])
        up_whole = lax.all_gather(after(up_own, s[-1]), spots, axis=0, tiled=True)
        y1, x1, sc3, dz2, p0 = together(
            (
                swap(cat(s[-2][: 2 * h], s[-1][: 2 * h]), "y"),
                swap(cat(s[-2][2 * h :], s[-1][2 * h :]), "x"),
                swap(s[-1]),
                hop(after(down_z[1], s[-1]), "z", nz, 1),
                swap(after(pairs[0], s[-1])),
            )
        )
        y_parts.append(y1)
        x_parts.append(x1)
        s_far.append(sc3)
        down_z.append(dz2)
        pair_far.append(p0)
        near = [*s, *y_parts, *x_parts]
        y_far.append(swap(y1))
        x_far.append(swap(x1))
        far = [*s_far, *y_far, *x_far]

        kept = []
        for number in range(4):
            pieces = near if number < 2 else far
            out = attn_fwd(
                attn_table, normed_a, bias_rows[number], pieces, attn_plans[number], seq
            )
            kept.append(out)
            normed_a = after(normed_a, out)
            if number == 0:
                dx2, dz3 = swap(down_z[2], "x"), hop(after(down_own, dz2), "z", nz, -1)
                y0 = swap(after(down_y[0], dz2))
                normed_a, dx2, dz3, far, y0 = together((normed_a, dx2, dz3, far, y0))
                down_z.append(dz3)
                pairs.append(cat(down_z[2], dx2))
            if number == 1:
                dx3, dy2 = swap(down_z[3], "x"), swap(pairs[2], "y")
                p1, y1 = swap(after(pairs[1], dx2)), swap(after(down_y[1], dx2))
                normed_a, dx3 = together((normed_a, dx3))
            if number == 2:
                normed_a, dx3, dy2, p1, y1 = together((normed_a, dx3, dy2, p1, y1))
                pair_far.append(p1)
                y_far_down += [y0, y1]
                pairs.append(cat(down_z[3], dx3))
                down_y.append(dy2)
                near_three = swap(after(down_z[3], out), "y")
                p2, y2, gl_far = swap(after(pairs[2], out)), swap(dy2), swap(after(gl_t, out))
        mixed_last, near_three, far_three, p2, y2 = together(
            (out[1], near_three, swap(dx3, "y"), p2, y2)
        )
        dy3 = cat(near_three, far_three)
        kept[3] = [out[0], mixed_last, *out[2:]]
    else:
        kept = []
        for number, g in enumerate(groups):
            kept.append(
                attn_fwd(
                    attn_table,
                    normed_a,
                    bias_rows[number],
                    attn_pieces[number],
                    attn_plans[number],
                    seq,
                )
            )

    hidden, normed_b, nb_t = norm(
        turn_ff,
        base,
        out_row,
        gain_two,
        shift_two,
        seq,
        [out[1] for out in kept],
        [out[4] for out in kept],
    )
    if linked:
        normed_b, gl_far = together((normed_b, gl_far))
        down_y.append(dy3)
        p3, y3 = swap(pairs[3]), swap(dy3)
        nb_far = swap(nb_t)
    active, slope, up_full = ff_up(zone_table, normed_b, shift, [up_whole], up_plan, nz)
    if linked:
        active, p3, y3, nb_far = together((active, p3, y3, nb_far))
        down_pieces = [*pairs, *down_y, *pair_far, p2, p3, *y_far_down, y2, y3]
        active_far = swap(active)
    else:
        down_plan, ff_table, down_pieces = up_plan, zone_table, [down_whole]
    mlp, grad_upper, upper_sums = ff_down(
        ff_table, grad_low, active, slope, down_pieces, down_plan, nz
    )

    def finish(rows):
        return (valid * (hidden + (rows + down_bias)))[:seq].astype(BF16)[None]

    def plus(*values):
        return sum(v.astype(F32) for v in values).astype(BF16)

    if linked:
        grad_upper, active_far = together((grad_upper, active_far))
        upper_far = swap(grad_upper)
        down_parts = [
            p[0] for p in ff_grad([gl_t, gl_far], [0, 1], [active, active_far], nz, 4, 1)
        ]
        down_one, down_two = swap(down_parts[3], "x"), swap(down_parts[1], "x")
        grad_upper_first = after(grad_upper, down_parts)
    else:
        spot = ("y", "x", "c")

        def spread(parts):
            part = lax.psum_scatter(parts[0], "z", scatter_dimension=0, tiled=True)[0]
            part = lax.psum_scatter(part, spot, scatter_dimension=0, tiled=True)
            return lax.optimization_barrier(part).astype(F32)

        down_sum = spread(ff_grad([gl_t], [0], [active], nz, 1, 1)[0])
        up_sum = spread(ff_grad([nb_t], [0], [grad_upper], nz, 1, 1)[0])
        grad_upper_first = grad_upper

    grad_hidden, ln2_gain_grad, ln2_bias_grad, grad_attn, ga_t, out_bias_sum = ff_back(
        turn_attn, grad_upper_first, up_full, hidden, gain_two, grad_low
    )

    def in_place(rows, places):
        at = jnp.arange(len(rows))[:, None]
        return sum(jnp.where(at == p, r, 0.0) for r, p in zip(rows, places))

    wide = max(d, 3 * width, cols)

    def fit(x):
        return jnp.pad(x, ((0, 0), (0, wide - x.shape[1])))

    def early_rows(ready):
        upper = after(upper_sums, ready)
        vectors = [
            out_bias_sum,
            ln2_gain_grad,
            ln2_bias_grad,
            down_bias_sum,
            in_place([after(v, ready) for v in sums], [after(k, ready) for k in groups]),
            in_place([upper[:, slot * cols : (slot + 1) * cols] for slot in range(nz)], zones),
        ]
        rows = cat(*[fit(v) for v in vectors])
        return jnp.pad(rows, ((0, -(rows.shape[0] + 2) % 8), (0, 0)))

    def fold(value, axis, step):
        return lax.ppermute(value, axis, [(i, i ^ step) for i in range(sizes[axis])])

    sums = [None] * len(groups)
    if linked:
        grads = {}
        ga_far = swap(ga_t)

        def back(number):
            proj, mixed, lse, _, wo = kept[number]
            grads[number], sums[number] = attn_bwd(proj, mixed, lse, ga_first, wo, seq)

        ga_first, upper_far = together((grad_attn, upper_far))
        back(3)
        far_grads = swap(grads[3])
        ga_first, down_one, _ = together((ga_first, down_one, grads[3]))
        down_one = plus(down_parts[2], down_one)
        down_other = swap(down_one, "y")
        back(1)
        grads[1], far_grads, ga_far, down_one = together((grads[1], far_grads, ga_far, down_one))
        more = attn_grad([na_t, na_far], [ga_t, ga_far], [grads[1], far_grads], 4)
        more_in = [None, None, swap(more[2], "x"), swap(more[3], "x")]
        upper_first, upper_far = together((grad_upper, upper_far, more))[:2]
        up_parts = ff_grad([nb_t, nb_far], [0, 1], [upper_first, upper_far], nz, 4, 2)
        up_parts, down_two, down_other, ga_first = together(
            (up_parts, down_two, down_other, ga_first)
        )
        up_near = [swap(up_parts[3][1], "y")]
        down_value = plus(down_parts[0], down_two, down_other)
        ga_first = after(ga_first, down_value)
        down_line = hop(down_value[nz - 1], "z", nz, -1)
        back(2)
        grads[2], down_line, more_in[2], more_in[3], up_near[0], ga_first = together(
            (grads[2], down_line, more_in[2], more_in[3], up_near[0], ga_first)
        )
        far_grads = swap(grads[2])
        more_in[1] = swap(after(more[1], more_in[3]), "x")
        up_near.append(swap(after(up_parts[2][1], grads[2]), "y"))
        down_line = plus(down_line, down_value[nz - 2])
        up_one = [None, plus(up_parts[1][1], up_near[0])]
        ga_first = after(ga_first, down_line, up_one[1])
        down_line = hop(down_line, "z", nz, -1)
        back(0)
        early = early_rows(None)
        grads[0], far_grads, up_near[1], down_line, more_in[1], early = together(
            (grads[0], far_grads, up_near[1], down_line, more_in[1], early)
        )
        more_in[0] = swap(after(more[0], grads[0]), "x")
        up_near.append(swap(after(up_parts[3][0], grads[0]), "y"))
        down_line = plus(down_line, down_value[nz - 3])
        grads_first = after(grads[0], down_line)
        down_line = hop(down_line, "z", nz, -1)
        input_grad, ln1_gain_grad, ln1_bias_grad = attn_back(
            [grads_first] + [grads[k] for k in range(1, 4)],
            [out[3] for out in kept],
            base,
            gain_one,
            grad_hidden,
            seq,
        )
        na_first, more_in[0], up_near[2], down_line, input_grad = together(
            (na_t, more_in[0], up_near[2], down_line, input_grad)
        )
        up_near.append(swap(after(up_parts[2][0], na_first), "y"))
        up_other = [None, swap(after(up_one[1], na_first), "x")]
        total = attn_grad(
            [na_first, na_far], [ga_t, ga_far], [grads[0], far_grads], 4, more_in
        )
        table = after(cat(fit(ln1_gain_grad), fit(ln1_bias_grad), early), na_first)
        total, up_near[3], up_other[1], other = together(
            (total, up_near[3], up_other[1], fold(table, "z", 1))
        )
        table = table + other
        far_y = [None, swap(total[3], "y")]
        up_one[0] = plus(up_parts[1][0], up_near[2])
        up_other[0] = swap(up_one[0], "x")
        up_high = plus(up_parts[0][1], up_near[1], up_other[1])
        up_line = hop(up_high[1], "z", nz, -1)
        far_y[1], up_line, up_other[0], near_y, other = together(
            (far_y[1], up_line, up_other[0], total[1], fold(table, "z", 2))
        )
        table = table + other
        far_y[0] = swap(after(total[2], near_y), "y")
        high = plus(near_y, far_y[1]).reshape(2, a_rows, 4 * width)
        last_far = [hop(high[k], "z", nz, -2 - k) for k in range(2)]
        up_line = hop(plus(up_line, up_high[0]), "z", nz, -1)
        output = finish(after(mlp, near_y))
        input_grad = after(input_grad, near_y)
        far_y[0], up_line, other, last_far, near_y = together(
            (far_y[0], up_line, fold(table, "x", 1), last_far, after(total[0], near_y))
        )
        table = table + other
        table = table + fold(table, "y", 1)
        table = table + fold(table, "c", 1)
        low = plus(near_y, far_y[0]).reshape(2, a_rows, 4 * width)
        last_far.append(hop(low[1], "z", nz, -1))
        up_low = plus(up_parts[0][0], up_near[3], up_other[0])
        up_line = hop(plus(up_line, up_low[1]), "z", nz, -1)
        down_sum = down_line.astype(F32) + down_value[0].astype(F32)
        up_sum = up_line.astype(F32) + up_low[0].astype(F32)
        attn_sum = sum(v.astype(F32) for v in (low[0], *last_far))
    else:
        output = finish(mlp)
        parts = []
        grads = {}
        for number, (proj, mixed, lse, _, wo) in enumerate(kept):
            grads[number], sums[number] = attn_bwd(proj, mixed, lse, grad_attn, wo, seq)
            parts.append(attn_grad([na_t], [ga_t], [grads[number]], 1)[0])
        part = lax.psum_scatter(jnp.stack(parts), ("x", "c"), scatter_dimension=0, tiled=True)[0]
        part = lax.psum_scatter(part, ("y", "z"), scatter_dimension=0, tiled=True)
        attn_sum = lax.optimization_barrier(part).astype(F32)
        input_grad, ln1_gain_grad, ln1_bias_grad = attn_back(
            [grads[k] for k in range(len(groups))],
            [out[3] for out in kept],
            base,
            gain_one,
            grad_hidden,
            seq,
        )


    if not linked:
        table = total_sum(cat(fit(ln1_gain_grad), fit(ln1_bias_grad), early_rows(None)), sizes)
    singles = [table[k, :d] for k in range(6)]
    qv = table[6 : 6 + len(groups)]
    qv_grad = jnp.stack([qv[:, :width].reshape(-1), qv[:, 2 * width : 3 * width].reshape(-1)])
    up_bias_grad = table[6 + len(groups) : 6 + len(groups) + nz, :unit_width].reshape(-1)

    qkv_grad = attn_sum[:, : 3 * width].reshape(a_rows, 3, width)
    out_weight_grad = attn_sum[:, 3 * width :].T
    up_grad = up_sum[:, :unit_width]
    down_grad = down_sum[:, :unit_width].T
    return (
        output,
        input_grad[None],
        singles[0],
        singles[1],
        qkv_grad,
        qv_grad,
        out_weight_grad,
        singles[2],
        singles[3],
        singles[4],
        up_grad,
        up_bias_grad,
        down_grad,
        singles[5],
    )


def solution(mesh):
    heads = mesh.shape["heads"]
    sizes = {"y": mesh.shape["fsdp"], "x": heads // 2, "c": 2, "z": mesh.shape["tensor"]}
    split = jax.sharding.Mesh(mesh.devices.reshape(tuple(sizes.values())), tuple(sizes))
    images = P(("y", "x", "c", "z"), None, None)
    attn_in = P(("y", "z"), None, ("x", "c"))
    attn_out = P(("x", "c"), ("y", "z"))
    up, down = P(("y", "x", "c"), "z"), P("z", ("y", "x", "c"))
    in_specs = (
        images,
        P(("y", "x", "c", "z")),
        P(),
        P(),
        attn_in,
        P(),
        attn_out,
        P(),
        P(),
        P(),
        up,
        P(),
        down,
        P(),
        images,
    )
    out_specs = (
        images,
        images,
        P(),
        P(),
        attn_in,
        P(),
        attn_out,
        P(),
        P(),
        P(),
        up,
        P(),
        down,
        P(),
    )
    return jax.shard_map(
        functools.partial(on_device, sizes),
        mesh=split,
        in_specs=in_specs,
        out_specs=out_specs,
        check_vma=False,
    )
```
